32 devices in a mesh: seq: 4 (over z), head: 2 (over x), dp: 4 (over y, core).
Axes of the slice: x: 2, y: 2, z: 4, core: 2. Of those that a mesh axis runs over, the one named last changes fastest.
Arguments:
- events: bfloat16 [12288, 1024], P(('dp', 'seq'), 'head'), parts along dimension 0
- w_proj: bfloat16 [4, 1024, 1024], P(None, None, 'head'), may hold values from -0.1875 to 0.1875
- w_out: bfloat16 [1024, 1024], P(None, 'head'), may hold values from -0.1875 to 0.1875
- block_target: int32 [768], P('dp'), parts along dimension 0, may hold values from 0 to 191, as said below
- user_lengths: int32 [12], P('dp'), parts along dimension 0, may hold values from 1 to 2880, 3072 in all
Outputs:
- layer_out: bfloat16 [12288, 1024], P(('dp', 'seq'), 'head'), parts along dimension 0
The draws below stay inside these ranges and needn't reach their ends.
There are 4 independent parts, one for each index of `dp`. The reference program is written for one: setup_inputs(seed, part) draws one part's arguments, and reference() takes and returns one part's arrays. A program takes and returns all parts, laid end to end along the dimension named above; an argument that names none is the same for every part. Nothing has to cross between parts.
Inputs may be any that keep to these rules, and one draw needn't show every extreme that they name: block_target is a permutation of 0 to 191; each aligned range of 12 values lies wholly in one aligned group of 48 entries (one log shard); each such group holds exactly 12 values in each aligned range of 48 values, and exactly 12 values v with (v mod 48) // 12 = i for each i below 4. `user_lengths`: the lengths sum to 3072.
All inputs are finite; a program needn't handle non-finite values.
Results may differ from the reference program's by a relative error of at most 0.0077.
Values may be sent and summed in bfloat16 or wider, within the bound.
No kernel may reach another device: no remote copies, remote signals or barrier semaphores. Data moves between devices by JAX's collectives and lax.ppermute only.
A program may use at most 64 MiB of HBM per device.

```python
import math
import jax
import jax.numpy as jnp
import numpy as np
from jax import lax

D = 1024
H = 16
DH = 64
L_DEV = 768
RB = 16
USERS = 3
SEQ = 3072
SHARE = 12
NBLK = 192


def shared_targets(key):
    key = jax.random.fold_in(key, 9)
    sigma_key, shift_key, order_key = jax.random.split(key, 3)
    shard_count = SEQ // L_DEV
    sigma = jax.random.permutation(sigma_key, shard_count).astype(jnp.int32)
    shifts = jax.random.permutation(shift_key, shard_count).astype(jnp.int32)
    cells = jnp.arange(shard_count * shard_count, dtype=jnp.int32)
    cell_row = cells // shard_count
    cell_col = cells % shard_count
    cell_shard = sigma[(shifts[cell_row] + cell_col) % shard_count]
    values = jnp.arange(NBLK, dtype=jnp.int32)
    value_shard = cell_shard[values // SHARE]
    ranks = jax.random.permutation(order_key, NBLK).astype(jnp.int32)
    score = value_shard * NBLK + ranks
    return jnp.argsort(score).astype(jnp.int32)


def draw_events(key, part):
    key = jax.random.fold_in(key, 5)
    base_key, column_key, row_key = jax.random.split(key, 3)
    column_scale = jnp.exp(jax.random.uniform(column_key, (D,), minval=math.log(0.3), maxval=math.log(3.0)))
    row_scale = jnp.exp(jax.random.uniform(row_key, (SEQ, 1), minval=math.log(0.5), maxval=math.log(1.5)))
    drawn = jax.random.normal(base_key, (SEQ, D)) * column_scale[None, :] * row_scale
    return (0.15 * drawn).astype(jnp.float32).astype(jnp.bfloat16)


def draw_block_target(key, part):
    return shared_targets(key)


def block_scale(stream_key, extent, cuts, least, largest):
    def one(position, shards_of):
        heights = jax.random.uniform(jax.random.fold_in(jax.random.fold_in(stream_key, 6), position), (shards_of,), jnp.float32, least / len(cuts), largest / len(cuts))
        return jnp.repeat(jnp.exp(heights), extent[position] // shards_of).reshape((-1,) + (1,) * (len(extent) - position - 1))

    loudness = one(*cuts[0])
    for cut in cuts[1:]:
        loudness = loudness * one(*cut)
    return loudness


def profile(count, total, reach, slope):
    loads = [(1 << 20) // math.isqrt(standing ** slope) + 1 for standing in range(2, count + 1)]
    surplus, holding = total - reach - (count - 1), [1] * (count - 1)
    while surplus > 0:
        free = [i for i in range(count - 1) if holding[i] < reach]
        pool, left = sum([loads[i] for i in free]), surplus
        for i in free:
            addition = min(reach - holding[i], max(1, left * loads[i] // pool), surplus)
            holding[i] = holding[i] + addition
            surplus = surplus - addition
    return np.array([reach] + holding)


def ragged(stream_key, amount, total, bound, skew):
    if amount == 2:
        one = jax.random.randint(stream_key, (), max(1, total - bound), min(bound, total - 1) + 1)
        return jnp.stack([one, total - one])
    tallies = jnp.asarray(profile(amount, total, bound, skew), jnp.int32)
    couples = (amount - 1) // 2
    giver, receiver = tallies[1:1 + 2 * couples:2], tallies[2:2 + 2 * couples:2]
    room = jnp.minimum(giver - 1, bound - receiver)
    passed = jax.random.randint(jax.random.fold_in(stream_key, 1), (couples,), 0, 1 << 20) % (room + 1)
    tallies = tallies.at[1:1 + 2 * couples:2].set(giver - passed).at[2:2 + 2 * couples:2].set(receiver + passed)
    return tallies[jax.random.permutation(jax.random.fold_in(stream_key, 2), amount)]


def bell_draw(own_key, shape, width, reach, shards=(), kind=jnp.bfloat16):
    values = width * jax.random.normal(own_key, shape, jnp.float32)
    if shards:
        values = values * block_scale(own_key, shape, shards, -0.22, 0.18)
    return jnp.clip(values, -reach, reach).astype(kind)


def setup_inputs(seed: int = 0, part: int = 0) -> dict:
    arg_keys = jax.random.split(jax.random.key(seed), 6)
    own_keys = jax.random.split(jax.random.fold_in(arg_keys[5], part), 6)
    return {
        "events": draw_events(jax.random.fold_in(jax.random.fold_in(arg_keys[5], part), 71), part),
        "w_proj": bell_draw(arg_keys[1], (4, D, D), D ** -0.5, 0.1875, ((2, 2),)),
        "w_out": bell_draw(arg_keys[2], (D, D), D ** -0.5, 0.1875, ((1, 2),)),
        "block_target": draw_block_target(jax.random.fold_in(jax.random.fold_in(arg_keys[5], part), 71), part),
        "user_lengths": ragged(own_keys[4], USERS, SEQ, SEQ - SEQ // 16, 0).astype(jnp.int32),
    }


eps_norm = 1e-05

def user_index(positions, user_ends):
    return lax.optimization_barrier(jnp.sum((positions[:, None] >= user_ends[None, :]).astype(jnp.int32), axis=1))

def layer_norm(matrix):
    mean_value = lax.optimization_barrier(jnp.mean(matrix, axis=1, keepdims=True))
    square_mean = lax.optimization_barrier(jnp.mean(matrix * matrix, axis=1, keepdims=True))
    return (matrix - mean_value) * lax.rsqrt(square_mean - mean_value * mean_value + eps_norm)

def reference(events, w_proj, w_out, block_target, user_lengths):
    blocks = events.reshape(SEQ // RB, RB, D)
    inverse = jnp.argsort(block_target).astype(jnp.int32)
    ordered = blocks[inverse].reshape(SEQ, D)
    normed = layer_norm(ordered.astype(jnp.float32)).astype(jnp.bfloat16)

    def project(weight):
        return jax.nn.silu(jnp.dot(normed, weight, preferred_element_type=jnp.float32)).astype(jnp.bfloat16)
    gate_rows = project(w_proj[0])
    value_rows = project(w_proj[1])
    query_rows = project(w_proj[2])
    key_rows = project(w_proj[3])
    user_ends = jnp.cumsum(user_lengths).astype(jnp.int32)
    block_total = SEQ // L_DEV
    query_blocks = query_rows.reshape(block_total, L_DEV, H, DH)
    key_blocks = key_rows.reshape(block_total, L_DEV, H, DH)
    value_blocks = value_rows.reshape(block_total, L_DEV, H, DH)
    block_starts = jnp.arange(block_total, dtype=jnp.int32) * L_DEV

    def attend(block_args):
        query_block, query_start = block_args
        query_pos = query_start + jnp.arange(L_DEV, dtype=jnp.int32)
        query_users = user_index(query_pos, user_ends)

        def visit_keys(running, inputs):
            key_block, value_block, key_start = inputs
            key_pos = key_start + jnp.arange(L_DEV, dtype=jnp.int32)
            key_users = user_index(key_pos, user_ends)
            allowed = (key_pos[None, :] <= query_pos[:, None]) & (key_users[None, :] == query_users[:, None])
            scores = jnp.einsum('lhd,nhd->hln', query_block.astype(jnp.float32), key_block.astype(jnp.float32))
            weights = jnp.where(allowed[None], jax.nn.silu(scores), 0.0).astype(jnp.bfloat16)
            summed = jnp.einsum('hln,nhd->lhd', weights.astype(jnp.float32), value_block.astype(jnp.float32))
            return (running + summed, None)
        start_sum = jnp.zeros((L_DEV, H, DH), jnp.float32)
        result, _ = lax.scan(visit_keys, start_sum, (key_blocks, value_blocks, block_starts))
        return result
    attended = lax.map(attend, (query_blocks, block_starts)).reshape(SEQ, D)
    gated_rows = (layer_norm(attended) * gate_rows.astype(jnp.float32)).astype(jnp.bfloat16)
    layer_out = ordered.astype(jnp.float32) + jnp.dot(gated_rows, w_out, preferred_element_type=jnp.float32)
    return layer_out.astype(jnp.bfloat16)
```

```python
import jax
import jax.numpy as jnp
from jax import lax
from jax.experimental import pallas as pl
from jax.experimental.pallas import tpu as pltpu
from jax.sharding import PartitionSpec as P

D = 1024
DH = 64
RB = 16


eps_norm = 1e-05


def from_behind(block, axis, distance):
    devices = range(lax.axis_size(axis))
    route = [((i - distance) % len(devices), i) for i in devices]
    return lax.ppermute(block, axis, route)


def user_index(positions, user_ends):
    return jnp.sum((positions[:, None] >= user_ends[None, :]).astype(jnp.int32), axis=1)


def body(events, w_proj, w_out, block_target, user_lengths):
    rows_here = events.shape[0]
    col_width = events.shape[1]
    seq_count = lax.axis_size("seq")
    seq_index = lax.axis_index("seq")
    block_count = rows_here // RB
    per_owner = block_count // seq_count

    def window_position(shard, local):
        return shard * rows_here + local

    owners = block_target // block_count
    slots = block_target % block_count
    my_owners = lax.dynamic_slice_in_dim(owners, seq_index * block_count, block_count)
    send_order = jnp.argsort(my_owners, stable=True)
    outgoing = events.reshape(block_count, RB, col_width)[send_order]
    outgoing = outgoing.reshape(seq_count, per_owner, RB, col_width)
    incoming = lax.all_to_all(outgoing, "seq", split_axis=0, concat_axis=0, tiled=True)
    arrived = jnp.argsort(jnp.where(owners == seq_index, 0, 1), stable=True)[:block_count]
    slot_ids = slots[arrived]
    placed = incoming.reshape(block_count, RB, col_width)[jnp.argsort(slot_ids)]
    ordered = placed.reshape(rows_here, col_width)
    widened = ordered.astype(jnp.float32)
    row_sum, row_squares = lax.psum(
        (jnp.sum(widened, axis=1), jnp.sum(widened * widened, axis=1)), "head"
    )
    mean_value = row_sum / D
    square_mean = row_squares / D
    normed = (
        (widened - mean_value[:, None])
        * lax.rsqrt(square_mean - mean_value * mean_value + eps_norm)[:, None]
    ).astype(jnp.bfloat16)
    weight_rows = w_proj
    projected = jnp.einsum(
        "ln,jnc->jlc",
        lax.all_gather(normed, "head", axis=1, tiled=True),
        weight_rows,
        preferred_element_type=jnp.float32,
    )
    activated = jax.nn.silu(projected).astype(jnp.bfloat16)
    gate_rows = activated[0]
    value_rows = activated[1]
    query_rows = activated[2]
    key_rows = activated[3]
    user_ends = jnp.cumsum(user_lengths)
    head_count = col_width // DH
    query_heads = query_rows.reshape(rows_here, head_count, DH)
    local_rows = jnp.arange(rows_here, dtype=jnp.int32)
    query_pos = window_position(seq_index, local_rows)
    query_users = user_index(query_pos, user_ends)
    zero_sum = jnp.zeros((rows_here, col_width), jnp.float32)

    def key_term(key_piece, value_piece, key_pos):
        row_count = key_piece.shape[0]
        key_heads = key_piece.reshape(row_count, head_count, DH)
        value_heads = value_piece.reshape(row_count, head_count, DH)
        key_users = user_index(key_pos, user_ends)
        allowed = (key_pos[None, :] <= query_pos[:, None]) & (
            key_users[None, :] == query_users[:, None]
        )
        scores = jnp.einsum(
            "lhd,nhd->hln", query_heads, key_heads, preferred_element_type=jnp.float32
        )
        weights = jnp.where(allowed[None], jax.nn.silu(scores), 0.0).astype(jnp.bfloat16)
        summed = jnp.einsum(
            "hln,nhd->lhd", weights, value_heads, preferred_element_type=jnp.float32
        )
        return summed.reshape(rows_here, col_width)

    def guarded_term(key_piece, value_piece, key_pos):
        return key_term(key_piece, value_piece, key_pos)

    def sweep_piece(running, key_piece, value_piece, key_pos):
        row_count = key_piece.shape[0]
        block_rows = min(row_count, 1024)
        rounds = row_count // block_rows

        def visit_block(partial_sum, inputs):
            key_block, value_block, block_pos = inputs
            return (partial_sum + guarded_term(key_block, value_block, block_pos), None)

        key_stack = key_piece.reshape(rounds, block_rows, col_width)
        value_stack = value_piece.reshape(rounds, block_rows, col_width)
        pos_stack = key_pos.reshape(rounds, block_rows)
        running, _ = lax.scan(visit_block, running, (key_stack, value_stack, pos_stack))
        return running

    stacked = jnp.stack([key_rows, value_rows])
    own_block = sweep_piece(zero_sum, key_rows, value_rows, query_pos)

    def relay_step(offset, loop_state):
        running, carried = loop_state
        carried = from_behind(carried, "seq", 1)
        source_shard = (seq_index - offset + seq_count) % seq_count
        running = sweep_piece(
            running, carried[0], carried[1], window_position(source_shard, local_rows)
        )
        return (running, carried)

    attended, _ = lax.fori_loop(1, seq_count, relay_step, (own_block, stacked))
    att_sum, att_squares = lax.psum(
        (jnp.sum(attended, axis=1), jnp.sum(attended * attended, axis=1)), "head"
    )
    att_mean = att_sum / D
    att_square_mean = att_squares / D
    scaled = (attended - att_mean[:, None]) * lax.rsqrt(
        att_square_mean - att_mean * att_mean + eps_norm
    )[:, None]
    gated_rows = (scaled * gate_rows.astype(jnp.float32)).astype(jnp.bfloat16)
    weight_rows = w_out
    projected_out = jnp.dot(
        lax.all_gather(gated_rows, "head", axis=1, tiled=True),
        weight_rows,
        preferred_element_type=jnp.float32,
    )
    finished = (widened + projected_out).astype(jnp.bfloat16)
    return finished


def team_plan(mesh):
    return jax.sharding.Mesh(
        mesh.devices.reshape(2, 2, 2, mesh.devices.shape[2] // 2, 2),
        ("half", "zlo", "head", "y", "core"),
    )


ROUTE = ("half", "zlo", "head", "core")


def route(rule):
    pairs = []
    for half in range(2):
        for zlo in range(2):
            for head in range(2):
                for core in range(2):
                    to = rule(half, zlo, head, core)
                    if to is not None:
                        pairs.append(
                            (
                                ((half * 2 + zlo) * 2 + head) * 2 + core,
                                ((to[0] * 2 + to[1]) * 2 + to[2]) * 2 + to[3],
                            )
                        )
    return pairs


def move(value, rule):
    return lax.ppermute(value, ROUTE, route(rule))


def to_partner(half, zlo, head, core):
    if core == half:
        return (half, 1 - zlo, head, 1 - half)
    return None


def to_other_team(half, zlo, head, core):
    if core == half:
        return None
    other = 1 - half
    inner = (zlo ^ half) == 1
    return (other, 1 - other, head, other if inner else 1 - other)


def inner_to_outer(half, zlo, head, core):
    if (zlo ^ half) == 1:
        return (half, 1 - zlo, head, core)
    return None


def across(select):
    def rule(half, zlo, head, core):
        if select(half, zlo, head, core):
            return (half, zlo, 1 - head, core)
        return None

    return rule


def other_core(half, zlo, head, core):
    return (half, zlo, head, 1 - core)


def project_kernel(info, own_a, own_b, other_a, other_b, w_ref, mine_ref, sib_ref, own_v, other_v, sems):
    rows = own_v.shape[0]
    width = own_v.shape[1]
    first = info[0] == 0

    @pl.when(first)
    def _():
        pltpu.make_async_copy(own_a, own_v, sems.at[0]).start()
        pltpu.make_async_copy(other_a, other_v, sems.at[1]).start()

    @pl.when(jnp.logical_not(first))
    def _():
        pltpu.make_async_copy(own_b, own_v, sems.at[0]).start()
        pltpu.make_async_copy(other_b, other_v, sems.at[1]).start()

    pltpu.make_async_copy(own_a, own_v, sems.at[0]).wait()
    pltpu.make_async_copy(other_a, other_v, sems.at[1]).wait()
    own_rows = pl.multiple_of(info[1] * width, width)
    other_rows = pl.multiple_of(info[2] * width, width)
    low_core = info[3] == 0
    step = 128

    @pl.loop(0, rows // step)
    def _(i):
        at = pl.ds(pl.multiple_of(i * step, step), step)
        a = own_v[at, :].astype(jnp.float32)
        b = other_v[at, :].astype(jnp.float32)
        mean = (jnp.sum(a, axis=1, keepdims=True) + jnp.sum(b, axis=1, keepdims=True)) / (2 * width)
        square = (
            jnp.sum(a * a, axis=1, keepdims=True) + jnp.sum(b * b, axis=1, keepdims=True)
        ) / (2 * width)
        scale = lax.rsqrt(square - mean * mean + eps_norm)
        a = ((a - mean) * scale).astype(jnp.bfloat16)
        b = ((b - mean) * scale).astype(jnp.bfloat16)
        for j in range(4):
            z = jnp.dot(
                a, w_ref[j, pl.ds(own_rows, width), :], preferred_element_type=jnp.float32
            ) + jnp.dot(
                b, w_ref[j, pl.ds(other_rows, width), :], preferred_element_type=jnp.float32
            )
            t = 0.5 * z
            act = (t + t * jnp.tanh(t)).astype(jnp.bfloat16)
            low, high = act[:, :128], act[:, 128:]
            cols = pl.ds(j * 128, 128)
            mine_ref[at, cols] = jnp.where(low_core, low, high)
            sib_ref[at, cols] = jnp.where(low_core, high, low)


def project(info, own_a, own_b, other_a, other_b, w, zlo):
    rows, width = own_a.shape
    anywhere = pl.BlockSpec(memory_space=pl.ANY)
    out = jax.ShapeDtypeStruct((rows, 512), jnp.bfloat16)
    return pl.pallas_call(
        project_kernel,
        out_shape=(out, out),
        in_specs=[pl.BlockSpec(memory_space=pltpu.SMEM)] + [anywhere] * 4 + [pl.BlockSpec(memory_space=pltpu.VMEM)],
        out_specs=(pl.BlockSpec(memory_space=pltpu.VMEM),) * 2,
        scratch_shapes=[
            pltpu.VMEM((rows, width), jnp.bfloat16),
            pltpu.VMEM((rows, width), jnp.bfloat16),
            pltpu.SemaphoreType.DMA((2,)),
        ],
        compiler_params=pltpu.CompilerParams(vmem_limit_bytes=40 * 1024 * 1024),
        cost_estimate=pl.CostEstimate(
            flops=2 * rows * D * 1024, bytes_accessed=rows * D * 4 + w.size * 2, transcendentals=rows * 1024
        ),
    )(info, own_a, own_b, other_a, other_b, w)


TQ = 256
TK = 512


def attend_kernel(info, targets, lengths, *refs):
    pieces, (att_ref, u_ref, stat_ref, q_s, v0, v1, k_s, k0, k1) = refs[:-9], refs[-9:]
    seq = att_ref.shape[0]
    lane = lax.broadcasted_iota(jnp.int32, (RB, 128), 1)
    low = lane < DH
    zero = jnp.zeros((RB, 128), jnp.bfloat16)

    for n, piece in enumerate(pieces):
        base = info[n]

        @pl.loop(0, piece.shape[0] // RB, unroll=4)
        def _(b):
            frm = pl.ds(pl.multiple_of(b * RB, RB), RB)
            to = pl.ds(pl.multiple_of(targets[base + b] * RB, RB), RB)
            u_ref[to, :] = piece[frm, 0:128]
            v = piece[frm, 128:256]
            v0[to, :] = jnp.where(low, v, zero)
            v1[to, :] = jnp.where(low, zero, v)
            q_s[to, :] = piece[frm, 256:384] * 0.5
            k_s[to, :] = piece[frm, 384:512]

    row = lax.broadcasted_iota(jnp.int32, (128, 256), 0)

    @pl.loop(0, seq // 256)
    def _(i):
        at = pl.ds(pl.multiple_of(i * 256, 256), 256)
        kt = k_s[at, :].T
        k0[:, at] = jnp.where(row < DH, kt, jnp.zeros_like(kt))
        k1[:, at] = jnp.where(row < DH, jnp.zeros_like(kt), kt)

    ends = []
    total = jnp.int32(0)
    for i in range(lengths.shape[0]):
        total = total + lengths[i]
        ends.append(total)

    def start_of(p):
        best = p * 0
        for e in ends:
            best = jnp.where(p >= e, e, best)
        return best

    @pl.loop(0, seq // TQ)
    def _(qi):
        q0 = qi * TQ
        at = pl.ds(pl.multiple_of(q0, TQ), TQ)
        q = q_s[at, :]

        def tile(j, acc, masked):
            ks = pl.ds(pl.multiple_of(j * TK, TK), TK)
            if masked:
                qp = q0 + lax.broadcasted_iota(jnp.int32, (TQ, 1), 0)
                kp = j * TK + lax.broadcasted_iota(jnp.int32, (1, TK), 1)
                ok = (kp <= qp) & (kp >= start_of(qp))
            for kt, vv in ((k0, v0), (k1, v1)):
                t = jnp.dot(q, kt[:, ks], preferred_element_type=jnp.float32)
                w = t + t * jnp.tanh(t)
                if masked:
                    w = jnp.where(ok, w, 0.0)
                acc = acc + jnp.dot(
                    w.astype(jnp.bfloat16), vv[ks, :], preferred_element_type=jnp.float32
                )
            return acc

        lo = start_of(q0) // TK
        last = start_of(q0 + TQ - 1)
        hi = (q0 + TQ + TK - 1) // TK
        diag = q0 // TK
        mid = jnp.minimum((last + TK - 1) // TK, diag)
        mid = jnp.maximum(mid, lo)
        acc = jnp.zeros((TQ, 128), jnp.float32)
        acc = lax.fori_loop(lo, mid, lambda j, c: tile(j, c, True), acc)
        acc = lax.fori_loop(mid, diag, lambda j, c: tile(j, c, False), acc)
        acc = lax.fori_loop(jnp.maximum(mid, diag), hi, lambda j, c: tile(j, c, True), acc)
        att_ref[at, :] = acc
        flip = acc.T
        stat_ref[0:1, at] = jnp.sum(flip, axis=0, keepdims=True)
        stat_ref[1:2, at] = jnp.sum(flip * flip, axis=0, keepdims=True)


def attend(info, targets, lengths, pieces):
    seq = sum(p.shape[0] for p in pieces)
    smem = pl.BlockSpec(memory_space=pltpu.SMEM)
    vmem = pl.BlockSpec(memory_space=pltpu.VMEM)
    return pl.pallas_call(
        attend_kernel,
        out_shape=(
            jax.ShapeDtypeStruct((seq, 128), jnp.float32),
            jax.ShapeDtypeStruct((seq, 128), jnp.bfloat16),
            jax.ShapeDtypeStruct((2, seq), jnp.float32),
        ),
        in_specs=[smem] * 3 + [vmem] * len(pieces),
        out_specs=(vmem,) * 3,
        scratch_shapes=[pltpu.VMEM((seq, 128), jnp.bfloat16)] * 4
        + [pltpu.VMEM((128, seq), jnp.bfloat16)] * 2,
        compiler_params=pltpu.CompilerParams(vmem_limit_bytes=40 * 1024 * 1024),
        cost_estimate=pl.CostEstimate(
            flops=2 * seq * seq * 128, bytes_accessed=seq * 128 * 14, transcendentals=seq * seq
        ),
    )(info, targets, lengths, *pieces)


def gate_kernel(info, att_ref, u_ref, stat_ref, *outs):
    rows = outs[0].shape[0]
    step = 256
    for k, out in enumerate(outs):
        block = lax.rem(info[0] + k, len(outs))

        @pl.loop(0, rows // step)
        def _(i):
            at = pl.ds(pl.multiple_of(block * rows + i * step, step), step)
            mean = stat_ref[0:1, at] / D
            square = stat_ref[1:2, at] / D
            scale = lax.rsqrt(square - mean * mean + eps_norm)
            mean = jnp.broadcast_to(mean, (128, step)).T
            scale = jnp.broadcast_to(scale, (128, step)).T
            gated = ((att_ref[at, :] - mean) * scale) * u_ref[at, :].astype(jnp.float32)
            out[pl.ds(pl.multiple_of(i * step, step), step), :] = gated.astype(jnp.bfloat16)


def gate(info, att, u, stat, count):
    rows = att.shape[0] // count
    vmem = pl.BlockSpec(memory_space=pltpu.VMEM)
    out = jax.ShapeDtypeStruct((rows, 128), jnp.bfloat16)
    return pl.pallas_call(
        gate_kernel,
        out_shape=(out,) * count,
        in_specs=[pl.BlockSpec(memory_space=pltpu.SMEM)] + [vmem] * 3,
        out_specs=(vmem,) * count,
        compiler_params=pltpu.CompilerParams(vmem_limit_bytes=40 * 1024 * 1024),
        cost_estimate=pl.CostEstimate(flops=att.size * 8, bytes_accessed=att.size * 8, transcendentals=0),
    )(info, att, u, stat)


def outgoing_kernel(info, targets, events_ref, out_ref):
    count = out_ref.shape[0]
    blocks = events_ref.shape[0] // RB
    base = info[0] * blocks

    def step(b, filled):
        owner = targets[base + b] // blocks
        place = jnp.int32(0)
        for k in range(count):
            place = jnp.where(owner == k, filled[k], place)
        frm = pl.ds(pl.multiple_of(b * RB, RB), RB)
        to = pl.ds(pl.multiple_of(place * RB, RB), RB)
        out_ref[pl.ds(owner, 1), to, :] = events_ref[frm, :][None]
        return tuple(filled[k] + (owner == k).astype(jnp.int32) for k in range(count))

    lax.fori_loop(0, blocks, step, (jnp.int32(0),) * count)


def outgoing(info, targets, events, count):
    smem = pl.BlockSpec(memory_space=pltpu.SMEM)
    vmem = pl.BlockSpec(memory_space=pltpu.VMEM)
    return pl.pallas_call(
        outgoing_kernel,
        out_shape=jax.ShapeDtypeStruct((count, events.shape[0] // count, events.shape[1]), events.dtype),
        in_specs=[smem, smem, vmem],
        out_specs=vmem,
        cost_estimate=pl.CostEstimate(flops=0, bytes_accessed=events.size * 4, transcendentals=0),
    )(info, targets, events)


def place_kernel(info, targets, in_ref, out_ref):
    blocks = out_ref.shape[0] // RB

    def step(g, filled):
        t = targets[g]
        mine = t // blocks == info[0]

        @pl.when(mine)
        def _():
            frm = pl.ds(pl.multiple_of(filled * RB, RB), RB)
            to = pl.ds(pl.multiple_of(lax.rem(t, blocks) * RB, RB), RB)
            out_ref[to, :] = in_ref[frm, :]

        return filled + mine.astype(jnp.int32)

    lax.fori_loop(0, targets.shape[0], step, jnp.int32(0))


def place(info, targets, incoming):
    smem = pl.BlockSpec(memory_space=pltpu.SMEM)
    vmem = pl.BlockSpec(memory_space=pltpu.VMEM)
    return pl.pallas_call(
        place_kernel,
        out_shape=jax.ShapeDtypeStruct(incoming.shape, incoming.dtype),
        in_specs=[smem, smem, vmem],
        out_specs=vmem,
        cost_estimate=pl.CostEstimate(flops=0, bytes_accessed=incoming.size * 4, transcendentals=0),
    )(info, targets, incoming)


def finish_kernel(info, res_ref, w_ref, *refs):
    pieces, out_ref = refs[:-1], refs[-1]
    step = 256
    rows = res_ref.shape[0]

    @pl.loop(0, rows // step)
    def _(i):
        at = pl.ds(pl.multiple_of(i * step, step), step)
        acc = res_ref[at, :].astype(jnp.float32)
        for n, piece in enumerate(pieces):
            feats = pl.ds(pl.multiple_of(info[n] * 128, 128), 128)
            acc = acc + jnp.dot(piece[at, :], w_ref[feats, :], preferred_element_type=jnp.float32)
        out_ref[at, :] = acc.astype(out_ref.dtype)


def finish(info, residual, w_out, pieces):
    vmem = pl.BlockSpec(memory_space=pltpu.VMEM)
    return pl.pallas_call(
        finish_kernel,
        out_shape=jax.ShapeDtypeStruct(residual.shape, jnp.bfloat16),
        in_specs=[pl.BlockSpec(memory_space=pltpu.SMEM)] + [vmem] * (2 + len(pieces)),
        out_specs=vmem,
        cost_estimate=pl.CostEstimate(
            flops=2 * residual.size * D, bytes_accessed=residual.size * 4 + w_out.size * 2, transcendentals=0
        ),
    )(info, residual, w_out, *pieces)


def team_body(events, w_proj, w_out, block_target, user_lengths):
    half, zlo = lax.axis_index("half"), lax.axis_index("zlo")
    head, core = lax.axis_index("head"), lax.axis_index("core")
    z = half * 2 + zlo
    foreign = core ^ half
    outer = 1 - (zlo ^ half)
    rows = events.shape[0]
    blocks = rows // RB
    targets_here = block_target
    other_ints = move(jnp.concatenate([block_target, user_lengths]), other_core)
    targets = jnp.where(foreign == 0, block_target, other_ints[: block_target.shape[0]])
    lengths = jnp.where(foreign == 0, user_lengths, other_ints[block_target.shape[0] :])
    w_mine = lax.dynamic_slice_in_dim(w_proj, zlo * 256, 256, axis=2)

    x_own = move(events, across(lambda half, zlo, head, core: core == half))
    partner = move(events, to_partner)
    parts = 2
    span = rows // parts
    remote = [move(events[i * span : (i + 1) * span], to_other_team) for i in range(parts)]
    x_partner = move(partner, across(lambda half, zlo, head, core: core != half))
    relayed = [move(r, inner_to_outer) for r in remote]
    x_inner = [move(r, across(lambda half, zlo, head, core: (zlo ^ half) == 1)) for r in remote]
    x_outer = [move(r, across(lambda half, zlo, head, core: (zlo ^ half) == 0)) for r in relayed]

    def ints(*values):
        return jnp.stack([jnp.asarray(v, jnp.int32) for v in values])

    mine1, sib1 = project(
        ints(foreign, head, 1 - head, core), events, partner, x_own, x_partner, w_mine, zlo
    )
    got1 = move(sib1, other_core)
    mine, got = [mine1], [got1]
    for i in range(parts):
        m, s = project(
            ints(outer, head, 1 - head, core), remote[i], relayed[i], x_inner[i], x_outer[i], w_mine, zlo
        )
        mine.append(m)
        got.append(move(s, other_core))

    near = half + 1
    near = jnp.where(half == 0, 2, 1)
    far = jnp.where(half == 0, 3, 0)
    slot1 = jnp.where(foreign == 0, z, z ^ 1)
    slot2 = jnp.where(foreign == 0, near, far)
    sib_slot1 = jnp.where(foreign == 0, z ^ 1, z)
    sib_slot2 = jnp.where(foreign == 0, far, near)
    part_blocks = span // RB
    starts = [slot1 * blocks]
    starts += [slot2 * blocks + i * part_blocks for i in range(parts)]
    starts += [sib_slot1 * blocks]
    starts += [sib_slot2 * blocks + i * part_blocks for i in range(parts)]
    att, u, stat = attend(ints(*starts), targets, lengths, mine + got)

    send = outgoing(ints(z), targets_here, events, 4)
    came = lax.all_to_all(send, ("half", "zlo"), split_axis=0, concat_axis=0, tiled=True)
    residual = place(ints(z), targets_here, came.reshape(rows, events.shape[1]))

    stat = lax.psum(stat, ("zlo", "head", "core"))
    me = zlo * 2 + core
    gated = gate(ints(me), att, u, stat, 4)

    def to_block(k):
        def rule(half, zlo, head, core):
            j = (zlo * 2 + core + k) % 4
            return (j // 2, j % 2, head, half)

        return rule

    pieces, feats = [], []
    for k in range(4):
        piece = move(gated[k], to_block(k))
        source = lax.rem(z - k + 4, 4)
        pieces += [piece, move(piece, across(lambda *p: True))]
        feats += [head * 4 + source, (1 - head) * 4 + source]
    return finish(ints(*feats), residual, w_out, pieces)


def solution(mesh):
    sizes = dict(mesh.shape)
    if sizes["seq"] == 4 and sizes["head"] == 2 and sizes["dp"] % 2 == 0:
        rows = P(("y", "core", "half", "zlo"), "head")
        part = P(("y", "core"))
        return jax.shard_map(
            team_body,
            mesh=team_plan(mesh),
            in_specs=(rows, P(None, None, "head"), P(None, "head"), part, part),
            out_specs=rows,
            check_vma=False,
        )
    placed = (P(("dp", "seq"), "head"), P(None, None, "head"), P(None, "head"), P("dp"), P("dp"))
    return jax.shard_map(
        body, mesh=mesh, in_specs=placed, out_specs=P(("dp", "seq"), "head"), check_vma=False
    )
```

```python
import jax
import jax.numpy as jnp
from jax import lax
from jax.experimental import pallas as pl
from jax.experimental.pallas import tpu as pltpu
from jax.sharding import PartitionSpec as P

D = 1024
DH = 64
RB = 16


eps_norm = 1e-05


def from_behind(block, axis, distance):
    devices = range(lax.axis_size(axis))
    route = [((i - distance) % len(devices), i) for i in devices]
    return lax.ppermute(block, axis, route)


def user_index(positions, user_ends):
    return jnp.sum((positions[:, None] >= user_ends[None, :]).astype(jnp.int32), axis=1)


def body(events, w_proj, w_out, block_target, user_lengths):
    rows_here = events.shape[0]
    col_width = events.shape[1]
    seq_count = lax.axis_size("seq")
    seq_index = lax.axis_index("seq")
    block_count = rows_here // RB
    per_owner = block_count // seq_count

    def window_position(shard, local):
        return shard * rows_here + local

    owners = block_target // block_count
    slots = block_target % block_count
    my_owners = lax.dynamic_slice_in_dim(owners, seq_index * block_count, block_count)
    send_order = jnp.argsort(my_owners, stable=True)
    outgoing = events.reshape(block_count, RB, col_width)[send_order]
    outgoing = outgoing.reshape(seq_count, per_owner, RB, col_width)
    incoming = lax.all_to_all(outgoing, "seq", split_axis=0, concat_axis=0, tiled=True)
    arrived = jnp.argsort(jnp.where(owners == seq_index, 0, 1), stable=True)[:block_count]
    slot_ids = slots[arrived]
    placed = incoming.reshape(block_count, RB, col_width)[jnp.argsort(slot_ids)]
    ordered = placed.reshape(rows_here, col_width)
    widened = ordered.astype(jnp.float32)
    row_sum, row_squares = lax.psum(
        (jnp.sum(widened, axis=1), jnp.sum(widened * widened, axis=1)), "head"
    )
    mean_value = row_sum / D
    square_mean = row_squares / D
    normed = (
        (widened - mean_value[:, None])
        * lax.rsqrt(square_mean - mean_value * mean_value + eps_norm)[:, None]
    ).astype(jnp.bfloat16)
    weight_rows = w_proj
    projected = jnp.einsum(
        "ln,jnc->jlc",
        lax.all_gather(normed, "head", axis=1, tiled=True),
        weight_rows,
        preferred_element_type=jnp.float32,
    )
    activated = jax.nn.silu(projected).astype(jnp.bfloat16)
    gate_rows = activated[0]
    value_rows = activated[1]
    query_rows = activated[2]
    key_rows = activated[3]
    user_ends = jnp.cumsum(user_lengths)
    head_count = col_width // DH
    query_heads = query_rows.reshape(rows_here, head_count, DH)
    local_rows = jnp.arange(rows_here, dtype=jnp.int32)
    query_pos = window_position(seq_index, local_rows)
    query_users = user_index(query_pos, user_ends)
    zero_sum = jnp.zeros((rows_here, col_width), jnp.float32)

    def key_term(key_piece, value_piece, key_pos):
        row_count = key_piece.shape[0]
        key_heads = key_piece.reshape(row_count, head_count, DH)
        value_heads = value_piece.reshape(row_count, head_count, DH)
        key_users = user_index(key_pos, user_ends)
        allowed = (key_pos[None, :] <= query_pos[:, None]) & (
            key_users[None, :] == query_users[:, None]
        )
        scores = jnp.einsum(
            "lhd,nhd->hln", query_heads, key_heads, preferred_element_type=jnp.float32
        )
        weights = jnp.where(allowed[None], jax.nn.silu(scores), 0.0).astype(jnp.bfloat16)
        summed = jnp.einsum(
            "hln,nhd->lhd", weights, value_heads, preferred_element_type=jnp.float32
        )
        return summed.reshape(rows_here, col_width)

    def guarded_term(key_piece, value_piece, key_pos):
        return key_term(key_piece, value_piece, key_pos)

    def sweep_piece(running, key_piece, value_piece, key_pos):
        row_count = key_piece.shape[0]
        block_rows = min(row_count, 1024)
        rounds = row_count // block_rows

        def visit_block(partial_sum, inputs):
            key_block, value_block, block_pos = inputs
            return (partial_sum + guarded_term(key_block, value_block, block_pos), None)

        key_stack = key_piece.reshape(rounds, block_rows, col_width)
        value_stack = value_piece.reshape(rounds, block_rows, col_width)
        pos_stack = key_pos.reshape(rounds, block_rows)
        running, _ = lax.scan(visit_block, running, (key_stack, value_stack, pos_stack))
        return running

    stacked = jnp.stack([key_rows, value_rows])
    own_block = sweep_piece(zero_sum, key_rows, value_rows, query_pos)

    def relay_step(offset, loop_state):
        running, carried = loop_state
        carried = from_behind(carried, "seq", 1)
        source_shard = (seq_index - offset + seq_count) % seq_count
        running = sweep_piece(
            running, carried[0], carried[1], window_position(source_shard, local_rows)
        )
        return (running, carried)

    attended, _ = lax.fori_loop(1, seq_count, relay_step, (own_block, stacked))
    att_sum, att_squares = lax.psum(
        (jnp.sum(attended, axis=1), jnp.sum(attended * attended, axis=1)), "head"
    )
    att_mean = att_sum / D
    att_square_mean = att_squares / D
    scaled = (attended - att_mean[:, None]) * lax.rsqrt(
        att_square_mean - att_mean * att_mean + eps_norm
    )[:, None]
    gated_rows = (scaled * gate_rows.astype(jnp.float32)).astype(jnp.bfloat16)
    weight_rows = w_out
    projected_out = jnp.dot(
        lax.all_gather(gated_rows, "head", axis=1, tiled=True),
        weight_rows,
        preferred_element_type=jnp.float32,
    )
    finished = (widened + projected_out).astype(jnp.bfloat16)
    return finished


def team_plan(mesh):
    return jax.sharding.Mesh(
        mesh.devices.reshape(2, 2, 2, mesh.devices.shape[2] // 2, 2),
        ("half", "zlo", "head", "y", "core"),
    )


ROUTE = ("half", "zlo", "head", "core")


def route(rule):
    pairs = []
    for half in range(2):
        for zlo in range(2):
            for head in range(2):
                for core in range(2):
                    to = rule(half, zlo, head, core)
                    if to is not None:
                        pairs.append(
                            (
                                ((half * 2 + zlo) * 2 + head) * 2 + core,
                                ((to[0] * 2 + to[1]) * 2 + to[2]) * 2 + to[3],
                            )
                        )
    return pairs


def move(value, rule):
    return lax.ppermute(value, ROUTE, route(rule))


def to_partner(half, zlo, head, core):
    if core == half:
        return (half, 1 - zlo, head, 1 - half)
    return None


def to_other_team(half, zlo, head, core):
    if core == half:
        return None
    other = 1 - half
    inner = (zlo ^ half) == 1
    return (other, 1 - other, head, other if inner else 1 - other)


def inner_to_outer(half, zlo, head, core):
    if (zlo ^ half) == 1:
        return (half, 1 - zlo, head, core)
    return None


def across(select):
    def rule(half, zlo, head, core):
        if select(half, zlo, head, core):
            return (half, zlo, 1 - head, core)
        return None

    return rule


def other_core(half, zlo, head, core):
    return (half, zlo, head, 1 - core)


def project_kernel(info, own_a, own_b, other_a, other_b, w_ref, mine_ref, sib_ref, own_v, other_v, sems):
    rows = own_v.shape[0]
    width = own_v.shape[1]
    first = info[0] == 0

    @pl.when(first)
    def _():
        pltpu.make_async_copy(own_a, own_v, sems.at[0]).start()
        pltpu.make_async_copy(other_a, other_v, sems.at[1]).start()

    @pl.when(jnp.logical_not(first))
    def _():
        pltpu.make_async_copy(own_b, own_v, sems.at[0]).start()
        pltpu.make_async_copy(other_b, other_v, sems.at[1]).start()

    pltpu.make_async_copy(own_a, own_v, sems.at[0]).wait()
    pltpu.make_async_copy(other_a, other_v, sems.at[1]).wait()
    own_rows = pl.multiple_of(info[1] * width, width)
    other_rows = pl.multiple_of(info[2] * width, width)
    low_core = info[3] == 0
    step = 128

    @pl.loop(0, rows // step)
    def _(i):
        at = pl.ds(pl.multiple_of(i * step, step), step)
        a = own_v[at, :].astype(jnp.float32)
        b = other_v[at, :].astype(jnp.float32)
        mean = (jnp.sum(a, axis=1, keepdims=True) + jnp.sum(b, axis=1, keepdims=True)) / (2 * width)
        square = (
            jnp.sum(a * a, axis=1, keepdims=True) + jnp.sum(b * b, axis=1, keepdims=True)
        ) / (2 * width)
        scale = lax.rsqrt(square - mean * mean + eps_norm)
        a = ((a - mean) * scale).astype(jnp.bfloat16)
        b = ((b - mean) * scale).astype(jnp.bfloat16)
        for j in range(4):
            z = jnp.dot(
                a, w_ref[j, pl.ds(own_rows, width), :], preferred_element_type=jnp.float32
            ) + jnp.dot(
                b, w_ref[j, pl.ds(other_rows, width), :], preferred_element_type=jnp.float32
            )
            t = 0.5 * z
            act = (t + t * jnp.tanh(t)).astype(jnp.bfloat16)
            low, high = act[:, :128], act[:, 128:]
            cols = pl.ds(j * 128, 128)
            mine_ref[at, cols] = jnp.where(low_core, low, high)
            sib_ref[at, cols] = jnp.where(low_core, high, low)


def project(info, own_a, own_b, other_a, other_b, w, zlo):
    rows, width = own_a.shape
    anywhere = pl.BlockSpec(memory_space=pl.ANY)
    out = jax.ShapeDtypeStruct((rows, 512), jnp.bfloat16)
    return pl.pallas_call(
        project_kernel,
        out_shape=(out, out),
        in_specs=[pl.BlockSpec(memory_space=pltpu.SMEM)] + [anywhere] * 4 + [pl.BlockSpec(memory_space=pltpu.VMEM)],
        out_specs=(pl.BlockSpec(memory_space=pltpu.VMEM),) * 2,
        scratch_shapes=[
            pltpu.VMEM((rows, width), jnp.bfloat16),
            pltpu.VMEM((rows, width), jnp.bfloat16),
            pltpu.SemaphoreType.DMA((2,)),
        ],
        compiler_params=pltpu.CompilerParams(vmem_limit_bytes=40 * 1024 * 1024),
        cost_estimate=pl.CostEstimate(
            flops=2 * rows * D * 1024, bytes_accessed=rows * D * 4 + w.size * 2, transcendentals=rows * 1024
        ),
    )(info, own_a, own_b, other_a, other_b, w)


TQ = 1536
TK = 512
SUB = 256
DSUB = 256


def attend_kernel(info, targets, lengths, *refs):
    pieces, (att_ref, u_ref, stat_ref, q_s, v0, v1, k0, k1) = refs[:-8], refs[-8:]
    seq = att_ref.shape[0]
    low = lax.broadcasted_iota(jnp.int32, (RB, 128), 1) < DH
    zero = jnp.zeros((RB, 128), jnp.bfloat16)
    for n, piece in enumerate(pieces):
        base = info[n]
        @pl.loop(0, piece.shape[0] // RB, unroll=8)
        def _(b):
            frm = pl.ds(pl.multiple_of(b * RB, RB), RB)
            to = pl.ds(pl.multiple_of(targets[base + b] * RB, RB), RB)
            u_ref[to, :] = piece[frm, 0:128]
            v = piece[frm, 128:256]
            v0[to, :] = jnp.where(low, v, zero)
            v1[to, :] = jnp.where(low, zero, v)
            q_s[to, :] = piece[frm, 256:384] * 0.5
            k = piece[frm, 384:512]
            k0[to, :] = jnp.where(low, k, zero)
            k1[to, :] = jnp.where(low, zero, k)
    ends = []
    total = jnp.int32(0)
    for i in range(lengths.shape[0]):
        total = total + lengths[i]
        ends.append(total)
    def start_of(p):
        best = p * 0
        for e in ends:
            best = jnp.where(p >= e, e, best)
        return best
    def term(q0, rows, k0_at, keys, first, causal):
        at = pl.ds(pl.multiple_of(q0, 256), rows)
        q = q_s[at, :]
        total = None
        for s in range(keys // SUB):
            ks = pl.ds(pl.multiple_of(k0_at + s * SUB, SUB), SUB)
            if first is not None:
                kp = k0_at + s * SUB + lax.broadcasted_iota(jnp.int32, (1, SUB), 1)
                ok = kp >= first
                if causal:
                    ok = ok & (kp <= q0 + lax.broadcasted_iota(jnp.int32, (rows, 1), 0))
            for kk, vv in ((k0, v0), (k1, v1)):
                t = lax.dot_general(q, kk[ks, :], (((1,), (1,)), ((), ())), preferred_element_type=jnp.float32)
                w = t + t * jnp.tanh(t)
                if first is not None:
                    w = jnp.where(ok, w, 0.0)
                d = jnp.dot(w.astype(jnp.bfloat16), vv[ks, :], preferred_element_type=jnp.float32)
                total = d if total is None else total + d
        att_ref[at, :] += total
    @pl.loop(0, seq // TQ)
    def _(qi):
        q0 = qi * TQ
        at = pl.ds(pl.multiple_of(q0, TQ), TQ)
        att_ref[at, :] = jnp.zeros((TQ, 128), jnp.float32)
        first = start_of(q0 + lax.broadcasted_iota(jnp.int32, (TQ, 1), 0))
        diag = q0 // TK
        lo = start_of(q0) // TK
        mid = jnp.minimum((start_of(q0 + TQ - 1) + TK - 1) // TK, diag)
        mid = jnp.maximum(mid, lo)
        @pl.loop(lo, mid)
        def _(j):
            term(q0, TQ, j * TK, TK, first, False)
        @pl.loop(mid, diag)
        def _(j):
            term(q0, TQ, j * TK, TK, None, False)
        for s in range(TQ // DSUB):
            term(q0 + s * DSUB, TQ - s * DSUB, q0 + s * DSUB, DSUB, first[s * DSUB :], True)
        for s in range(TQ // 256):
            part = pl.ds(pl.multiple_of(q0 + s * 256, 256), 256)
            flip = att_ref[part, :].T
            stat_ref[0:1, part] = jnp.sum(flip, axis=0, keepdims=True)
            stat_ref[1:2, part] = jnp.sum(flip * flip, axis=0, keepdims=True)
def attend(info, targets, lengths, pieces):
    seq = sum(p.shape[0] for p in pieces)
    smem = pl.BlockSpec(memory_space=pltpu.SMEM)
    vmem = pl.BlockSpec(memory_space=pltpu.VMEM)
    return pl.pallas_call(
        attend_kernel,
        out_shape=(jax.ShapeDtypeStruct((seq, 128), jnp.float32), jax.ShapeDtypeStruct((seq, 128), jnp.bfloat16), jax.ShapeDtypeStruct((2, seq), jnp.float32)),
        in_specs=[smem] * 3 + [vmem] * len(pieces), out_specs=(vmem,) * 3,
        scratch_shapes=[pltpu.VMEM((seq, 128), jnp.bfloat16)] * 5,
        compiler_params=pltpu.CompilerParams(vmem_limit_bytes=50 * 1024 * 1024),
        cost_estimate=pl.CostEstimate(
            flops=2 * seq * seq * 128, bytes_accessed=seq * 128 * 14, transcendentals=seq * seq
        ),
    )(info, targets, lengths, *pieces)


def gate_kernel(info, att_ref, u_ref, *refs):
    stats, outs = refs[:4], refs[4:]
    rows = outs[0].shape[0]
    step = 256
    for k, out in enumerate(outs):
        block = lax.rem(info[0] + k, len(outs))

        @pl.loop(0, rows // step)
        def _(i):
            at = pl.ds(pl.multiple_of(block * rows + i * step, step), step)
            sums = stats[0][:, at]
            for other in stats[1:]:
                sums = sums + other[:, at]
            mean = sums[0:1] / D
            square = sums[1:2] / D
            scale = lax.rsqrt(square - mean * mean + eps_norm)
            mean = jnp.broadcast_to(mean, (128, step)).T
            scale = jnp.broadcast_to(scale, (128, step)).T
            gated = ((att_ref[at, :] - mean) * scale) * u_ref[at, :].astype(jnp.float32)
            out[pl.ds(pl.multiple_of(i * step, step), step), :] = gated.astype(jnp.bfloat16)


def gate(info, att, u, stats, count):
    rows = att.shape[0] // count
    vmem = pl.BlockSpec(memory_space=pltpu.VMEM)
    out = jax.ShapeDtypeStruct((rows, 128), jnp.bfloat16)
    return pl.pallas_call(
        gate_kernel,
        out_shape=(out,) * count,
        in_specs=[pl.BlockSpec(memory_space=pltpu.SMEM)] + [vmem] * (2 + len(stats)),
        out_specs=(vmem,) * count,
        compiler_params=pltpu.CompilerParams(vmem_limit_bytes=40 * 1024 * 1024),
        cost_estimate=pl.CostEstimate(flops=att.size * 8, bytes_accessed=att.size * 8, transcendentals=0),
    )(info, att, u, *stats)


def outgoing_kernel(info, targets, events_ref, after_ref, out_ref):
    count = out_ref.shape[0]
    blocks = events_ref.shape[0] // RB
    base = info[0] * blocks

    @pl.loop(0, blocks, unroll=4)
    def _(b):
        t = targets[base + b]
        frm = pl.ds(pl.multiple_of(b * RB, RB), RB)
        to = pl.ds(pl.multiple_of(lax.rem(t, blocks // count) * RB, RB), RB)
        out_ref[pl.ds(t // blocks, 1), to, :] = events_ref[frm, :][None]


def outgoing(info, targets, events, after, count):
    smem = pl.BlockSpec(memory_space=pltpu.SMEM)
    vmem = pl.BlockSpec(memory_space=pltpu.VMEM)
    return pl.pallas_call(
        outgoing_kernel,
        out_shape=jax.ShapeDtypeStruct((count, events.shape[0] // count, events.shape[1]), events.dtype),
        in_specs=[smem, smem, vmem, pl.BlockSpec(memory_space=pl.ANY)],
        out_specs=vmem,
        cost_estimate=pl.CostEstimate(flops=0, bytes_accessed=events.size * 4, transcendentals=0),
    )(info, targets, events, after)


def finish_kernel(info, quarter, res_ref, w_ref, *refs):
    pieces, out_ref = refs[:-1], refs[-1]
    count, step = res_ref.shape[0], res_ref.shape[1]

    @pl.loop(0, count)
    def _(i):
        at = pl.ds(pl.multiple_of(quarter[i] * step, step), step)
        acc = res_ref[i].astype(jnp.float32)
        for n in range(0, len(pieces), 2):
            two = (n, n + 1)
            left = jnp.concatenate([pieces[m][at, :] for m in two], axis=1)
            right = jnp.concatenate(
                [w_ref[pl.ds(pl.multiple_of(info[m] * 128, 128), 128), :] for m in two], axis=0
            )
            acc = acc + jnp.dot(left, right, preferred_element_type=jnp.float32)
        out_ref[at, :] = acc.astype(out_ref.dtype)


def finish(info, quarter, residual, w_out, pieces):
    smem = pl.BlockSpec(memory_space=pltpu.SMEM)
    vmem = pl.BlockSpec(memory_space=pltpu.VMEM)
    rows = residual.shape[0] * residual.shape[1]
    return pl.pallas_call(
        finish_kernel,
        out_shape=jax.ShapeDtypeStruct((rows, residual.shape[2]), jnp.bfloat16),
        in_specs=[smem] * 2 + [vmem] * (2 + len(pieces)),
        out_specs=vmem,
        cost_estimate=pl.CostEstimate(
            flops=2 * residual.size * D, bytes_accessed=residual.size * 4 + w_out.size * 2, transcendentals=0
        ),
    )(info, quarter, residual, w_out, *pieces)


def team_body(events, w_proj, w_out, block_target, user_lengths):
    half, zlo = lax.axis_index("half"), lax.axis_index("zlo")
    head, core = lax.axis_index("head"), lax.axis_index("core")
    z = half * 2 + zlo
    foreign = core ^ half
    outer = 1 - (zlo ^ half)
    rows = events.shape[0]
    blocks = rows // RB
    targets_here = block_target
    other_ints = move(jnp.concatenate([block_target, user_lengths]), other_core)
    targets = jnp.where(foreign == 0, block_target, other_ints[: block_target.shape[0]])
    lengths = jnp.where(foreign == 0, user_lengths, other_ints[block_target.shape[0] :])
    w_mine = lax.dynamic_slice_in_dim(w_proj, zlo * 256, 256, axis=2)

    x_own = move(events, across(lambda half, zlo, head, core: core == half))
    partner = move(events, to_partner)
    parts = 2
    span = rows // parts
    remote = []
    for i in range(parts):
        chunk = events[i * span : (i + 1) * span]
        if remote:
            chunk, _ = lax.optimization_barrier((chunk, remote[-1]))
        remote.append(move(chunk, to_other_team))
    x_partner = move(partner, across(lambda half, zlo, head, core: core != half))
    relayed = [move(r, inner_to_outer) for r in remote]
    x_inner = [move(r, across(lambda half, zlo, head, core: (zlo ^ half) == 1)) for r in remote]
    x_outer = [move(r, across(lambda half, zlo, head, core: (zlo ^ half) == 0)) for r in relayed]

    def ints(*values):
        return jnp.stack([jnp.asarray(v, jnp.int32) for v in values])

    mine1, sib1 = project(
        ints(foreign, head, 1 - head, core), events, partner, x_own, x_partner, w_mine, zlo
    )
    got1 = move(sib1, other_core)
    mine, got = [mine1], [got1]
    for i in range(parts):
        m, s = project(
            ints(outer, head, 1 - head, core), remote[i], relayed[i], x_inner[i], x_outer[i], w_mine, zlo
        )
        mine.append(m)
        got.append(move(s, other_core))

    near = half + 1
    near = jnp.where(half == 0, 2, 1)
    far = jnp.where(half == 0, 3, 0)
    slot1 = jnp.where(foreign == 0, z, z ^ 1)
    slot2 = jnp.where(foreign == 0, near, far)
    sib_slot1 = jnp.where(foreign == 0, z ^ 1, z)
    sib_slot2 = jnp.where(foreign == 0, far, near)
    part_blocks = span // RB
    starts = [slot1 * blocks]
    starts += [slot2 * blocks + i * part_blocks for i in range(parts)]
    starts += [sib_slot1 * blocks]
    starts += [sib_slot2 * blocks + i * part_blocks for i in range(parts)]
    att, u, stat = attend(ints(*starts), targets, lengths, mine + got)

    send = outgoing(ints(z), targets_here, events, mine[-1], 4)
    residual = lax.all_to_all(send, ("half", "zlo"), split_axis=0, concat_axis=0, tiled=True)
    by_shard = targets_here.reshape(4, blocks)
    quarter = jnp.max(
        jnp.where(by_shard // blocks == z, by_shard % blocks // (blocks // 4), 0), axis=1
    )

    stat = stat + move(stat, other_core)
    stats = [stat]
    for dz, dx in ((0, 1), (1, 0), (1, 1)):
        stats.append(
            move(stat, lambda half, zlo, head, core, dz=dz, dx=dx: (half, zlo ^ dz, head ^ dx, core))
        )
    me = zlo * 2 + core
    gated = gate(ints(me), att, u, stats, 4)

    def to_block(k):
        def rule(half, zlo, head, core):
            j = (zlo * 2 + core + k) % 4
            return (j // 2, j % 2, head, half)

        return rule

    pieces, feats = [], []
    for k in range(4):
        piece = move(gated[k], to_block(k))
        source = lax.rem(z - k + 4, 4)
        pieces += [piece, move(piece, across(lambda *p: True))]
        feats += [head * 4 + source, (1 - head) * 4 + source]
    return finish(ints(*feats), quarter, residual, w_out, pieces)


def solution(mesh):
    sizes = dict(mesh.shape)
    if sizes["seq"] == 4 and sizes["head"] == 2 and sizes["dp"] % 2 == 0:
        rows = P(("y", "core", "half", "zlo"), "head")
        part = P(("y", "core"))
        return jax.shard_map(
            team_body,
            mesh=team_plan(mesh),
            in_specs=(rows, P(None, None, "head"), P(None, "head"), part, part),
            out_specs=rows,
            check_vma=False,
        )
    placed = (P(("dp", "seq"), "head"), P(None, None, "head"), P(None, "head"), P("dp"), P("dp"))
    return jax.shard_map(
        body, mesh=mesh, in_specs=placed, out_specs=P(("dp", "seq"), "head"), check_vma=False
    )
```

```python
import functools

import jax
import jax.numpy as jnp
from jax import lax
from jax.experimental import pallas as pl
from jax.experimental.pallas import tpu as pltpu
from jax.sharding import PartitionSpec as P

D = 1024
DH = 64
RB = 16


eps_norm = 1e-05


def from_behind(block, axis, distance):
    devices = range(lax.axis_size(axis))
    route = [((i - distance) % len(devices), i) for i in devices]
    return lax.ppermute(block, axis, route)


def user_index(positions, user_ends):
    return jnp.sum((positions[:, None] >= user_ends[None, :]).astype(jnp.int32), axis=1)


def body(events, w_proj, w_out, block_target, user_lengths):
    rows_here = events.shape[0]
    col_width = events.shape[1]
    seq_count = lax.axis_size("seq")
    seq_index = lax.axis_index("seq")
    block_count = rows_here // RB
    per_owner = block_count // seq_count

    def window_position(shard, local):
        return shard * rows_here + local

    owners = block_target // block_count
    slots = block_target % block_count
    my_owners = lax.dynamic_slice_in_dim(owners, seq_index * block_count, block_count)
    send_order = jnp.argsort(my_owners, stable=True)
    outgoing = events.reshape(block_count, RB, col_width)[send_order]
    outgoing = outgoing.reshape(seq_count, per_owner, RB, col_width)
    incoming = lax.all_to_all(outgoing, "seq", split_axis=0, concat_axis=0, tiled=True)
    arrived = jnp.argsort(jnp.where(owners == seq_index, 0, 1), stable=True)[:block_count]
    slot_ids = slots[arrived]
    placed = incoming.reshape(block_count, RB, col_width)[jnp.argsort(slot_ids)]
    ordered = placed.reshape(rows_here, col_width)
    widened = ordered.astype(jnp.float32)
    row_sum, row_squares = lax.psum(
        (jnp.sum(widened, axis=1), jnp.sum(widened * widened, axis=1)), "head"
    )
    mean_value = row_sum / D
    square_mean = row_squares / D
    normed = (
        (widened - mean_value[:, None])
        * lax.rsqrt(square_mean - mean_value * mean_value + eps_norm)[:, None]
    ).astype(jnp.bfloat16)
    weight_rows = w_proj
    projected = jnp.einsum(
        "ln,jnc->jlc",
        lax.all_gather(normed, "head", axis=1, tiled=True),
        weight_rows,
        preferred_element_type=jnp.float32,
    )
    activated = jax.nn.silu(projected).astype(jnp.bfloat16)
    gate_rows = activated[0]
    value_rows = activated[1]
    query_rows = activated[2]
    key_rows = activated[3]
    user_ends = jnp.cumsum(user_lengths)
    head_count = col_width // DH
    query_heads = query_rows.reshape(rows_here, head_count, DH)
    local_rows = jnp.arange(rows_here, dtype=jnp.int32)
    query_pos = window_position(seq_index, local_rows)
    query_users = user_index(query_pos, user_ends)
    zero_sum = jnp.zeros((rows_here, col_width), jnp.float32)

    def key_term(key_piece, value_piece, key_pos):
        row_count = key_piece.shape[0]
        key_heads = key_piece.reshape(row_count, head_count, DH)
        value_heads = value_piece.reshape(row_count, head_count, DH)
        key_users = user_index(key_pos, user_ends)
        allowed = (key_pos[None, :] <= query_pos[:, None]) & (
            key_users[None, :] == query_users[:, None]
        )
        scores = jnp.einsum(
            "lhd,nhd->hln", query_heads, key_heads, preferred_element_type=jnp.float32
        )
        weights = jnp.where(allowed[None], jax.nn.silu(scores), 0.0).astype(jnp.bfloat16)
        summed = jnp.einsum(
            "hln,nhd->lhd", weights, value_heads, preferred_element_type=jnp.float32
        )
        return summed.reshape(rows_here, col_width)

    def guarded_term(key_piece, value_piece, key_pos):
        return key_term(key_piece, value_piece, key_pos)

    def sweep_piece(running, key_piece, value_piece, key_pos):
        row_count = key_piece.shape[0]
        block_rows = min(row_count, 1024)
        rounds = row_count // block_rows

        def visit_block(partial_sum, inputs):
            key_block, value_block, block_pos = inputs
            return (partial_sum + guarded_term(key_block, value_block, block_pos), None)

        key_stack = key_piece.reshape(rounds, block_rows, col_width)
        value_stack = value_piece.reshape(rounds, block_rows, col_width)
        pos_stack = key_pos.reshape(rounds, block_rows)
        running, _ = lax.scan(visit_block, running, (key_stack, value_stack, pos_stack))
        return running

    stacked = jnp.stack([key_rows, value_rows])
    own_block = sweep_piece(zero_sum, key_rows, value_rows, query_pos)

    def relay_step(offset, loop_state):
        running, carried = loop_state
        carried = from_behind(carried, "seq", 1)
        source_shard = (seq_index - offset + seq_count) % seq_count
        running = sweep_piece(
            running, carried[0], carried[1], window_position(source_shard, local_rows)
        )
        return (running, carried)

    attended, _ = lax.fori_loop(1, seq_count, relay_step, (own_block, stacked))
    att_sum, att_squares = lax.psum(
        (jnp.sum(attended, axis=1), jnp.sum(attended * attended, axis=1)), "head"
    )
    att_mean = att_sum / D
    att_square_mean = att_squares / D
    scaled = (attended - att_mean[:, None]) * lax.rsqrt(
        att_square_mean - att_mean * att_mean + eps_norm
    )[:, None]
    gated_rows = (scaled * gate_rows.astype(jnp.float32)).astype(jnp.bfloat16)
    weight_rows = w_out
    projected_out = jnp.dot(
        lax.all_gather(gated_rows, "head", axis=1, tiled=True),
        weight_rows,
        preferred_element_type=jnp.float32,
    )
    finished = (widened + projected_out).astype(jnp.bfloat16)
    return finished


def team_plan(mesh):
    return jax.sharding.Mesh(
        mesh.devices.reshape(2, 2, 2, mesh.devices.shape[2] // 2, 2),
        ("half", "zlo", "head", "y", "core"),
    )


ROUTE = ("half", "zlo", "head", "core")


def route(rule):
    pairs = []
    for half in range(2):
        for zlo in range(2):
            for head in range(2):
                for core in range(2):
                    to = rule(half, zlo, head, core)
                    if to is not None:
                        pairs.append(
                            (
                                ((half * 2 + zlo) * 2 + head) * 2 + core,
                                ((to[0] * 2 + to[1]) * 2 + to[2]) * 2 + to[3],
                            )
                        )
    return pairs


def move(value, rule):
    return lax.ppermute(value, ROUTE, route(rule))


def to_partner(half, zlo, head, core):
    if core == half:
        return (half, 1 - zlo, head, 1 - half)
    return None


def to_other_team(half, zlo, head, core):
    if core == half:
        return None
    other = 1 - half
    inner = (zlo ^ half) == 1
    return (other, 1 - other, head, other if inner else 1 - other)


def inner_to_outer(half, zlo, head, core):
    if (zlo ^ half) == 1:
        return (half, 1 - zlo, head, core)
    return None


def across(select):
    def rule(half, zlo, head, core):
        if select(half, zlo, head, core):
            return (half, zlo, 1 - head, core)
        return None

    return rule


def other_core(half, zlo, head, core):
    return (half, zlo, head, 1 - core)


def project_kernel(waited, info, lengths, *refs):
    pairs = refs[: -6 - waited]
    w_ref, mine_ref, sib_ref, own_v, other_v, sems = refs[-6:]
    pairs = [(pairs[i], pairs[i + 1]) for i in range(0, len(pairs), 2)]
    rows, width = own_v.shape
    step = rows // 2

    def copies(pair, i):
        at = pl.ds(i * step, step)
        return (
            pltpu.make_async_copy(pair[0].at[at, :], own_v.at[at, :], sems.at[2 * i]),
            pltpu.make_async_copy(pair[1].at[at, :], other_v.at[at, :], sems.at[2 * i + 1]),
        )

    for n, pair in enumerate(pairs):

        @pl.when(info[0] == n)
        def _():
            for i in range(2):
                for copy in copies(pair, i):
                    copy.start()

    own_rows = pl.multiple_of(info[1] * width, width)
    other_rows = pl.multiple_of(info[2] * width, width)
    low_core = info[3] == 0
    for i in range(2):
        for copy in copies(pairs[0], i):
            copy.wait()
        at = pl.ds(i * step, step)
        a = own_v[at, :].astype(jnp.float32)
        b = other_v[at, :].astype(jnp.float32)
        mean = (jnp.sum(a, axis=1, keepdims=True) + jnp.sum(b, axis=1, keepdims=True)) / (2 * width)
        square = (
            jnp.sum(a * a, axis=1, keepdims=True) + jnp.sum(b * b, axis=1, keepdims=True)
        ) / (2 * width)
        scale = lax.rsqrt(square - mean * mean + eps_norm)
        a = ((a - mean) * scale).astype(jnp.bfloat16)
        b = ((b - mean) * scale).astype(jnp.bfloat16)
        for j in range(4):
            z = jnp.dot(
                a, w_ref[j, pl.ds(own_rows, width), :], preferred_element_type=jnp.float32
            ) + jnp.dot(
                b, w_ref[j, pl.ds(other_rows, width), :], preferred_element_type=jnp.float32
            )
            t = 0.5 * z
            act = (t + t * jnp.tanh(t)).astype(jnp.bfloat16)
            low, high = act[:, :128], act[:, 128:]
            cols = pl.ds(j * 128, 128)
            mine_ref[at, cols] = jnp.where(low_core, low, high)
            sib_ref[at, cols] = jnp.where(low_core, high, low)


def project(info, lengths, pairs, w, after):
    rows, width = pairs[0].shape
    anywhere = pl.BlockSpec(memory_space=pl.ANY)
    vmem = pl.BlockSpec(memory_space=pltpu.VMEM)
    out = jax.ShapeDtypeStruct((rows, 512), jnp.bfloat16)
    return pl.pallas_call(
        functools.partial(project_kernel, len(after)),
        out_shape=(out, out),
        in_specs=[pl.BlockSpec(memory_space=pltpu.SMEM)] * 2 + [anywhere] * (len(pairs) + len(after)) + [vmem],
        out_specs=(vmem, vmem),
        scratch_shapes=[
            pltpu.VMEM((rows, width), jnp.bfloat16),
            pltpu.VMEM((rows, width), jnp.bfloat16),
            pltpu.SemaphoreType.DMA((4,)),
        ],
        compiler_params=pltpu.CompilerParams(vmem_limit_bytes=16 * 1024 * 1024),
        cost_estimate=pl.CostEstimate(
            flops=2 * rows * D * 1024, bytes_accessed=rows * D * 4 + w.size * 2, transcendentals=rows * 1024
        ),
    )(info, lengths, *pairs, *after, w)


TQ = 1536
TK = 512
SUB = 256
DSUB = 256


def attend_kernel(info, targets, lengths, *refs):
    pieces, (att_ref, u_ref, stat_ref, q_s, v0, v1, k0, k1) = refs[:-8], refs[-8:]
    seq = att_ref.shape[0]
    low = lax.broadcasted_iota(jnp.int32, (RB, 128), 1) < DH
    zero = jnp.zeros((RB, 128), jnp.bfloat16)
    for n, piece in enumerate(pieces):
        base = info[n]

        @pl.loop(0, piece.shape[0] // RB, unroll=8)
        def _(b):
            frm = pl.ds(pl.multiple_of(b * RB, RB), RB)
            to = pl.ds(pl.multiple_of(targets[base + b] * RB, RB), RB)
            u_ref[to, :] = piece[frm, 0:128]
            v = piece[frm, 128:256]
            v0[to, :] = jnp.where(low, v, zero)
            v1[to, :] = jnp.where(low, zero, v)
            q_s[to, :] = piece[frm, 256:384] * 0.5
            k = piece[frm, 384:512]
            k0[to, :] = jnp.where(low, k, zero)
            k1[to, :] = jnp.where(low, zero, k)
    ends = []
    total = jnp.int32(0)
    for i in range(lengths.shape[0]):
        total = total + lengths[i]
        ends.append(total)
    def start_of(p):
        best = p * 0
        for e in ends:
            best = jnp.where(p >= e, e, best)
        return best
    def term(q0, rows, k0_at, keys, first, causal):
        at = pl.ds(pl.multiple_of(q0, 256), rows)
        q = q_s[at, :]
        total = None
        for s in range(keys // SUB):
            ks = pl.ds(pl.multiple_of(k0_at + s * SUB, SUB), SUB)
            if first is not None:
                kp = k0_at + s * SUB + lax.broadcasted_iota(jnp.int32, (1, SUB), 1)
                ok = kp >= first
                if causal:
                    ok = ok & (kp <= q0 + lax.broadcasted_iota(jnp.int32, (rows, 1), 0))
            for kk, vv in ((k0, v0), (k1, v1)):
                t = lax.dot_general(q, kk[ks, :], (((1,), (1,)), ((), ())), preferred_element_type=jnp.float32)
                w = t + t * jnp.tanh(t)
                if first is not None:
                    w = jnp.where(ok, w, 0.0)
                d = jnp.dot(w.astype(jnp.bfloat16), vv[ks, :], preferred_element_type=jnp.float32)
                total = d if total is None else total + d
        att_ref[at, :] += total
    @pl.loop(0, seq // TQ)
    def _(qi):
        q0 = qi * TQ
        at = pl.ds(pl.multiple_of(q0, TQ), TQ)
        att_ref[at, :] = jnp.zeros((TQ, 128), jnp.float32)
        first = start_of(q0 + lax.broadcasted_iota(jnp.int32, (TQ, 1), 0))
        diag = q0 // TK
        lo = start_of(q0) // TK
        mid = jnp.minimum((start_of(q0 + TQ - 1) + TK - 1) // TK, diag)
        mid = jnp.maximum(mid, lo)
        @pl.loop(lo, mid)
        def _(j):
            term(q0, TQ, j * TK, TK, first, False)
        @pl.loop(mid, diag)
        def _(j):
            term(q0, TQ, j * TK, TK, None, False)
        for s in range(TQ // DSUB):
            term(q0 + s * DSUB, TQ - s * DSUB, q0 + s * DSUB, DSUB, first[s * DSUB :], True)
        for s in range(TQ // 256):
            part = pl.ds(pl.multiple_of(q0 + s * 256, 256), 256)
            flip = att_ref[part, :].T
            stat_ref[0:1, part] = jnp.sum(flip, axis=0, keepdims=True)
            stat_ref[1:2, part] = jnp.sum(flip * flip, axis=0, keepdims=True)
def attend(info, targets, lengths, pieces):
    seq = sum(p.shape[0] for p in pieces)
    smem = pl.BlockSpec(memory_space=pltpu.SMEM)
    vmem = pl.BlockSpec(memory_space=pltpu.VMEM)
    return pl.pallas_call(
        attend_kernel,
        out_shape=(jax.ShapeDtypeStruct((seq, 128), jnp.float32), jax.ShapeDtypeStruct((seq, 128), jnp.bfloat16), jax.ShapeDtypeStruct((2, seq), jnp.float32)),
        in_specs=[smem] * 3 + [vmem] * len(pieces),
        out_specs=(vmem,) * 3,
        scratch_shapes=[pltpu.VMEM((seq, 128), jnp.bfloat16)] * 5,
        compiler_params=pltpu.CompilerParams(vmem_limit_bytes=56 * 1024 * 1024),
        cost_estimate=pl.CostEstimate(
            flops=2 * seq * seq * 128, bytes_accessed=seq * 128 * 14, transcendentals=seq * seq
        ),
    )(info, targets, lengths, *pieces)


def gate_kernel(info, att_ref, u_ref, *refs):
    stats, outs = refs[:4], refs[4:]
    rows = outs[0].shape[0]
    step = 256
    for k, out in enumerate(outs):
        block = lax.rem(info[0] + k, len(outs))

        @pl.loop(0, rows // step)
        def _(i):
            at = pl.ds(pl.multiple_of(block * rows + i * step, step), step)
            sums = stats[0][:, at]
            for other in stats[1:]:
                sums = sums + other[:, at]
            mean = sums[0:1] / D
            square = sums[1:2] / D
            scale = lax.rsqrt(square - mean * mean + eps_norm)
            mean = jnp.broadcast_to(mean, (128, step)).T
            scale = jnp.broadcast_to(scale, (128, step)).T
            gated = ((att_ref[at, :] - mean) * scale) * u_ref[at, :].astype(jnp.float32)
            out[pl.ds(pl.multiple_of(i * step, step), step), :] = gated.astype(jnp.bfloat16)


def gate(info, att, u, stats, count):
    rows = att.shape[0] // count
    vmem = pl.BlockSpec(memory_space=pltpu.VMEM)
    out = jax.ShapeDtypeStruct((rows, 128), jnp.bfloat16)
    return pl.pallas_call(
        gate_kernel,
        out_shape=(out,) * count,
        in_specs=[pl.BlockSpec(memory_space=pltpu.SMEM)] + [vmem] * (2 + len(stats)),
        out_specs=(vmem,) * count,
        compiler_params=pltpu.CompilerParams(vmem_limit_bytes=14 * 1024 * 1024),
        cost_estimate=pl.CostEstimate(flops=att.size * 8, bytes_accessed=att.size * 8, transcendentals=0),
    )(info, att, u, *stats)


def outgoing_kernel(info, targets, events_ref, after_ref, out_ref):
    count = out_ref.shape[0]
    blocks = events_ref.shape[0] // RB
    base = info[0] * blocks

    @pl.loop(0, blocks, unroll=4)
    def _(b):
        t = targets[base + b]
        frm = pl.ds(pl.multiple_of(b * RB, RB), RB)
        to = pl.ds(pl.multiple_of(lax.rem(t, blocks // count) * RB, RB), RB)
        out_ref[pl.ds(t // blocks, 1), to, :] = events_ref[frm, :][None]


def outgoing(info, targets, events, after, count):
    smem = pl.BlockSpec(memory_space=pltpu.SMEM)
    vmem = pl.BlockSpec(memory_space=pltpu.VMEM)
    return pl.pallas_call(
        outgoing_kernel,
        out_shape=jax.ShapeDtypeStruct((count, events.shape[0] // count, events.shape[1]), events.dtype),
        in_specs=[smem, smem, vmem, pl.BlockSpec(memory_space=pl.ANY)],
        out_specs=vmem,
        compiler_params=pltpu.CompilerParams(vmem_limit_bytes=8 * 1024 * 1024),
        cost_estimate=pl.CostEstimate(flops=0, bytes_accessed=events.size * 4, transcendentals=0),
    )(info, targets, events, after)


def finish_kernel(info, quarter, w_ref, *refs):
    residual, pieces, (out_ref, acc_ref) = refs[0], refs[1:-2], refs[-2:]
    count, part = residual.shape[0], residual.shape[1]
    step = acc_ref.shape[0] // 2
    for i in range(2):
        at = pl.ds(i * step, step)
        acc = None
        for n in range(0, len(pieces), 2):
            two = (n, n + 1)
            left = jnp.concatenate([pieces[m][at, :] for m in two], axis=1)
            right = jnp.concatenate(
                [w_ref[pl.ds(pl.multiple_of(info[m] * 128, 128), 128), :] for m in two], axis=0
            )
            term = jnp.dot(left, right, preferred_element_type=jnp.float32)
            acc = term if acc is None else acc + term
        acc_ref[at, :] = acc

    for i in range(count):
        at = pl.ds(pl.multiple_of(quarter[i] * part, part), part)
        out_ref[at, :] = (acc_ref[at, :] + residual[i].astype(jnp.float32)).astype(out_ref.dtype)


def finish(info, quarter, residual, w_out, pieces):
    smem = pl.BlockSpec(memory_space=pltpu.SMEM)
    vmem = pl.BlockSpec(memory_space=pltpu.VMEM)
    shape = (residual.shape[0] * residual.shape[1], residual.shape[2])
    return pl.pallas_call(
        finish_kernel,
        out_shape=jax.ShapeDtypeStruct(shape, jnp.bfloat16),
        in_specs=[smem] * 2 + [vmem] * (2 + len(pieces)),
        out_specs=vmem,
        scratch_shapes=[pltpu.VMEM(shape, jnp.float32)],
        compiler_params=pltpu.CompilerParams(vmem_limit_bytes=14 * 1024 * 1024),
        cost_estimate=pl.CostEstimate(
            flops=2 * shape[0] * shape[1] * D, bytes_accessed=8 * 1024 * 1024, transcendentals=0
        ),
    )(info, quarter, w_out, residual, *pieces)


def team_body(events, w_proj, w_out, block_target, user_lengths):
    half, zlo = lax.axis_index("half"), lax.axis_index("zlo")
    head, core = lax.axis_index("head"), lax.axis_index("core")
    z = half * 2 + zlo
    foreign = core ^ half
    outer = 1 - (zlo ^ half)
    rows = events.shape[0]
    blocks = rows // RB
    targets_here = block_target
    other_ints = move(jnp.concatenate([block_target, user_lengths]), other_core)
    targets = jnp.where(foreign == 0, block_target, other_ints[: block_target.shape[0]])
    lengths = jnp.where(foreign == 0, user_lengths, other_ints[block_target.shape[0] :])
    w_mine = lax.dynamic_slice_in_dim(w_proj, zlo * 256, 256, axis=2)

    parts = 2
    span = rows // parts
    partner = move(events, to_partner)
    x_own = move(events, across(lambda half, zlo, head, core: core == half))
    remote = []
    for i in range(parts):
        chunk = events[i * span : (i + 1) * span]
        if remote:
            chunk, _ = lax.optimization_barrier((chunk, remote[-1]))
        remote.append(move(chunk, to_other_team))
    x_partner = move(partner, across(lambda half, zlo, head, core: core != half))
    relayed = [move(r, inner_to_outer) for r in remote]

    def ints(*values):
        return jnp.stack([jnp.asarray(v, jnp.int32) for v in values])

    mine1, sib1 = project(
        ints(foreign, head, 1 - head, core), user_lengths, [events, x_own, partner, x_partner], w_mine, []
    )
    x_inner = [move(r, across(lambda half, zlo, head, core: (zlo ^ half) == 1)) for r in remote]
    x_outer = [move(r, across(lambda half, zlo, head, core: (zlo ^ half) == 0)) for r in relayed]
    mine, got = [mine1], [move(sib1, other_core)]
    send = outgoing(ints(z), targets_here, events, remote[-1], 4)
    residual = lax.all_to_all(send, ("half", "zlo"), split_axis=0, concat_axis=0, tiled=True)
    for i in range(parts):
        m, s = project(
            ints(outer, head, 1 - head, core),
            user_lengths,
            [remote[i], x_inner[i], relayed[i], x_outer[i]],
            w_mine,
            [send] if i == 0 else [],
        )
        mine.append(m)
        got.append(move(s, other_core))

    near = jnp.where(half == 0, 2, 1)
    far = jnp.where(half == 0, 3, 0)
    mine_second = jnp.where(foreign == 0, near, far)
    other_second = jnp.where(foreign == 0, far, near)
    part_blocks = span // RB
    starts = [jnp.where(foreign == 0, z, z ^ 1) * blocks]
    starts += [mine_second * blocks + i * part_blocks for i in range(parts)]
    starts += [jnp.where(foreign == 0, z ^ 1, z) * blocks]
    starts += [other_second * blocks + i * part_blocks for i in range(parts)]
    att, u, stat = attend(ints(*starts), targets, lengths, mine + got)

    by_shard = targets_here.reshape(4, blocks)
    quarter = jnp.max(
        jnp.where(by_shard // blocks == z, by_shard % blocks // (blocks // 4), 0), axis=1
    )

    stat = stat + move(stat, other_core)
    stats = [stat]
    for dz, dx in ((0, 1), (1, 0), (1, 1)):
        stats.append(
            move(stat, lambda half, zlo, head, core, dz=dz, dx=dx: (half, zlo ^ dz, head ^ dx, core))
        )
    me = zlo * 2 + core
    gated = gate(ints(me), att, u, stats, 4)

    def to_block(k):
        def rule(half, zlo, head, core):
            j = (zlo * 2 + core + k) % 4
            return (j // 2, j % 2, head, half)

        return rule

    pieces, feats = [], []
    for k in range(4):
        piece = move(gated[k], to_block(k))
        source = lax.rem(z - k + 4, 4)
        pieces += [piece, move(piece, across(lambda *p: True))]
        feats += [head * 4 + source, (1 - head) * 4 + source]
    return finish(ints(*feats), quarter, residual, w_out, pieces)


def solution(mesh):
    sizes = dict(mesh.shape)
    if sizes["seq"] == 4 and sizes["head"] == 2 and sizes["dp"] % 2 == 0:
        rows = P(("y", "core", "half", "zlo"), "head")
        part = P(("y", "core"))
        return jax.shard_map(
            team_body,
            mesh=team_plan(mesh),
            in_specs=(rows, P(None, None, "head"), P(None, "head"), part, part),
            out_specs=rows,
            check_vma=False,
        )
    placed = (P(("dp", "seq"), "head"), P(None, None, "head"), P(None, "head"), P("dp"), P("dp"))
    return jax.shard_map(
        body, mesh=mesh, in_specs=placed, out_specs=P(("dp", "seq"), "head"), check_vma=False
    )
```

```python
import functools

import jax
import jax.numpy as jnp
from jax import lax
from jax.experimental import pallas as pl
from jax.experimental.pallas import tpu as pltpu
from jax.sharding import PartitionSpec as P

D = 1024
DH = 64
RB = 16


eps_norm = 1e-05


def from_behind(block, axis, distance):
    devices = range(lax.axis_size(axis))
    route = [((i - distance) % len(devices), i) for i in devices]
    return lax.ppermute(block, axis, route)


def user_index(positions, user_ends):
    return jnp.sum((positions[:, None] >= user_ends[None, :]).astype(jnp.int32), axis=1)


def body(events, w_proj, w_out, block_target, user_lengths):
    rows_here = events.shape[0]
    col_width = events.shape[1]
    seq_count = lax.axis_size("seq")
    seq_index = lax.axis_index("seq")
    block_count = rows_here // RB
    per_owner = block_count // seq_count

    def window_position(shard, local):
        return shard * rows_here + local

    owners = block_target // block_count
    slots = block_target % block_count
    my_owners = lax.dynamic_slice_in_dim(owners, seq_index * block_count, block_count)
    send_order = jnp.argsort(my_owners, stable=True)
    outgoing = events.reshape(block_count, RB, col_width)[send_order]
    outgoing = outgoing.reshape(seq_count, per_owner, RB, col_width)
    incoming = lax.all_to_all(outgoing, "seq", split_axis=0, concat_axis=0, tiled=True)
    arrived = jnp.argsort(jnp.where(owners == seq_index, 0, 1), stable=True)[:block_count]
    slot_ids = slots[arrived]
    placed = incoming.reshape(block_count, RB, col_width)[jnp.argsort(slot_ids)]
    ordered = placed.reshape(rows_here, col_width)
    widened = ordered.astype(jnp.float32)
    row_sum, row_squares = lax.psum(
        (jnp.sum(widened, axis=1), jnp.sum(widened * widened, axis=1)), "head"
    )
    mean_value = row_sum / D
    square_mean = row_squares / D
    normed = (
        (widened - mean_value[:, None])
        * lax.rsqrt(square_mean - mean_value * mean_value + eps_norm)[:, None]
    ).astype(jnp.bfloat16)
    weight_rows = w_proj
    projected = jnp.einsum(
        "ln,jnc->jlc",
        lax.all_gather(normed, "head", axis=1, tiled=True),
        weight_rows,
        preferred_element_type=jnp.float32,
    )
    activated = jax.nn.silu(projected).astype(jnp.bfloat16)
    gate_rows = activated[0]
    value_rows = activated[1]
    query_rows = activated[2]
    key_rows = activated[3]
    user_ends = jnp.cumsum(user_lengths)
    head_count = col_width // DH
    query_heads = query_rows.reshape(rows_here, head_count, DH)
    local_rows = jnp.arange(rows_here, dtype=jnp.int32)
    query_pos = window_position(seq_index, local_rows)
    query_users = user_index(query_pos, user_ends)
    zero_sum = jnp.zeros((rows_here, col_width), jnp.float32)

    def key_term(key_piece, value_piece, key_pos):
        row_count = key_piece.shape[0]
        key_heads = key_piece.reshape(row_count, head_count, DH)
        value_heads = value_piece.reshape(row_count, head_count, DH)
        key_users = user_index(key_pos, user_ends)
        allowed = (key_pos[None, :] <= query_pos[:, None]) & (
            key_users[None, :] == query_users[:, None]
        )
        scores = jnp.einsum(
            "lhd,nhd->hln", query_heads, key_heads, preferred_element_type=jnp.float32
        )
        weights = jnp.where(allowed[None], jax.nn.silu(scores), 0.0).astype(jnp.bfloat16)
        summed = jnp.einsum(
            "hln,nhd->lhd", weights, value_heads, preferred_element_type=jnp.float32
        )
        return summed.reshape(rows_here, col_width)

    def guarded_term(key_piece, value_piece, key_pos):
        return key_term(key_piece, value_piece, key_pos)

    def sweep_piece(running, key_piece, value_piece, key_pos):
        row_count = key_piece.shape[0]
        block_rows = min(row_count, 1024)
        rounds = row_count // block_rows

        def visit_block(partial_sum, inputs):
            key_block, value_block, block_pos = inputs
            return (partial_sum + guarded_term(key_block, value_block, block_pos), None)

        key_stack = key_piece.reshape(rounds, block_rows, col_width)
        value_stack = value_piece.reshape(rounds, block_rows, col_width)
        pos_stack = key_pos.reshape(rounds, block_rows)
        running, _ = lax.scan(visit_block, running, (key_stack, value_stack, pos_stack))
        return running

    stacked = jnp.stack([key_rows, value_rows])
    own_block = sweep_piece(zero_sum, key_rows, value_rows, query_pos)

    def relay_step(offset, loop_state):
        running, carried = loop_state
        carried = from_behind(carried, "seq", 1)
        source_shard = (seq_index - offset + seq_count) % seq_count
        running = sweep_piece(
            running, carried[0], carried[1], window_position(source_shard, local_rows)
        )
        return (running, carried)

    attended, _ = lax.fori_loop(1, seq_count, relay_step, (own_block, stacked))
    att_sum, att_squares = lax.psum(
        (jnp.sum(attended, axis=1), jnp.sum(attended * attended, axis=1)), "head"
    )
    att_mean = att_sum / D
    att_square_mean = att_squares / D
    scaled = (attended - att_mean[:, None]) * lax.rsqrt(
        att_square_mean - att_mean * att_mean + eps_norm
    )[:, None]
    gated_rows = (scaled * gate_rows.astype(jnp.float32)).astype(jnp.bfloat16)
    weight_rows = w_out
    projected_out = jnp.dot(
        lax.all_gather(gated_rows, "head", axis=1, tiled=True),
        weight_rows,
        preferred_element_type=jnp.float32,
    )
    finished = (widened + projected_out).astype(jnp.bfloat16)
    return finished


def team_plan(mesh):
    return jax.sharding.Mesh(
        mesh.devices.reshape(2, 2, 2, mesh.devices.shape[2] // 2, 2),
        ("half", "zlo", "head", "y", "core"),
    )


ROUTE = ("half", "zlo", "head", "core")


def route(rule):
    pairs = []
    for half in range(2):
        for zlo in range(2):
            for head in range(2):
                for core in range(2):
                    to = rule(half, zlo, head, core)
                    if to is not None:
                        pairs.append(
                            (
                                ((half * 2 + zlo) * 2 + head) * 2 + core,
                                ((to[0] * 2 + to[1]) * 2 + to[2]) * 2 + to[3],
                            )
                        )
    return pairs


def move(value, rule):
    return lax.ppermute(value, ROUTE, route(rule))


def to_partner(half, zlo, head, core):
    if core == half:
        return (half, 1 - zlo, head, 1 - half)
    return None


def to_other_team(half, zlo, head, core):
    if core == half:
        return None
    other = 1 - half
    inner = (zlo ^ half) == 1
    return (other, 1 - other, head, other if inner else 1 - other)


def inner_to_outer(half, zlo, head, core):
    if (zlo ^ half) == 1:
        return (half, 1 - zlo, head, core)
    return None


def across(select):
    def rule(half, zlo, head, core):
        if select(half, zlo, head, core):
            return (half, zlo, 1 - head, core)
        return None

    return rule


def other_core(half, zlo, head, core):
    return (half, zlo, head, 1 - core)


def project_kernel(waited, info, lengths, *refs):
    pairs = refs[: -6 - waited]
    w_ref, mine_ref, sib_ref, own_v, other_v, sems = refs[-6:]
    pairs = [(pairs[i], pairs[i + 1]) for i in range(0, len(pairs), 2)]
    rows, width = own_v.shape
    step = rows // 2

    def copies(pair, i):
        at = pl.ds(i * step, step)
        return (
            pltpu.make_async_copy(pair[0].at[at, :], own_v.at[at, :], sems.at[2 * i]),
            pltpu.make_async_copy(pair[1].at[at, :], other_v.at[at, :], sems.at[2 * i + 1]),
        )

    for n, pair in enumerate(pairs):

        @pl.when(info[0] == n)
        def _():
            for i in range(2):
                for copy in copies(pair, i):
                    copy.start()

    own_rows = pl.multiple_of(info[1] * width, width)
    other_rows = pl.multiple_of(info[2] * width, width)
    low_core = info[3] == 0
    for i in range(2):
        for copy in copies(pairs[0], i):
            copy.wait()
        at = pl.ds(i * step, step)
        a = own_v[at, :].astype(jnp.float32)
        b = other_v[at, :].astype(jnp.float32)
        mean = (jnp.sum(a, axis=1, keepdims=True) + jnp.sum(b, axis=1, keepdims=True)) / (2 * width)
        square = (
            jnp.sum(a * a, axis=1, keepdims=True) + jnp.sum(b * b, axis=1, keepdims=True)
        ) / (2 * width)
        scale = lax.rsqrt(square - mean * mean + eps_norm)
        a = ((a - mean) * scale).astype(jnp.bfloat16)
        b = ((b - mean) * scale).astype(jnp.bfloat16)
        for j in range(4):
            z = jnp.dot(
                a, w_ref[j, pl.ds(own_rows, width), :], preferred_element_type=jnp.float32
            ) + jnp.dot(
                b, w_ref[j, pl.ds(other_rows, width), :], preferred_element_type=jnp.float32
            )
            t = 0.5 * z
            act = (t + t * jnp.tanh(t)).astype(jnp.bfloat16)
            if j == 2:
                act = act * 0.5
            low, high = act[:, :128], act[:, 128:]
            cols = pl.ds(j * 128, 128)
            mine_ref[at, cols] = jnp.where(low_core, low, high)
            sib_ref[at, cols] = jnp.where(low_core, high, low)


def project(info, lengths, pairs, w, after):
    rows, width = pairs[0].shape
    anywhere = pl.BlockSpec(memory_space=pl.ANY)
    vmem = pl.BlockSpec(memory_space=pltpu.VMEM)
    out = jax.ShapeDtypeStruct((rows, 512), jnp.bfloat16)
    return pl.pallas_call(
        functools.partial(project_kernel, len(after)),
        out_shape=(out, out),
        in_specs=[pl.BlockSpec(memory_space=pltpu.SMEM)] * 2 + [anywhere] * (len(pairs) + len(after)) + [vmem],
        out_specs=(vmem, vmem),
        scratch_shapes=[
            pltpu.VMEM((rows, width), jnp.bfloat16),
            pltpu.VMEM((rows, width), jnp.bfloat16),
            pltpu.SemaphoreType.DMA((4,)),
        ],
        compiler_params=pltpu.CompilerParams(vmem_limit_bytes=16 * 1024 * 1024),
        cost_estimate=pl.CostEstimate(
            flops=2 * rows * D * 1024, bytes_accessed=rows * D * 4 + w.size * 2, transcendentals=rows * 1024
        ),
    )(info, lengths, *pairs, *after, w)


TQ = 1536
TK = 512
SUB = 256
DSUB = 256


def attend_kernel(info, here_targets, here_lengths, there, *refs):
    pieces, (att_ref, u_ref, stat_ref, held) = refs[:-4], refs[-4:]
    own = info[len(pieces)] == 0
    blocks = here_targets.shape[0]
    seq = att_ref.shape[0]
    low = lax.broadcasted_iota(jnp.int32, (SUB, 128), 1) < DH
    zero = jnp.zeros((SUB, 128), jnp.bfloat16)
    for n, piece in enumerate(pieces):
        base = info[n]

        @pl.loop(0, piece.shape[0] // RB, unroll=8)
        def _(b):
            frm = pl.ds(pl.multiple_of(b * RB, RB), RB)
            to = pl.ds(
                pl.multiple_of(jnp.where(own, here_targets[base + b], there[base + b]) * RB, RB), RB
            )
            u_ref[to, :] = piece[frm, 0:128]
            held[to, :] = piece[frm, 128:512]

    ends = []
    total = jnp.int32(0)
    for i in range(here_lengths.shape[0]):
        total = total + jnp.where(own, here_lengths[i], there[blocks + i])
        ends.append(total)
    def start_of(p):
        best = p * 0
        for e in ends:
            best = jnp.where(p >= e, e, best)
        return best
    def term(q0, rows, k0_at, keys, first, causal):
        at = pl.ds(pl.multiple_of(q0, 256), rows)
        q = held[at, 128:256]
        total = None
        for s in range(keys // SUB):
            ks = pl.ds(pl.multiple_of(k0_at + s * SUB, SUB), SUB)
            if first is not None:
                kp = k0_at + s * SUB + lax.broadcasted_iota(jnp.int32, (1, SUB), 1)
                ok = kp >= first
                if causal:
                    ok = ok & (kp <= q0 + lax.broadcasted_iota(jnp.int32, (rows, 1), 0))
            v, k = held[ks, 0:128], held[ks, 256:384]
            for upper in (False, True):
                kk, vv = (jnp.where(low, zero, m) if upper else jnp.where(low, m, zero) for m in (k, v))
                t = lax.dot_general(q, kk, (((1,), (1,)), ((), ())), preferred_element_type=jnp.float32)
                w = t + t * jnp.tanh(t)
                if first is not None:
                    w = jnp.where(ok, w, 0.0)
                d = jnp.dot(w.astype(jnp.bfloat16), vv, preferred_element_type=jnp.float32)
                total = d if total is None else total + d
        att_ref[at, :] += total
    @pl.loop(0, seq // TQ)
    def _(qi):
        q0 = qi * TQ
        at = pl.ds(pl.multiple_of(q0, TQ), TQ)
        att_ref[at, :] = jnp.zeros((TQ, 128), jnp.float32)
        first = start_of(q0 + lax.broadcasted_iota(jnp.int32, (TQ, 1), 0))
        diag = q0 // TK
        lo = start_of(q0) // TK
        mid = jnp.minimum((start_of(q0 + TQ - 1) + TK - 1) // TK, diag)
        mid = jnp.maximum(mid, lo)
        @pl.loop(lo, mid)
        def _(j):
            term(q0, TQ, j * TK, TK, first, False)
        @pl.loop(mid, diag)
        def _(j):
            term(q0, TQ, j * TK, TK, None, False)
        for s in range(TQ // DSUB):
            term(q0 + s * DSUB, TQ - s * DSUB, q0 + s * DSUB, DSUB, first[s * DSUB :], True)
        for s in range(TQ // 256):
            part = pl.ds(pl.multiple_of(q0 + s * 256, 256), 256)
            flip = att_ref[part, :].T
            stat_ref[0:1, part] = jnp.sum(flip, axis=0, keepdims=True)
            stat_ref[1:2, part] = jnp.sum(flip * flip, axis=0, keepdims=True)
def attend(info, targets, lengths, there, pieces):
    seq = sum(p.shape[0] for p in pieces)
    smem = pl.BlockSpec(memory_space=pltpu.SMEM)
    vmem = pl.BlockSpec(memory_space=pltpu.VMEM)
    return pl.pallas_call(
        attend_kernel,
        out_shape=(jax.ShapeDtypeStruct((seq, 128), jnp.float32), jax.ShapeDtypeStruct((seq, 128), jnp.bfloat16), jax.ShapeDtypeStruct((2, seq), jnp.float32)),
        in_specs=[smem] * 4 + [vmem] * len(pieces),
        out_specs=(vmem,) * 3,
        scratch_shapes=[pltpu.VMEM((seq, 384), jnp.bfloat16)],
        compiler_params=pltpu.CompilerParams(vmem_limit_bytes=56 * 1024 * 1024),
        cost_estimate=pl.CostEstimate(
            flops=2 * seq * seq * 128, bytes_accessed=seq * 128 * 14, transcendentals=seq * seq
        ),
    )(info, targets, lengths, there, *pieces)


def gate_kernel(info, att_ref, u_ref, *refs):
    stats, outs = refs[:4], refs[4:]
    rows = outs[0].shape[0]
    step = 256
    for k, out in enumerate(outs):
        block = lax.rem(info[0] + k, len(outs))

        @pl.loop(0, rows // step)
        def _(i):
            at = pl.ds(pl.multiple_of(block * rows + i * step, step), step)
            sums = stats[0][:, at]
            for other in stats[1:]:
                sums = sums + other[:, at]
            mean = sums[0:1] / D
            square = sums[1:2] / D
            scale = lax.rsqrt(square - mean * mean + eps_norm)
            mean = jnp.broadcast_to(mean, (128, step)).T
            scale = jnp.broadcast_to(scale, (128, step)).T
            gated = ((att_ref[at, :] - mean) * scale) * u_ref[at, :].astype(jnp.float32)
            out[pl.ds(pl.multiple_of(i * step, step), step), :] = gated.astype(jnp.bfloat16)


def gate(info, att, u, stats, count):
    rows = att.shape[0] // count
    vmem = pl.BlockSpec(memory_space=pltpu.VMEM)
    out = jax.ShapeDtypeStruct((rows, 128), jnp.bfloat16)
    return pl.pallas_call(
        gate_kernel,
        out_shape=(out,) * count,
        in_specs=[pl.BlockSpec(memory_space=pltpu.SMEM)] + [vmem] * (2 + len(stats)),
        out_specs=(vmem,) * count,
        compiler_params=pltpu.CompilerParams(vmem_limit_bytes=14 * 1024 * 1024),
        cost_estimate=pl.CostEstimate(flops=att.size * 8, bytes_accessed=att.size * 8, transcendentals=0),
    )(info, att, u, *stats)


def outgoing_kernel(info, targets, events_ref, after_ref, out_ref):
    count = out_ref.shape[0]
    blocks = events_ref.shape[0] // RB
    base = info[0] * blocks

    @pl.loop(0, blocks, unroll=4)
    def _(b):
        t = targets[base + b]
        frm = pl.ds(pl.multiple_of(b * RB, RB), RB)
        to = pl.ds(pl.multiple_of(lax.rem(t, blocks // count) * RB, RB), RB)
        out_ref[pl.ds(t // blocks, 1), to, :] = events_ref[frm, :][None]


def outgoing(info, targets, events, after, count):
    smem = pl.BlockSpec(memory_space=pltpu.SMEM)
    vmem = pl.BlockSpec(memory_space=pltpu.VMEM)
    return pl.pallas_call(
        outgoing_kernel,
        out_shape=jax.ShapeDtypeStruct((count, events.shape[0] // count, events.shape[1]), events.dtype),
        in_specs=[smem, smem, vmem, pl.BlockSpec(memory_space=pl.ANY)],
        out_specs=vmem,
        compiler_params=pltpu.CompilerParams(vmem_limit_bytes=8 * 1024 * 1024),
        cost_estimate=pl.CostEstimate(flops=0, bytes_accessed=events.size * 4, transcendentals=0),
    )(info, targets, events, after)


def finish_kernel(info, quarter, w_ref, *refs):
    residual, pieces, (out_ref, acc_ref) = refs[0], refs[1:-2], refs[-2:]
    count, part = residual.shape[0], residual.shape[1]
    step = acc_ref.shape[0] // 2
    for i in range(2):
        at = pl.ds(i * step, step)
        acc = None
        for n in range(0, len(pieces), 2):
            two = (n, n + 1)
            left = jnp.concatenate([pieces[m][at, :] for m in two], axis=1)
            right = jnp.concatenate(
                [w_ref[pl.ds(pl.multiple_of(info[m] * 128, 128), 128), :] for m in two], axis=0
            )
            term = jnp.dot(left, right, preferred_element_type=jnp.float32)
            acc = term if acc is None else acc + term
        acc_ref[at, :] = acc

    for i in range(count):
        at = pl.ds(pl.multiple_of(quarter[i] * part, part), part)
        out_ref[at, :] = (acc_ref[at, :] + residual[i].astype(jnp.float32)).astype(out_ref.dtype)


def finish(info, quarter, residual, w_out, pieces):
    smem = pl.BlockSpec(memory_space=pltpu.SMEM)
    vmem = pl.BlockSpec(memory_space=pltpu.VMEM)
    shape = (residual.shape[0] * residual.shape[1], residual.shape[2])
    return pl.pallas_call(
        finish_kernel,
        out_shape=jax.ShapeDtypeStruct(shape, jnp.bfloat16),
        in_specs=[smem] * 2 + [vmem] * (2 + len(pieces)),
        out_specs=vmem,
        scratch_shapes=[pltpu.VMEM(shape, jnp.float32)],
        compiler_params=pltpu.CompilerParams(vmem_limit_bytes=14 * 1024 * 1024),
        cost_estimate=pl.CostEstimate(
            flops=2 * shape[0] * shape[1] * D, bytes_accessed=8 * 1024 * 1024, transcendentals=0
        ),
    )(info, quarter, w_out, residual, *pieces)


def team_body(events, w_proj, w_out, block_target, user_lengths):
    half, zlo = lax.axis_index("half"), lax.axis_index("zlo")
    head, core = lax.axis_index("head"), lax.axis_index("core")
    z = half * 2 + zlo
    foreign = core ^ half
    outer = 1 - (zlo ^ half)
    rows = events.shape[0]
    blocks = rows // RB
    targets_here = block_target
    other_ints = move(jnp.concatenate([block_target, user_lengths]), other_core)
    w_mine = lax.dynamic_slice_in_dim(w_proj, zlo * 256, 256, axis=2)

    parts = 2
    span = rows // parts
    partner = move(events, to_partner)
    x_own = move(events, across(lambda half, zlo, head, core: core == half))
    remote = []
    for i in range(parts):
        chunk = events[i * span : (i + 1) * span]
        if remote:
            chunk, _ = lax.optimization_barrier((chunk, remote[-1]))
        remote.append(move(chunk, to_other_team))
    x_partner = move(partner, across(lambda half, zlo, head, core: core != half))
    relayed = [move(r, inner_to_outer) for r in remote]

    def ints(*values):
        return jnp.stack([jnp.asarray(v, jnp.int32) for v in values])

    mine1, sib1 = project(
        ints(foreign, head, 1 - head, core), user_lengths, [events, x_own, partner, x_partner], w_mine, []
    )
    x_inner = [move(r, across(lambda half, zlo, head, core: (zlo ^ half) == 1)) for r in remote]
    x_outer = [move(r, across(lambda half, zlo, head, core: (zlo ^ half) == 0)) for r in relayed]
    mine, got = [mine1], [move(sib1, other_core)]
    send = outgoing(ints(z), targets_here, events, remote[-1], 4)
    residual = lax.all_to_all(send, ("half", "zlo"), split_axis=0, concat_axis=0, tiled=True)
    for i in range(parts):
        m, s = project(
            ints(outer, head, 1 - head, core),
            user_lengths,
            [remote[i], x_inner[i], relayed[i], x_outer[i]],
            w_mine,
            [send] if i == 0 else [],
        )
        mine.append(m)
        got.append(move(s, other_core))

    near = jnp.where(half == 0, 2, 1)
    far = jnp.where(half == 0, 3, 0)
    mine_second = jnp.where(foreign == 0, near, far)
    other_second = jnp.where(foreign == 0, far, near)
    part_blocks = span // RB
    starts = [jnp.where(foreign == 0, z, z ^ 1) * blocks]
    starts += [mine_second * blocks + i * part_blocks for i in range(parts)]
    starts += [jnp.where(foreign == 0, z ^ 1, z) * blocks]
    starts += [other_second * blocks + i * part_blocks for i in range(parts)]
    att, u, stat = attend(ints(*starts, foreign), block_target, user_lengths, other_ints, mine + got)

    by_shard = targets_here.reshape(4, blocks)
    quarter = jnp.max(
        jnp.where(by_shard // blocks == z, by_shard % blocks // (blocks // 4), 0), axis=1
    )

    stat = stat + move(stat, other_core)
    stats = [stat]
    for dz, dx in ((0, 1), (1, 0), (1, 1)):
        stats.append(
            move(stat, lambda half, zlo, head, core, dz=dz, dx=dx: (half, zlo ^ dz, head ^ dx, core))
        )
    me = zlo * 2 + core
    gated = gate(ints(me), att, u, stats, 4)

    def to_block(k):
        def rule(half, zlo, head, core):
            j = (zlo * 2 + core + k) % 4
            return (j // 2, j % 2, head, half)

        return rule

    pieces, feats = [], []
    for k in range(4):
        piece = move(gated[k], to_block(k))
        source = lax.rem(z - k + 4, 4)
        pieces += [piece, move(piece, across(lambda *p: True))]
        feats += [head * 4 + source, (1 - head) * 4 + source]
    return finish(ints(*feats), quarter, residual, w_out, pieces)


def solution(mesh):
    sizes = dict(mesh.shape)
    if sizes["seq"] == 4 and sizes["head"] == 2 and sizes["dp"] % 2 == 0:
        rows = P(("y", "core", "half", "zlo"), "head")
        part = P(("y", "core"))
        return jax.shard_map(
            team_body,
            mesh=team_plan(mesh),
            in_specs=(rows, P(None, None, "head"), P(None, "head"), part, part),
            out_specs=rows,
            check_vma=False,
        )
    placed = (P(("dp", "seq"), "head"), P(None, None, "head"), P(None, "head"), P("dp"), P("dp"))
    return jax.shard_map(
        body, mesh=mesh, in_specs=placed, out_specs=P(("dp", "seq"), "head"), check_vma=False
    )
```

```python
import functools

import jax
import jax.numpy as jnp
from jax import lax
from jax.experimental import pallas as pl
from jax.experimental.pallas import tpu as pltpu
from jax.sharding import PartitionSpec as P

D = 1024
DH = 64
RB = 16


eps_norm = 1e-05


def from_behind(block, axis, distance):
    devices = range(lax.axis_size(axis))
    route = [((i - distance) % len(devices), i) for i in devices]
    return lax.ppermute(block, axis, route)


def user_index(positions, user_ends):
    return jnp.sum((positions[:, None] >= user_ends[None, :]).astype(jnp.int32), axis=1)


def body(events, w_proj, w_out, block_target, user_lengths):
    rows_here = events.shape[0]
    col_width = events.shape[1]
    seq_count = lax.axis_size("seq")
    seq_index = lax.axis_index("seq")
    block_count = rows_here // RB
    per_owner = block_count // seq_count

    def window_position(shard, local):
        return shard * rows_here + local

    owners = block_target // block_count
    slots = block_target % block_count
    my_owners = lax.dynamic_slice_in_dim(owners, seq_index * block_count, block_count)
    send_order = jnp.argsort(my_owners, stable=True)
    outgoing = events.reshape(block_count, RB, col_width)[send_order]
    outgoing = outgoing.reshape(seq_count, per_owner, RB, col_width)
    incoming = lax.all_to_all(outgoing, "seq", split_axis=0, concat_axis=0, tiled=True)
    arrived = jnp.argsort(jnp.where(owners == seq_index, 0, 1), stable=True)[:block_count]
    slot_ids = slots[arrived]
    placed = incoming.reshape(block_count, RB, col_width)[jnp.argsort(slot_ids)]
    ordered = placed.reshape(rows_here, col_width)
    widened = ordered.astype(jnp.float32)
    row_sum, row_squares = lax.psum(
        (jnp.sum(widened, axis=1), jnp.sum(widened * widened, axis=1)), "head"
    )
    mean_value = row_sum / D
    square_mean = row_squares / D
    normed = (
        (widened - mean_value[:, None])
        * lax.rsqrt(square_mean - mean_value * mean_value + eps_norm)[:, None]
    ).astype(jnp.bfloat16)
    weight_rows = w_proj
    projected = jnp.einsum(
        "ln,jnc->jlc",
        lax.all_gather(normed, "head", axis=1, tiled=True),
        weight_rows,
        preferred_element_type=jnp.float32,
    )
    activated = jax.nn.silu(projected).astype(jnp.bfloat16)
    gate_rows = activated[0]
    value_rows = activated[1]
    query_rows = activated[2]
    key_rows = activated[3]
    user_ends = jnp.cumsum(user_lengths)
    head_count = col_width // DH
    query_heads = query_rows.reshape(rows_here, head_count, DH)
    local_rows = jnp.arange(rows_here, dtype=jnp.int32)
    query_pos = window_position(seq_index, local_rows)
    query_users = user_index(query_pos, user_ends)
    zero_sum = jnp.zeros((rows_here, col_width), jnp.float32)

    def key_term(key_piece, value_piece, key_pos):
        row_count = key_piece.shape[0]
        key_heads = key_piece.reshape(row_count, head_count, DH)
        value_heads = value_piece.reshape(row_count, head_count, DH)
        key_users = user_index(key_pos, user_ends)
        allowed = (key_pos[None, :] <= query_pos[:, None]) & (
            key_users[None, :] == query_users[:, None]
        )
        scores = jnp.einsum(
            "lhd,nhd->hln", query_heads, key_heads, preferred_element_type=jnp.float32
        )
        weights = jnp.where(allowed[None], jax.nn.silu(scores), 0.0).astype(jnp.bfloat16)
        summed = jnp.einsum(
            "hln,nhd->lhd", weights, value_heads, preferred_element_type=jnp.float32
        )
        return summed.reshape(rows_here, col_width)

    def guarded_term(key_piece, value_piece, key_pos):
        return key_term(key_piece, value_piece, key_pos)

    def sweep_piece(running, key_piece, value_piece, key_pos):
        row_count = key_piece.shape[0]
        block_rows = min(row_count, 1024)
        rounds = row_count // block_rows

        def visit_block(partial_sum, inputs):
            key_block, value_block, block_pos = inputs
            return (partial_sum + guarded_term(key_block, value_block, block_pos), None)

        key_stack = key_piece.reshape(rounds, block_rows, col_width)
        value_stack = value_piece.reshape(rounds, block_rows, col_width)
        pos_stack = key_pos.reshape(rounds, block_rows)
        running, _ = lax.scan(visit_block, running, (key_stack, value_stack, pos_stack))
        return running

    stacked = jnp.stack([key_rows, value_rows])
    own_block = sweep_piece(zero_sum, key_rows, value_rows, query_pos)

    def relay_step(offset, loop_state):
        running, carried = loop_state
        carried = from_behind(carried, "seq", 1)
        source_shard = (seq_index - offset + seq_count) % seq_count
        running = sweep_piece(
            running, carried[0], carried[1], window_position(source_shard, local_rows)
        )
        return (running, carried)

    attended, _ = lax.fori_loop(1, seq_count, relay_step, (own_block, stacked))
    att_sum, att_squares = lax.psum(
        (jnp.sum(attended, axis=1), jnp.sum(attended * attended, axis=1)), "head"
    )
    att_mean = att_sum / D
    att_square_mean = att_squares / D
    scaled = (attended - att_mean[:, None]) * lax.rsqrt(
        att_square_mean - att_mean * att_mean + eps_norm
    )[:, None]
    gated_rows = (scaled * gate_rows.astype(jnp.float32)).astype(jnp.bfloat16)
    weight_rows = w_out
    projected_out = jnp.dot(
        lax.all_gather(gated_rows, "head", axis=1, tiled=True),
        weight_rows,
        preferred_element_type=jnp.float32,
    )
    finished = (widened + projected_out).astype(jnp.bfloat16)
    return finished


def team_plan(mesh):
    return jax.sharding.Mesh(
        mesh.devices.reshape(2, 2, 2, mesh.devices.shape[2] // 2, 2),
        ("half", "zlo", "head", "y", "core"),
    )


ROUTE = ("half", "zlo", "head", "core")


def route(rule):
    pairs = []
    for half in range(2):
        for zlo in range(2):
            for head in range(2):
                for core in range(2):
                    to = rule(half, zlo, head, core)
                    if to is not None:
                        pairs.append(
                            (
                                ((half * 2 + zlo) * 2 + head) * 2 + core,
                                ((to[0] * 2 + to[1]) * 2 + to[2]) * 2 + to[3],
                            )
                        )
    return pairs


def move(value, rule):
    return lax.ppermute(value, ROUTE, route(rule))


def to_partner(half, zlo, head, core):
    if core == half:
        return (half, 1 - zlo, head, 1 - half)
    return None


def to_other_team(half, zlo, head, core):
    if core == half:
        return None
    other = 1 - half
    inner = (zlo ^ half) == 1
    return (other, 1 - other, head, other if inner else 1 - other)


def inner_to_outer(half, zlo, head, core):
    if (zlo ^ half) == 1:
        return (half, 1 - zlo, head, core)
    return None


def across(select):
    def rule(half, zlo, head, core):
        if select(half, zlo, head, core):
            return (half, zlo, 1 - head, core)
        return None

    return rule


def other_core(half, zlo, head, core):
    return (half, zlo, head, 1 - core)


def project_kernel(waited, info, lengths, *refs):
    pairs = refs[: -6 - waited]
    w_ref, mine_ref, sib_ref, own_v, other_v, sems = refs[-6:]
    pairs = [(pairs[i], pairs[i + 1]) for i in range(0, len(pairs), 2)]
    rows, width = own_v.shape
    step = rows // 2

    def copies(pair, i):
        at = pl.ds(i * step, step)
        return (
            pltpu.make_async_copy(pair[0].at[at, :], own_v.at[at, :], sems.at[2 * i]),
            pltpu.make_async_copy(pair[1].at[at, :], other_v.at[at, :], sems.at[2 * i + 1]),
        )

    for n, pair in enumerate(pairs):

        @pl.when(info[0] == n)
        def _():
            for i in range(2):
                for copy in copies(pair, i):
                    copy.start()

    own_rows = pl.multiple_of(info[1] * width, width)
    other_rows = pl.multiple_of(info[2] * width, width)
    low_core = info[3] == 0
    for i in range(2):
        for copy in copies(pairs[0], i):
            copy.wait()
        at = pl.ds(i * step, step)
        a = own_v[at, :].astype(jnp.float32)
        b = other_v[at, :].astype(jnp.float32)
        mean = (jnp.sum(a, axis=1, keepdims=True) + jnp.sum(b, axis=1, keepdims=True)) / (2 * width)
        square = (
            jnp.sum(a * a, axis=1, keepdims=True) + jnp.sum(b * b, axis=1, keepdims=True)
        ) / (2 * width)
        scale = lax.rsqrt(square - mean * mean + eps_norm)
        a = ((a - mean) * scale).astype(jnp.bfloat16)
        b = ((b - mean) * scale).astype(jnp.bfloat16)
        for j in range(4):
            z = jnp.dot(
                a, w_ref[j, pl.ds(own_rows, width), :], preferred_element_type=jnp.float32
            ) + jnp.dot(
                b, w_ref[j, pl.ds(other_rows, width), :], preferred_element_type=jnp.float32
            )
            t = 0.5 * z
            act = (t + t * jnp.tanh(t)).astype(jnp.bfloat16)
            if j == 2:
                act = act * 0.5
            low, high = act[:, :128], act[:, 128:]
            cols = pl.ds(j * 128, 128)
            mine_ref[at, cols] = jnp.where(low_core, low, high)
            sib_ref[at, cols] = jnp.where(low_core, high, low)


def project(info, lengths, pairs, w, after):
    rows, width = pairs[0].shape
    anywhere = pl.BlockSpec(memory_space=pl.ANY)
    vmem = pl.BlockSpec(memory_space=pltpu.VMEM)
    out = jax.ShapeDtypeStruct((rows, 512), jnp.bfloat16)
    return pl.pallas_call(
        functools.partial(project_kernel, len(after)),
        out_shape=(out, out),
        in_specs=[pl.BlockSpec(memory_space=pltpu.SMEM)] * 2 + [anywhere] * (len(pairs) + len(after)) + [vmem],
        out_specs=(vmem, vmem),
        scratch_shapes=[
            pltpu.VMEM((rows, width), jnp.bfloat16),
            pltpu.VMEM((rows, width), jnp.bfloat16),
            pltpu.SemaphoreType.DMA((4,)),
        ],
        compiler_params=pltpu.CompilerParams(vmem_limit_bytes=16 * 1024 * 1024),
        cost_estimate=pl.CostEstimate(
            flops=2 * rows * D * 1024, bytes_accessed=rows * D * 4 + w.size * 2, transcendentals=rows * 1024
        ),
    )(info, lengths, *pairs, *after, w)


TQ = 1536
TK = 512
SUB = 256
DSUB = 256


def attend_kernel(info, here_targets, here_lengths, there, *refs):
    pieces, (out_ref, u_ref, stat_ref, held, att_ref) = refs[:-5], refs[-5:]
    own = info[len(pieces)] == 0
    blocks = here_targets.shape[0]
    seq = att_ref.shape[0]
    low = lax.broadcasted_iota(jnp.int32, (SUB, 128), 1) < DH
    zero = jnp.zeros((SUB, 128), jnp.bfloat16)
    for n, piece in enumerate(pieces):
        base = info[n]

        @pl.loop(0, piece.shape[0] // RB, unroll=8)
        def _(b):
            frm = pl.ds(pl.multiple_of(b * RB, RB), RB)
            to = pl.ds(
                pl.multiple_of(jnp.where(own, here_targets[base + b], there[base + b]) * RB, RB), RB
            )
            u_ref[to, :] = piece[frm, 0:128]
            held[to, :] = piece[frm, 128:512]

    ends = []
    total = jnp.int32(0)
    for i in range(here_lengths.shape[0]):
        total = total + jnp.where(own, here_lengths[i], there[blocks + i])
        ends.append(total)
    def start_of(p):
        best = p * 0
        for e in ends:
            best = jnp.where(p >= e, e, best)
        return best
    def term(q0, rows, k0_at, keys, first, causal):
        at = pl.ds(pl.multiple_of(q0, 256), rows)
        q = held[at, 128:256]
        total = None
        for s in range(keys // SUB):
            ks = pl.ds(pl.multiple_of(k0_at + s * SUB, SUB), SUB)
            if first is not None:
                kp = k0_at + s * SUB + lax.broadcasted_iota(jnp.int32, (1, SUB), 1)
                ok = kp >= first
                if causal:
                    ok = ok & (kp <= q0 + lax.broadcasted_iota(jnp.int32, (rows, 1), 0))
            v, k = held[ks, 0:128], held[ks, 256:384]
            for upper in (False, True):
                kk, vv = (jnp.where(low, zero, m) if upper else jnp.where(low, m, zero) for m in (k, v))
                t = lax.dot_general(q, kk, (((1,), (1,)), ((), ())), preferred_element_type=jnp.float32)
                w = t + t * jnp.tanh(t)
                if first is not None:
                    w = jnp.where(ok, w, 0.0)
                d = jnp.dot(w.astype(jnp.bfloat16), vv, preferred_element_type=jnp.float32)
                total = d if total is None else total + d
        att_ref[at, :] += total
    @pl.loop(0, seq // TQ)
    def _(qi):
        q0 = qi * TQ
        at = pl.ds(pl.multiple_of(q0, TQ), TQ)
        att_ref[at, :] = jnp.zeros((TQ, 128), jnp.float32)
        first = start_of(q0 + lax.broadcasted_iota(jnp.int32, (TQ, 1), 0))
        diag = q0 // TK
        lo = start_of(q0) // TK
        mid = jnp.minimum((start_of(q0 + TQ - 1) + TK - 1) // TK, diag)
        mid = jnp.maximum(mid, lo)
        @pl.loop(lo, mid)
        def _(j):
            term(q0, TQ, j * TK, TK, first, False)
        @pl.loop(mid, diag)
        def _(j):
            term(q0, TQ, j * TK, TK, None, False)
        for s in range(TQ // DSUB):
            term(q0 + s * DSUB, TQ - s * DSUB, q0 + s * DSUB, DSUB, first[s * DSUB :], True)
        for s in range(TQ // 256):
            part = pl.ds(pl.multiple_of(q0 + s * 256, 256), 256)
            sums = att_ref[part, :]
            out_ref[part, :] = sums.astype(jnp.bfloat16)
            flip = sums.T
            stat_ref[0:1, part] = jnp.sum(flip, axis=0, keepdims=True)
            stat_ref[1:2, part] = jnp.sum(flip * flip, axis=0, keepdims=True)
def attend(info, targets, lengths, there, pieces):
    seq = sum(p.shape[0] for p in pieces)
    smem = pl.BlockSpec(memory_space=pltpu.SMEM)
    vmem = pl.BlockSpec(memory_space=pltpu.VMEM)
    return pl.pallas_call(
        attend_kernel,
        out_shape=(jax.ShapeDtypeStruct((seq, 128), jnp.bfloat16), jax.ShapeDtypeStruct((seq, 128), jnp.bfloat16), jax.ShapeDtypeStruct((2, seq), jnp.float32)),
        in_specs=[smem] * 4 + [vmem] * len(pieces),
        out_specs=(vmem,) * 3,
        scratch_shapes=[pltpu.VMEM((seq, 384), jnp.bfloat16), pltpu.VMEM((seq, 128), jnp.float32)],
        compiler_params=pltpu.CompilerParams(vmem_limit_bytes=56 * 1024 * 1024),
        cost_estimate=pl.CostEstimate(
            flops=2 * seq * seq * 128, bytes_accessed=seq * 128 * 14, transcendentals=seq * seq
        ),
    )(info, targets, lengths, there, *pieces)


def add_kernel(a_ref, b_ref, out_ref):
    out_ref[...] = a_ref[...] + b_ref[...]


def add(a, b):
    return pl.pallas_call(
        add_kernel,
        out_shape=jax.ShapeDtypeStruct(a.shape, a.dtype),
        compiler_params=pltpu.CompilerParams(vmem_limit_bytes=1024 * 1024),
        cost_estimate=pl.CostEstimate(flops=a.size, bytes_accessed=a.size * 12, transcendentals=0),
    )(a, b)


def gate_kernel(info, att_ref, u_ref, *refs):
    stats, outs = refs[:4], refs[4:]
    rows = outs[0].shape[0]
    step = 256
    for k, out in enumerate(outs):
        block = lax.rem(info[0] + k, len(outs))

        @pl.loop(0, rows // step)
        def _(i):
            at = pl.ds(pl.multiple_of(block * rows + i * step, step), step)
            sums = stats[0][:, at]
            for other in stats[1:]:
                sums = sums + other[:, at]
            mean = sums[0:1] / D
            square = sums[1:2] / D
            scale = lax.rsqrt(square - mean * mean + eps_norm)
            mean = jnp.broadcast_to(mean, (128, step)).T
            scale = jnp.broadcast_to(scale, (128, step)).T
            gated = ((att_ref[at, :].astype(jnp.float32) - mean) * scale) * u_ref[at, :].astype(jnp.float32)
            out[pl.ds(pl.multiple_of(i * step, step), step), :] = gated.astype(jnp.bfloat16)


def gate(info, att, u, stats, count):
    rows = att.shape[0] // count
    vmem = pl.BlockSpec(memory_space=pltpu.VMEM)
    out = jax.ShapeDtypeStruct((rows, 128), jnp.bfloat16)
    return pl.pallas_call(
        gate_kernel,
        out_shape=(out,) * count,
        in_specs=[pl.BlockSpec(memory_space=pltpu.SMEM)] + [vmem] * (2 + len(stats)),
        out_specs=(vmem,) * count,
        compiler_params=pltpu.CompilerParams(vmem_limit_bytes=14 * 1024 * 1024),
        cost_estimate=pl.CostEstimate(flops=att.size * 8, bytes_accessed=att.size * 8, transcendentals=0),
    )(info, att, u, *stats)


def outgoing_kernel(info, targets, events_ref, after_ref, out_ref):
    count = out_ref.shape[0]
    blocks = events_ref.shape[0] // RB
    base = info[0] * blocks

    @pl.loop(0, blocks, unroll=4)
    def _(b):
        t = targets[base + b]
        frm = pl.ds(pl.multiple_of(b * RB, RB), RB)
        to = pl.ds(pl.multiple_of(lax.rem(t, blocks // count) * RB, RB), RB)
        out_ref[pl.ds(t // blocks, 1), to, :] = events_ref[frm, :][None]


def outgoing(info, targets, events, after, count):
    smem = pl.BlockSpec(memory_space=pltpu.SMEM)
    vmem = pl.BlockSpec(memory_space=pltpu.VMEM)
    return pl.pallas_call(
        outgoing_kernel,
        out_shape=jax.ShapeDtypeStruct((count, events.shape[0] // count, events.shape[1]), events.dtype),
        in_specs=[smem, smem, vmem, pl.BlockSpec(memory_space=pl.ANY)],
        out_specs=vmem,
        compiler_params=pltpu.CompilerParams(vmem_limit_bytes=8 * 1024 * 1024),
        cost_estimate=pl.CostEstimate(flops=0, bytes_accessed=events.size * 4, transcendentals=0),
    )(info, targets, events, after)


def finish_kernel(info, quarter, w_ref, *refs):
    residual, pieces, (out_ref, acc_ref) = refs[0], refs[1:-2], refs[-2:]
    count, part = residual.shape[0], residual.shape[1]
    step = acc_ref.shape[0] // 2
    for i in range(2):
        at = pl.ds(i * step, step)
        acc = None
        for n in range(0, len(pieces), 2):
            two = (n, n + 1)
            left = jnp.concatenate([pieces[m][at, :] for m in two], axis=1)
            right = jnp.concatenate(
                [w_ref[pl.ds(pl.multiple_of(info[m] * 128, 128), 128), :] for m in two], axis=0
            )
            term = jnp.dot(left, right, preferred_element_type=jnp.float32)
            acc = term if acc is None else acc + term
        acc_ref[at, :] = acc

    for i in range(count):
        at = pl.ds(pl.multiple_of(quarter[i] * part, part), part)
        out_ref[at, :] = (acc_ref[at, :] + residual[i].astype(jnp.float32)).astype(out_ref.dtype)


def finish(info, quarter, residual, w_out, pieces):
    smem = pl.BlockSpec(memory_space=pltpu.SMEM)
    vmem = pl.BlockSpec(memory_space=pltpu.VMEM)
    shape = (residual.shape[0] * residual.shape[1], residual.shape[2])
    return pl.pallas_call(
        finish_kernel,
        out_shape=jax.ShapeDtypeStruct(shape, jnp.bfloat16),
        in_specs=[smem] * 2 + [vmem] * (2 + len(pieces)),
        out_specs=vmem,
        scratch_shapes=[pltpu.VMEM(shape, jnp.float32)],
        compiler_params=pltpu.CompilerParams(vmem_limit_bytes=14 * 1024 * 1024),
        cost_estimate=pl.CostEstimate(
            flops=2 * shape[0] * shape[1] * D, bytes_accessed=8 * 1024 * 1024, transcendentals=0
        ),
    )(info, quarter, w_out, residual, *pieces)


def team_body(events, w_proj, w_out, block_target, user_lengths):
    half, zlo = lax.axis_index("half"), lax.axis_index("zlo")
    head, core = lax.axis_index("head"), lax.axis_index("core")
    z = half * 2 + zlo
    foreign = core ^ half
    outer = 1 - (zlo ^ half)
    rows = events.shape[0]
    blocks = rows // RB
    targets_here = block_target
    other_ints = move(jnp.concatenate([block_target, user_lengths]), other_core)
    w_mine = lax.dynamic_slice_in_dim(w_proj, zlo * 256, 256, axis=2)

    parts = 2
    span = rows // parts
    partner = move(events, to_partner)
    x_own = move(events, across(lambda half, zlo, head, core: core == half))
    remote = []
    for i in range(parts):
        chunk = events[i * span : (i + 1) * span]
        if remote:
            chunk, _ = lax.optimization_barrier((chunk, remote[-1]))
        remote.append(move(chunk, to_other_team))
    send = outgoing(jnp.stack([z]), targets_here, events, events, 4)
    partner, send = lax.optimization_barrier((partner, send))
    x_partner = move(partner, across(lambda half, zlo, head, core: core != half))
    relayed = [move(r, inner_to_outer) for r in remote]

    def ints(*values):
        return jnp.stack([jnp.asarray(v, jnp.int32) for v in values])

    mine1, sib1 = project(
        ints(foreign, head, 1 - head, core), user_lengths, [events, x_own, partner, x_partner], w_mine, []
    )
    x_inner = [move(r, across(lambda half, zlo, head, core: (zlo ^ half) == 1)) for r in remote]
    x_outer = [move(r, across(lambda half, zlo, head, core: (zlo ^ half) == 0)) for r in relayed]
    mine, got = [mine1], [move(sib1, other_core)]
    residual = lax.all_to_all(send, ("half", "zlo"), split_axis=0, concat_axis=0, tiled=True)
    for i in range(parts):
        m, s = project(
            ints(outer, head, 1 - head, core),
            user_lengths,
            [remote[i], x_inner[i], relayed[i], x_outer[i]],
            w_mine,
            [send] if i == 0 else [],
        )
        mine.append(m)
        got.append(move(s, other_core))

    near = jnp.where(half == 0, 2, 1)
    far = jnp.where(half == 0, 3, 0)
    mine_second = jnp.where(foreign == 0, near, far)
    other_second = jnp.where(foreign == 0, far, near)
    part_blocks = span // RB
    starts = [jnp.where(foreign == 0, z, z ^ 1) * blocks]
    starts += [mine_second * blocks + i * part_blocks for i in range(parts)]
    starts += [jnp.where(foreign == 0, z ^ 1, z) * blocks]
    starts += [other_second * blocks + i * part_blocks for i in range(parts)]
    att, u, stat = attend(ints(*starts, foreign), block_target, user_lengths, other_ints, mine + got)

    by_shard = targets_here.reshape(4, blocks)
    quarter = jnp.max(
        jnp.where(by_shard // blocks == z, by_shard % blocks // (blocks // 4), 0), axis=1
    )

    stat = add(stat, move(stat, other_core))
    stats = [stat]
    for dz, dx in ((0, 1), (1, 0), (1, 1)):
        stats.append(
            move(stat, lambda half, zlo, head, core, dz=dz, dx=dx: (half, zlo ^ dz, head ^ dx, core))
        )
    me = zlo * 2 + core
    gated = gate(ints(me), att, u, stats, 4)

    def to_block(k):
        def rule(half, zlo, head, core):
            j = (zlo * 2 + core + k) % 4
            return (j // 2, j % 2, head, half)

        return rule

    pieces, feats = [], []
    for k in range(4):
        piece = move(gated[k], to_block(k))
        source = lax.rem(z - k + 4, 4)
        pieces += [piece, move(piece, across(lambda *p: True))]
        feats += [head * 4 + source, (1 - head) * 4 + source]
    return finish(ints(*feats), quarter, residual, w_out, pieces)


def solution(mesh):
    sizes = dict(mesh.shape)
    if sizes["seq"] == 4 and sizes["head"] == 2 and sizes["dp"] % 2 == 0:
        rows = P(("y", "core", "half", "zlo"), "head")
        part = P(("y", "core"))
        return jax.shard_map(
            team_body,
            mesh=team_plan(mesh),
            in_specs=(rows, P(None, None, "head"), P(None, "head"), part, part),
            out_specs=rows,
            check_vma=False,
        )
    placed = (P(("dp", "seq"), "head"), P(None, None, "head"), P(None, "head"), P("dp"), P("dp"))
    return jax.shard_map(
        body, mesh=mesh, in_specs=placed, out_specs=P(("dp", "seq"), "head"), check_vma=False
    )
```

```python
import functools

import jax
import jax.numpy as jnp
from jax import lax
from jax.experimental import pallas as pl
from jax.experimental.pallas import tpu as pltpu
from jax.sharding import PartitionSpec as P

D = 1024
DH = 64
RB = 16


eps_norm = 1e-05


def from_behind(block, axis, distance):
    devices = range(lax.axis_size(axis))
    route = [((i - distance) % len(devices), i) for i in devices]
    return lax.ppermute(block, axis, route)


def user_index(positions, user_ends):
    return jnp.sum((positions[:, None] >= user_ends[None, :]).astype(jnp.int32), axis=1)


def body(events, w_proj, w_out, block_target, user_lengths):
    rows_here = events.shape[0]
    col_width = events.shape[1]
    seq_count = lax.axis_size("seq")
    seq_index = lax.axis_index("seq")
    block_count = rows_here // RB
    per_owner = block_count // seq_count

    def window_position(shard, local):
        return shard * rows_here + local

    owners = block_target // block_count
    slots = block_target % block_count
    my_owners = lax.dynamic_slice_in_dim(owners, seq_index * block_count, block_count)
    send_order = jnp.argsort(my_owners, stable=True)
    outgoing = events.reshape(block_count, RB, col_width)[send_order]
    outgoing = outgoing.reshape(seq_count, per_owner, RB, col_width)
    incoming = lax.all_to_all(outgoing, "seq", split_axis=0, concat_axis=0, tiled=True)
    arrived = jnp.argsort(jnp.where(owners == seq_index, 0, 1), stable=True)[:block_count]
    slot_ids = slots[arrived]
    placed = incoming.reshape(block_count, RB, col_width)[jnp.argsort(slot_ids)]
    ordered = placed.reshape(rows_here, col_width)
    widened = ordered.astype(jnp.float32)
    row_sum, row_squares = lax.psum(
        (jnp.sum(widened, axis=1), jnp.sum(widened * widened, axis=1)), "head"
    )
    mean_value = row_sum / D
    square_mean = row_squares / D
    normed = (
        (widened - mean_value[:, None])
        * lax.rsqrt(square_mean - mean_value * mean_value + eps_norm)[:, None]
    ).astype(jnp.bfloat16)
    weight_rows = w_proj
    projected = jnp.einsum(
        "ln,jnc->jlc",
        lax.all_gather(normed, "head", axis=1, tiled=True),
        weight_rows,
        preferred_element_type=jnp.float32,
    )
    activated = jax.nn.silu(projected).astype(jnp.bfloat16)
    gate_rows = activated[0]
    value_rows = activated[1]
    query_rows = activated[2]
    key_rows = activated[3]
    user_ends = jnp.cumsum(user_lengths)
    head_count = col_width // DH
    query_heads = query_rows.reshape(rows_here, head_count, DH)
    local_rows = jnp.arange(rows_here, dtype=jnp.int32)
    query_pos = window_position(seq_index, local_rows)
    query_users = user_index(query_pos, user_ends)
    zero_sum = jnp.zeros((rows_here, col_width), jnp.float32)

    def key_term(key_piece, value_piece, key_pos):
        row_count = key_piece.shape[0]
        key_heads = key_piece.reshape(row_count, head_count, DH)
        value_heads = value_piece.reshape(row_count, head_count, DH)
        key_users = user_index(key_pos, user_ends)
        allowed = (key_pos[None, :] <= query_pos[:, None]) & (
            key_users[None, :] == query_users[:, None]
        )
        scores = jnp.einsum(
            "lhd,nhd->hln", query_heads, key_heads, preferred_element_type=jnp.float32
        )
        weights = jnp.where(allowed[None], jax.nn.silu(scores), 0.0).astype(jnp.bfloat16)
        summed = jnp.einsum(
            "hln,nhd->lhd", weights, value_heads, preferred_element_type=jnp.float32
        )
        return summed.reshape(rows_here, col_width)

    def guarded_term(key_piece, value_piece, key_pos):
        return key_term(key_piece, value_piece, key_pos)

    def sweep_piece(running, key_piece, value_piece, key_pos):
        row_count = key_piece.shape[0]
        block_rows = min(row_count, 1024)
        rounds = row_count // block_rows

        def visit_block(partial_sum, inputs):
            key_block, value_block, block_pos = inputs
            return (partial_sum + guarded_term(key_block, value_block, block_pos), None)

        key_stack = key_piece.reshape(rounds, block_rows, col_width)
        value_stack = value_piece.reshape(rounds, block_rows, col_width)
        pos_stack = key_pos.reshape(rounds, block_rows)
        running, _ = lax.scan(visit_block, running, (key_stack, value_stack, pos_stack))
        return running

    stacked = jnp.stack([key_rows, value_rows])
    own_block = sweep_piece(zero_sum, key_rows, value_rows, query_pos)

    def relay_step(offset, loop_state):
        running, carried = loop_state
        carried = from_behind(carried, "seq", 1)
        source_shard = (seq_index - offset + seq_count) % seq_count
        running = sweep_piece(
            running, carried[0], carried[1], window_position(source_shard, local_rows)
        )
        return (running, carried)

    attended, _ = lax.fori_loop(1, seq_count, relay_step, (own_block, stacked))
    att_sum, att_squares = lax.psum(
        (jnp.sum(attended, axis=1), jnp.sum(attended * attended, axis=1)), "head"
    )
    att_mean = att_sum / D
    att_square_mean = att_squares / D
    scaled = (attended - att_mean[:, None]) * lax.rsqrt(
        att_square_mean - att_mean * att_mean + eps_norm
    )[:, None]
    gated_rows = (scaled * gate_rows.astype(jnp.float32)).astype(jnp.bfloat16)
    weight_rows = w_out
    projected_out = jnp.dot(
        lax.all_gather(gated_rows, "head", axis=1, tiled=True),
        weight_rows,
        preferred_element_type=jnp.float32,
    )
    finished = (widened + projected_out).astype(jnp.bfloat16)
    return finished


def team_plan(mesh):
    return jax.sharding.Mesh(
        mesh.devices.reshape(2, 2, 2, mesh.devices.shape[2] // 2, 2),
        ("half", "zlo", "head", "y", "core"),
    )


ROUTE = ("half", "zlo", "head", "core")


def route(rule):
    pairs = []
    for half in range(2):
        for zlo in range(2):
            for head in range(2):
                for core in range(2):
                    to = rule(half, zlo, head, core)
                    if to is not None:
                        pairs.append(
                            (
                                ((half * 2 + zlo) * 2 + head) * 2 + core,
                                ((to[0] * 2 + to[1]) * 2 + to[2]) * 2 + to[3],
                            )
                        )
    return pairs


def move(value, rule):
    return lax.ppermute(value, ROUTE, route(rule))


def to_partner(half, zlo, head, core):
    if core == half:
        return (half, 1 - zlo, head, 1 - half)
    return None


def to_other_team(half, zlo, head, core):
    if core == half:
        return None
    other = 1 - half
    inner = (zlo ^ half) == 1
    return (other, 1 - other, head, other if inner else 1 - other)


def inner_to_outer(half, zlo, head, core):
    if (zlo ^ half) == 1:
        return (half, 1 - zlo, head, core)
    return None


def across(select):
    def rule(half, zlo, head, core):
        if select(half, zlo, head, core):
            return (half, zlo, 1 - head, core)
        return None

    return rule


def other_core(half, zlo, head, core):
    return (half, zlo, head, 1 - core)


def project_kernel(waited, info, lengths, *refs):
    pairs = refs[: -6 - waited]
    w_ref, mine_ref, sib_ref, own_v, other_v, sems = refs[-6:]
    pairs = [(pairs[i], pairs[i + 1]) for i in range(0, len(pairs), 2)]
    rows, width = own_v.shape
    step = rows // 2

    def copies(pair, i):
        at = pl.ds(i * step, step)
        return (
            pltpu.make_async_copy(pair[0].at[at, :], own_v.at[at, :], sems.at[2 * i]),
            pltpu.make_async_copy(pair[1].at[at, :], other_v.at[at, :], sems.at[2 * i + 1]),
        )

    for n, pair in enumerate(pairs):

        @pl.when(info[0] == n)
        def _():
            for i in range(2):
                for copy in copies(pair, i):
                    copy.start()

    own_rows = pl.multiple_of(info[1] * width, width)
    other_rows = pl.multiple_of(info[2] * width, width)
    low_core = info[3] == 0
    for i in range(2):
        for copy in copies(pairs[0], i):
            copy.wait()
        at = pl.ds(i * step, step)
        a = own_v[at, :].astype(jnp.float32)
        b = other_v[at, :].astype(jnp.float32)
        mean = (jnp.sum(a, axis=1, keepdims=True) + jnp.sum(b, axis=1, keepdims=True)) / (2 * width)
        square = (
            jnp.sum(a * a, axis=1, keepdims=True) + jnp.sum(b * b, axis=1, keepdims=True)
        ) / (2 * width)
        scale = lax.rsqrt(square - mean * mean + eps_norm)
        a = ((a - mean) * scale).astype(jnp.bfloat16)
        b = ((b - mean) * scale).astype(jnp.bfloat16)
        for j in range(4):
            z = jnp.dot(
                a, w_ref[j, pl.ds(own_rows, width), :], preferred_element_type=jnp.float32
            ) + jnp.dot(
                b, w_ref[j, pl.ds(other_rows, width), :], preferred_element_type=jnp.float32
            )
            t = 0.5 * z
            act = (t + t * jnp.tanh(t)).astype(jnp.bfloat16)
            if j == 2:
                act = act * 0.5
            low, high = act[:, :128], act[:, 128:]
            cols = pl.ds(j * 128, 128)
            mine_ref[at, cols] = jnp.where(low_core, low, high)
            sib_ref[at, cols] = jnp.where(low_core, high, low)


def project(info, lengths, pairs, w, after):
    rows, width = pairs[0].shape
    anywhere = pl.BlockSpec(memory_space=pl.ANY)
    vmem = pl.BlockSpec(memory_space=pltpu.VMEM)
    out = jax.ShapeDtypeStruct((rows, 512), jnp.bfloat16)
    return pl.pallas_call(
        functools.partial(project_kernel, len(after)),
        out_shape=(out, out),
        in_specs=[pl.BlockSpec(memory_space=pltpu.SMEM)] * 2 + [anywhere] * (len(pairs) + len(after)) + [vmem],
        out_specs=(vmem, vmem),
        scratch_shapes=[
            pltpu.VMEM((rows, width), jnp.bfloat16),
            pltpu.VMEM((rows, width), jnp.bfloat16),
            pltpu.SemaphoreType.DMA((4,)),
        ],
        compiler_params=pltpu.CompilerParams(vmem_limit_bytes=16 * 1024 * 1024),
        cost_estimate=pl.CostEstimate(
            flops=2 * rows * D * 1024, bytes_accessed=rows * D * 4 + w.size * 2, transcendentals=rows * 1024
        ),
    )(info, lengths, *pairs, *after, w)


TQ = 1536
TK = 512
SUB = 256
DSUB = 256


def attend_kernel(info, here_targets, here_lengths, there, *refs):
    pieces, (att_ref, u_ref, stat_ref, held) = refs[:-4], refs[-4:]
    own = info[len(pieces)] == 0
    blocks = here_targets.shape[0]
    seq = att_ref.shape[0]
    low = lax.broadcasted_iota(jnp.int32, (SUB, 128), 1) < DH
    zero = jnp.zeros((SUB, 128), jnp.bfloat16)
    for n, piece in enumerate(pieces):
        base = info[n]

        @pl.loop(0, piece.shape[0] // RB, unroll=8)
        def _(b):
            frm = pl.ds(pl.multiple_of(b * RB, RB), RB)
            to = pl.ds(
                pl.multiple_of(jnp.where(own, here_targets[base + b], there[base + b]) * RB, RB), RB
            )
            u_ref[to, :] = piece[frm, 0:128]
            held[to, :] = piece[frm, 128:512]

    ends = []
    total = jnp.int32(0)
    for i in range(here_lengths.shape[0]):
        total = total + jnp.where(own, here_lengths[i], there[blocks + i])
        ends.append(total)
    def start_of(p):
        best = p * 0
        for e in ends:
            best = jnp.where(p >= e, e, best)
        return best
    def term(q0, rows, k0_at, keys, first, causal):
        at = pl.ds(pl.multiple_of(q0, 256), rows)
        q = held[at, 128:256]
        total = None
        for s in range(keys // SUB):
            ks = pl.ds(pl.multiple_of(k0_at + s * SUB, SUB), SUB)
            if first is not None:
                kp = k0_at + s * SUB + lax.broadcasted_iota(jnp.int32, (1, SUB), 1)
                ok = kp >= first
                if causal:
                    ok = ok & (kp <= q0 + lax.broadcasted_iota(jnp.int32, (rows, 1), 0))
            v, k = held[ks, 0:128], held[ks, 256:384]
            for upper in (False, True):
                kk, vv = (jnp.where(low, zero, m) if upper else jnp.where(low, m, zero) for m in (k, v))
                t = lax.dot_general(q, kk, (((1,), (1,)), ((), ())), preferred_element_type=jnp.float32)
                w = t + t * jnp.tanh(t)
                if first is not None:
                    w = jnp.where(ok, w, 0.0)
                d = jnp.dot(w.astype(jnp.bfloat16), vv, preferred_element_type=jnp.float32)
                total = d if total is None else total + d
        att_ref[at, :] += total
    @pl.loop(0, seq // TQ)
    def _(qi):
        q0 = qi * TQ
        at = pl.ds(pl.multiple_of(q0, TQ), TQ)
        att_ref[at, :] = jnp.zeros((TQ, 128), jnp.float32)
        first = start_of(q0 + lax.broadcasted_iota(jnp.int32, (TQ, 1), 0))
        diag = q0 // TK
        lo = start_of(q0) // TK
        mid = jnp.minimum((start_of(q0 + TQ - 1) + TK - 1) // TK, diag)
        mid = jnp.maximum(mid, lo)
        @pl.loop(lo, mid)
        def _(j):
            term(q0, TQ, j * TK, TK, first, False)
        @pl.loop(mid, diag)
        def _(j):
            term(q0, TQ, j * TK, TK, None, False)
        for s in range(TQ // DSUB):
            term(q0 + s * DSUB, TQ - s * DSUB, q0 + s * DSUB, DSUB, first[s * DSUB :], True)
        for s in range(TQ // 256):
            part = pl.ds(pl.multiple_of(q0 + s * 256, 256), 256)
            flip = att_ref[part, :].T
            stat_ref[0:1, part] = jnp.sum(flip, axis=0, keepdims=True)
            stat_ref[1:2, part] = jnp.sum(flip * flip, axis=0, keepdims=True)
def attend(info, targets, lengths, there, pieces):
    seq = sum(p.shape[0] for p in pieces)
    smem = pl.BlockSpec(memory_space=pltpu.SMEM)
    vmem = pl.BlockSpec(memory_space=pltpu.VMEM)
    return pl.pallas_call(
        attend_kernel,
        out_shape=(jax.ShapeDtypeStruct((seq, 128), jnp.float32), jax.ShapeDtypeStruct((seq, 128), jnp.bfloat16), jax.ShapeDtypeStruct((2, seq), jnp.float32)),
        in_specs=[smem] * 4 + [vmem] * len(pieces),
        out_specs=(vmem,) * 3,
        scratch_shapes=[pltpu.VMEM((seq, 384), jnp.bfloat16)],
        compiler_params=pltpu.CompilerParams(vmem_limit_bytes=56 * 1024 * 1024),
        cost_estimate=pl.CostEstimate(
            flops=2 * seq * seq * 128, bytes_accessed=seq * 128 * 14, transcendentals=seq * seq
        ),
    )(info, targets, lengths, there, *pieces)


def add_kernel(a_ref, b_ref, out_ref):
    out_ref[...] = a_ref[...] + b_ref[...]


def add(a, b):
    return pl.pallas_call(
        add_kernel,
        out_shape=jax.ShapeDtypeStruct(a.shape, a.dtype),
        compiler_params=pltpu.CompilerParams(vmem_limit_bytes=1024 * 1024),
        cost_estimate=pl.CostEstimate(flops=a.size, bytes_accessed=a.size * 12, transcendentals=0),
    )(a, b)


def gate_kernel(info, att_ref, u_ref, *refs):
    stats, outs = refs[:4], refs[4:]
    rows = outs[0].shape[0]
    step = 256
    for k, out in enumerate(outs):
        block = lax.rem(info[0] + k, len(outs))

        @pl.loop(0, rows // step)
        def _(i):
            at = pl.ds(pl.multiple_of(block * rows + i * step, step), step)
            sums = stats[0][:, at]
            for other in stats[1:]:
                sums = sums + other[:, at]
            mean = sums[0:1] / D
            square = sums[1:2] / D
            scale = lax.rsqrt(square - mean * mean + eps_norm)
            mean = jnp.broadcast_to(mean, (128, step)).T
            scale = jnp.broadcast_to(scale, (128, step)).T
            gated = ((att_ref[at, :] - mean) * scale) * u_ref[at, :].astype(jnp.float32)
            out[pl.ds(pl.multiple_of(i * step, step), step), :] = gated.astype(jnp.bfloat16)


def gate(info, att, u, stats, count):
    rows = att.shape[0] // count
    vmem = pl.BlockSpec(memory_space=pltpu.VMEM)
    out = jax.ShapeDtypeStruct((rows, 128), jnp.bfloat16)
    return pl.pallas_call(
        gate_kernel,
        out_shape=(out,) * count,
        in_specs=[pl.BlockSpec(memory_space=pltpu.SMEM)] + [vmem] * (2 + len(stats)),
        out_specs=(vmem,) * count,
        compiler_params=pltpu.CompilerParams(vmem_limit_bytes=14 * 1024 * 1024),
        cost_estimate=pl.CostEstimate(flops=att.size * 8, bytes_accessed=att.size * 8, transcendentals=0),
    )(info, att, u, *stats)


def outgoing_kernel(info, targets, events_ref, after_ref, out_ref):
    count = out_ref.shape[0]
    blocks = events_ref.shape[0] // RB
    base = info[0] * blocks

    @pl.loop(0, blocks, unroll=4)
    def _(b):
        t = targets[base + b]
        frm = pl.ds(pl.multiple_of(b * RB, RB), RB)
        to = pl.ds(pl.multiple_of(lax.rem(t, blocks // count) * RB, RB), RB)
        out_ref[pl.ds(t // blocks, 1), to, :] = events_ref[frm, :][None]


def outgoing(info, targets, events, after, count):
    smem = pl.BlockSpec(memory_space=pltpu.SMEM)
    vmem = pl.BlockSpec(memory_space=pltpu.VMEM)
    return pl.pallas_call(
        outgoing_kernel,
        out_shape=jax.ShapeDtypeStruct((count, events.shape[0] // count, events.shape[1]), events.dtype),
        in_specs=[smem, smem, vmem, pl.BlockSpec(memory_space=pl.ANY)],
        out_specs=vmem,
        compiler_params=pltpu.CompilerParams(vmem_limit_bytes=8 * 1024 * 1024),
        cost_estimate=pl.CostEstimate(flops=0, bytes_accessed=events.size * 4, transcendentals=0),
    )(info, targets, events, after)


def finish_kernel(info, quarter, w_ref, *refs):
    residual, pieces, (out_ref, acc_ref) = refs[0], refs[1:-2], refs[-2:]
    count, part = residual.shape[0], residual.shape[1]
    step = acc_ref.shape[0] // 2
    for i in range(2):
        at = pl.ds(i * step, step)
        acc = None
        for n in range(0, len(pieces), 2):
            two = (n, n + 1)
            left = jnp.concatenate([pieces[m][at, :] for m in two], axis=1)
            right = jnp.concatenate(
                [w_ref[pl.ds(pl.multiple_of(info[m] * 128, 128), 128), :] for m in two], axis=0
            )
            term = jnp.dot(left, right, preferred_element_type=jnp.float32)
            acc = term if acc is None else acc + term
        acc_ref[at, :] = acc

    for i in range(count):
        at = pl.ds(pl.multiple_of(quarter[i] * part, part), part)
        out_ref[at, :] = (acc_ref[at, :] + residual[i].astype(jnp.float32)).astype(out_ref.dtype)


def finish(info, quarter, residual, w_out, pieces):
    smem = pl.BlockSpec(memory_space=pltpu.SMEM)
    vmem = pl.BlockSpec(memory_space=pltpu.VMEM)
    shape = (residual.shape[0] * residual.shape[1], residual.shape[2])
    return pl.pallas_call(
        finish_kernel,
        out_shape=jax.ShapeDtypeStruct(shape, jnp.bfloat16),
        in_specs=[smem] * 2 + [vmem] * (2 + len(pieces)),
        out_specs=vmem,
        scratch_shapes=[pltpu.VMEM(shape, jnp.float32)],
        compiler_params=pltpu.CompilerParams(vmem_limit_bytes=14 * 1024 * 1024),
        cost_estimate=pl.CostEstimate(
            flops=2 * shape[0] * shape[1] * D, bytes_accessed=8 * 1024 * 1024, transcendentals=0
        ),
    )(info, quarter, w_out, residual, *pieces)


def team_body(events, w_proj, w_out, block_target, user_lengths):
    half, zlo = lax.axis_index("half"), lax.axis_index("zlo")
    head, core = lax.axis_index("head"), lax.axis_index("core")
    z = half * 2 + zlo
    foreign = core ^ half
    outer = 1 - (zlo ^ half)
    rows = events.shape[0]
    blocks = rows // RB
    targets_here = block_target
    other_ints = move(jnp.concatenate([block_target, user_lengths]), other_core)
    w_mine = lax.dynamic_slice_in_dim(w_proj, zlo * 256, 256, axis=2)

    parts = 2
    span = rows // parts
    partner = move(events, to_partner)
    x_own = move(events, across(lambda half, zlo, head, core: core == half))
    remote = []
    for i in range(parts):
        chunk = events[i * span : (i + 1) * span]
        if remote:
            chunk, _ = lax.optimization_barrier((chunk, remote[-1]))
        remote.append(move(chunk, to_other_team))
    send = outgoing(jnp.stack([z]), targets_here, events, events, 4)
    partner, send = lax.optimization_barrier((partner, send))
    x_partner = move(partner, across(lambda half, zlo, head, core: core != half))
    relayed = [move(r, inner_to_outer) for r in remote]

    def ints(*values):
        return jnp.stack([jnp.asarray(v, jnp.int32) for v in values])

    mine1, sib1 = project(
        ints(foreign, head, 1 - head, core), user_lengths, [events, x_own, partner, x_partner], w_mine, []
    )
    x_inner = [move(r, across(lambda half, zlo, head, core: (zlo ^ half) == 1)) for r in remote]
    x_outer = [move(r, across(lambda half, zlo, head, core: (zlo ^ half) == 0)) for r in relayed]
    mine, got = [mine1], [move(sib1, other_core)]
    residual = lax.all_to_all(send, ("half", "zlo"), split_axis=0, concat_axis=0, tiled=True)
    for i in range(parts):
        m, s = project(
            ints(outer, head, 1 - head, core),
            user_lengths,
            [remote[i], x_inner[i], relayed[i], x_outer[i]],
            w_mine,
            [send] if i == 0 else [],
        )
        mine.append(m)
        got.append(move(s, other_core))

    near = jnp.where(half == 0, 2, 1)
    far = jnp.where(half == 0, 3, 0)
    mine_second = jnp.where(foreign == 0, near, far)
    other_second = jnp.where(foreign == 0, far, near)
    part_blocks = span // RB
    starts = [jnp.where(foreign == 0, z, z ^ 1) * blocks]
    starts += [mine_second * blocks + i * part_blocks for i in range(parts)]
    starts += [jnp.where(foreign == 0, z ^ 1, z) * blocks]
    starts += [other_second * blocks + i * part_blocks for i in range(parts)]
    att, u, stat = attend(ints(*starts, foreign), block_target, user_lengths, other_ints, mine + got)

    by_shard = targets_here.reshape(4, blocks)
    quarter = jnp.max(
        jnp.where(by_shard // blocks == z, by_shard % blocks // (blocks // 4), 0), axis=1
    )

    stat = add(stat, move(stat, other_core))
    stats = [stat]
    for dz, dx in ((0, 1), (1, 0), (1, 1)):
        stats.append(
            move(stat, lambda half, zlo, head, core, dz=dz, dx=dx: (half, zlo ^ dz, head ^ dx, core))
        )
    me = zlo * 2 + core
    gated = gate(ints(me), att, u, stats, 4)

    def to_block(k):
        def rule(half, zlo, head, core):
            j = (zlo * 2 + core + k) % 4
            return (j // 2, j % 2, head, half)

        return rule

    pieces, feats = [], []
    for k in range(4):
        piece = move(gated[k], to_block(k))
        source = lax.rem(z - k + 4, 4)
        pieces += [piece, move(piece, across(lambda *p: True))]
        feats += [head * 4 + source, (1 - head) * 4 + source]
    return finish(ints(*feats), quarter, residual, w_out, pieces)


def solution(mesh):
    sizes = dict(mesh.shape)
    if sizes["seq"] == 4 and sizes["head"] == 2 and sizes["dp"] % 2 == 0:
        rows = P(("y", "core", "half", "zlo"), "head")
        part = P(("y", "core"))
        return jax.shard_map(
            team_body,
            mesh=team_plan(mesh),
            in_specs=(rows, P(None, None, "head"), P(None, "head"), part, part),
            out_specs=rows,
            check_vma=False,
        )
    placed = (P(("dp", "seq"), "head"), P(None, None, "head"), P(None, "head"), P("dp"), P("dp"))
    return jax.shard_map(
        body, mesh=mesh, in_specs=placed, out_specs=P(("dp", "seq"), "head"), check_vma=False
    )
```

```python
import functools

import jax
import jax.numpy as jnp
from jax import lax
from jax.experimental import pallas as pl
from jax.experimental.pallas import tpu as pltpu
from jax.sharding import PartitionSpec as P

D = 1024
DH = 64
RB = 16


eps_norm = 1e-05


def from_behind(block, axis, distance):
    devices = range(lax.axis_size(axis))
    route = [((i - distance) % len(devices), i) for i in devices]
    return lax.ppermute(block, axis, route)


def user_index(positions, user_ends):
    return jnp.sum((positions[:, None] >= user_ends[None, :]).astype(jnp.int32), axis=1)


def body(events, w_proj, w_out, block_target, user_lengths):
    rows_here = events.shape[0]
    col_width = events.shape[1]
    seq_count = lax.axis_size("seq")
    seq_index = lax.axis_index("seq")
    block_count = rows_here // RB
    per_owner = block_count // seq_count

    def window_position(shard, local):
        return shard * rows_here + local

    owners = block_target // block_count
    slots = block_target % block_count
    my_owners = lax.dynamic_slice_in_dim(owners, seq_index * block_count, block_count)
    send_order = jnp.argsort(my_owners, stable=True)
    outgoing = events.reshape(block_count, RB, col_width)[send_order]
    outgoing = outgoing.reshape(seq_count, per_owner, RB, col_width)
    incoming = lax.all_to_all(outgoing, "seq", split_axis=0, concat_axis=0, tiled=True)
    arrived = jnp.argsort(jnp.where(owners == seq_index, 0, 1), stable=True)[:block_count]
    slot_ids = slots[arrived]
    placed = incoming.reshape(block_count, RB, col_width)[jnp.argsort(slot_ids)]
    ordered = placed.reshape(rows_here, col_width)
    widened = ordered.astype(jnp.float32)
    row_sum, row_squares = lax.psum(
        (jnp.sum(widened, axis=1), jnp.sum(widened * widened, axis=1)), "head"
    )
    mean_value = row_sum / D
    square_mean = row_squares / D
    normed = (
        (widened - mean_value[:, None])
        * lax.rsqrt(square_mean - mean_value * mean_value + eps_norm)[:, None]
    ).astype(jnp.bfloat16)
    weight_rows = w_proj
    projected = jnp.einsum(
        "ln,jnc->jlc",
        lax.all_gather(normed, "head", axis=1, tiled=True),
        weight_rows,
        preferred_element_type=jnp.float32,
    )
    activated = jax.nn.silu(projected).astype(jnp.bfloat16)
    gate_rows = activated[0]
    value_rows = activated[1]
    query_rows = activated[2]
    key_rows = activated[3]
    user_ends = jnp.cumsum(user_lengths)
    head_count = col_width // DH
    query_heads = query_rows.reshape(rows_here, head_count, DH)
    local_rows = jnp.arange(rows_here, dtype=jnp.int32)
    query_pos = window_position(seq_index, local_rows)
    query_users = user_index(query_pos, user_ends)
    zero_sum = jnp.zeros((rows_here, col_width), jnp.float32)

    def key_term(key_piece, value_piece, key_pos):
        row_count = key_piece.shape[0]
        key_heads = key_piece.reshape(row_count, head_count, DH)
        value_heads = value_piece.reshape(row_count, head_count, DH)
        key_users = user_index(key_pos, user_ends)
        allowed = (key_pos[None, :] <= query_pos[:, None]) & (
            key_users[None, :] == query_users[:, None]
        )
        scores = jnp.einsum(
            "lhd,nhd->hln", query_heads, key_heads, preferred_element_type=jnp.float32
        )
        weights = jnp.where(allowed[None], jax.nn.silu(scores), 0.0).astype(jnp.bfloat16)
        summed = jnp.einsum(
            "hln,nhd->lhd", weights, value_heads, preferred_element_type=jnp.float32
        )
        return summed.reshape(rows_here, col_width)

    def guarded_term(key_piece, value_piece, key_pos):
        return key_term(key_piece, value_piece, key_pos)

    def sweep_piece(running, key_piece, value_piece, key_pos):
        row_count = key_piece.shape[0]
        block_rows = min(row_count, 1024)
        rounds = row_count // block_rows

        def visit_block(partial_sum, inputs):
            key_block, value_block, block_pos = inputs
            return (partial_sum + guarded_term(key_block, value_block, block_pos), None)

        key_stack = key_piece.reshape(rounds, block_rows, col_width)
        value_stack = value_piece.reshape(rounds, block_rows, col_width)
        pos_stack = key_pos.reshape(rounds, block_rows)
        running, _ = lax.scan(visit_block, running, (key_stack, value_stack, pos_stack))
        return running

    stacked = jnp.stack([key_rows, value_rows])
    own_block = sweep_piece(zero_sum, key_rows, value_rows, query_pos)

    def relay_step(offset, loop_state):
        running, carried = loop_state
        carried = from_behind(carried, "seq", 1)
        source_shard = (seq_index - offset + seq_count) % seq_count
        running = sweep_piece(
            running, carried[0], carried[1], window_position(source_shard, local_rows)
        )
        return (running, carried)

    attended, _ = lax.fori_loop(1, seq_count, relay_step, (own_block, stacked))
    att_sum, att_squares = lax.psum(
        (jnp.sum(attended, axis=1), jnp.sum(attended * attended, axis=1)), "head"
    )
    att_mean = att_sum / D
    att_square_mean = att_squares / D
    scaled = (attended - att_mean[:, None]) * lax.rsqrt(
        att_square_mean - att_mean * att_mean + eps_norm
    )[:, None]
    gated_rows = (scaled * gate_rows.astype(jnp.float32)).astype(jnp.bfloat16)
    weight_rows = w_out
    projected_out = jnp.dot(
        lax.all_gather(gated_rows, "head", axis=1, tiled=True),
        weight_rows,
        preferred_element_type=jnp.float32,
    )
    finished = (widened + projected_out).astype(jnp.bfloat16)
    return finished


def team_plan(mesh):
    return jax.sharding.Mesh(
        mesh.devices.reshape(2, 2, 2, mesh.devices.shape[2] // 2, 2),
        ("half", "zlo", "head", "y", "core"),
    )


ROUTE = ("half", "zlo", "head", "core")


def route(rule):
    pairs = []
    for half in range(2):
        for zlo in range(2):
            for head in range(2):
                for core in range(2):
                    to = rule(half, zlo, head, core)
                    if to is not None:
                        pairs.append(
                            (
                                ((half * 2 + zlo) * 2 + head) * 2 + core,
                                ((to[0] * 2 + to[1]) * 2 + to[2]) * 2 + to[3],
                            )
                        )
    return pairs


def move(value, rule):
    return lax.ppermute(value, ROUTE, route(rule))


def to_partner(half, zlo, head, core):
    if core == half:
        return (half, 1 - zlo, head, 1 - half)
    return None


def to_other_team(half, zlo, head, core):
    if core == half:
        return None
    other = 1 - half
    inner = (zlo ^ half) == 1
    return (other, 1 - other, head, other if inner else 1 - other)


def inner_to_outer(half, zlo, head, core):
    if (zlo ^ half) == 1:
        return (half, 1 - zlo, head, core)
    return None


def across(select):
    def rule(half, zlo, head, core):
        if select(half, zlo, head, core):
            return (half, zlo, 1 - head, core)
        return None

    return rule


def other_core(half, zlo, head, core):
    return (half, zlo, head, 1 - core)


def project_kernel(waited, info, lengths, *refs):
    pairs = refs[: -6 - waited]
    w_ref, mine_ref, sib_ref, own_v, other_v, sems = refs[-6:]
    pairs = [(pairs[i], pairs[i + 1]) for i in range(0, len(pairs), 2)]
    rows, width = own_v.shape
    step = rows // 2

    def copies(pair, i):
        at = pl.ds(i * step, step)
        return (
            pltpu.make_async_copy(pair[0].at[at, :], own_v.at[at, :], sems.at[2 * i]),
            pltpu.make_async_copy(pair[1].at[at, :], other_v.at[at, :], sems.at[2 * i + 1]),
        )

    for n, pair in enumerate(pairs):

        @pl.when(info[0] == n)
        def _():
            for i in range(2):
                for copy in copies(pair, i):
                    copy.start()

    own_rows = pl.multiple_of(info[1] * width, width)
    other_rows = pl.multiple_of(info[2] * width, width)
    low_core = info[3] == 0
    for i in range(2):
        for copy in copies(pairs[0], i):
            copy.wait()
        at = pl.ds(i * step, step)
        a = own_v[at, :].astype(jnp.float32)
        b = other_v[at, :].astype(jnp.float32)
        mean = (jnp.sum(a, axis=1, keepdims=True) + jnp.sum(b, axis=1, keepdims=True)) / (2 * width)
        square = (
            jnp.sum(a * a, axis=1, keepdims=True) + jnp.sum(b * b, axis=1, keepdims=True)
        ) / (2 * width)
        scale = lax.rsqrt(square - mean * mean + eps_norm)
        a = ((a - mean) * scale).astype(jnp.bfloat16)
        b = ((b - mean) * scale).astype(jnp.bfloat16)
        for j in range(4):
            z = jnp.dot(
                a, w_ref[j, pl.ds(own_rows, width), :], preferred_element_type=jnp.float32
            ) + jnp.dot(
                b, w_ref[j, pl.ds(other_rows, width), :], preferred_element_type=jnp.float32
            )
            t = 0.5 * z
            act = (t + t * jnp.tanh(t)).astype(jnp.bfloat16)
            if j == 2:
                act = act * 0.5
            low, high = act[:, :128], act[:, 128:]
            cols = pl.ds(j * 128, 128)
            mine_ref[at, cols] = jnp.where(low_core, low, high)
            sib_ref[at, cols] = jnp.where(low_core, high, low)


def project(info, lengths, pairs, w, after):
    rows, width = pairs[0].shape
    anywhere = pl.BlockSpec(memory_space=pl.ANY)
    vmem = pl.BlockSpec(memory_space=pltpu.VMEM)
    out = jax.ShapeDtypeStruct((rows, 512), jnp.bfloat16)
    return pl.pallas_call(
        functools.partial(project_kernel, len(after)),
        out_shape=(out, out),
        in_specs=[pl.BlockSpec(memory_space=pltpu.SMEM)] * 2 + [anywhere] * (len(pairs) + len(after)) + [vmem],
        out_specs=(vmem, vmem),
        scratch_shapes=[
            pltpu.VMEM((rows, width), jnp.bfloat16),
            pltpu.VMEM((rows, width), jnp.bfloat16),
            pltpu.SemaphoreType.DMA((4,)),
        ],
        compiler_params=pltpu.CompilerParams(vmem_limit_bytes=16 * 1024 * 1024),
        cost_estimate=pl.CostEstimate(
            flops=2 * rows * D * 1024, bytes_accessed=rows * D * 4 + w.size * 2, transcendentals=rows * 1024
        ),
    )(info, lengths, *pairs, *after, w)


TQ = 1536
TK = 512
SUB = 256
DSUB = 256


def attend_kernel(info, here_targets, here_lengths, there, *refs):
    pieces, (att_ref, u_ref, stat_ref, held) = refs[:-4], refs[-4:]
    own = info[len(pieces)] == 0
    blocks = here_targets.shape[0]
    seq = att_ref.shape[0]
    low = lax.broadcasted_iota(jnp.int32, (512, 128), 1) < DH
    zero = jnp.zeros((512, 128), jnp.bfloat16)
    for n, piece in enumerate(pieces):
        base = info[n]

        @pl.loop(0, piece.shape[0] // RB, unroll=8)
        def _(b):
            frm = pl.ds(pl.multiple_of(b * RB, RB), RB)
            to = pl.ds(
                pl.multiple_of(jnp.where(own, here_targets[base + b], there[base + b]) * RB, RB), RB
            )
            u_ref[to, :] = piece[frm, 0:128]
            held[to, :] = piece[frm, 128:512]

    ends = []
    total = jnp.int32(0)
    for i in range(here_lengths.shape[0]):
        total = total + jnp.where(own, here_lengths[i], there[blocks + i])
        ends.append(total)
    def start_of(p):
        best = p * 0
        for e in ends:
            best = jnp.where(p >= e, e, best)
        return best
    def term(q0, rows, k0_at, keys, first, causal):
        at = pl.ds(pl.multiple_of(q0, 256), rows)
        q = held[at, 128:256]
        total = None
        sub = min(keys, 512)
        for s in range(keys // sub):
            ks = pl.ds(pl.multiple_of(k0_at + s * sub, sub), sub)
            if first is not None:
                kp = k0_at + s * sub + lax.broadcasted_iota(jnp.int32, (1, sub), 1)
                ok = kp >= first
                if causal:
                    ok = ok & (kp <= q0 + lax.broadcasted_iota(jnp.int32, (rows, 1), 0))
            v, k = held[ks, 0:128], held[ks, 256:384]
            for upper in (False, True):
                kk, vv = (jnp.where(low[:sub], zero[:sub], m) if upper else jnp.where(low[:sub], m, zero[:sub]) for m in (k, v))
                t = lax.dot_general(q, kk, (((1,), (1,)), ((), ())), preferred_element_type=jnp.float32)
                w = t + t * jnp.tanh(t)
                if first is not None:
                    w = jnp.where(ok, w, 0.0)
                d = jnp.dot(w.astype(jnp.bfloat16), vv, preferred_element_type=jnp.float32)
                total = d if total is None else total + d
        att_ref[at, :] += total
    @pl.loop(0, seq // TQ)
    def _(qi):
        q0 = qi * TQ
        at = pl.ds(pl.multiple_of(q0, TQ), TQ)
        att_ref[at, :] = jnp.zeros((TQ, 128), jnp.float32)
        first = start_of(q0 + lax.broadcasted_iota(jnp.int32, (TQ, 1), 0))
        diag = q0 // TK
        lo = start_of(q0) // TK
        mid = jnp.minimum((start_of(q0 + TQ - 1) + TK - 1) // TK, diag)
        mid = jnp.maximum(mid, lo)
        @pl.loop(lo, mid)
        def _(j):
            term(q0, TQ, j * TK, TK, first, False)
        @pl.loop(mid, diag)
        def _(j):
            term(q0, TQ, j * TK, TK, None, False)
        for s in range(TQ // DSUB):
            term(q0 + s * DSUB, TQ - s * DSUB, q0 + s * DSUB, DSUB, first[s * DSUB :], True)
        for s in range(TQ // 256):
            part = pl.ds(pl.multiple_of(q0 + s * 256, 256), 256)
            flip = att_ref[part, :].T
            stat_ref[0:1, part] = jnp.sum(flip, axis=0, keepdims=True)
            stat_ref[1:2, part] = jnp.sum(flip * flip, axis=0, keepdims=True)
def attend(info, targets, lengths, there, pieces):
    seq = sum(p.shape[0] for p in pieces)
    smem = pl.BlockSpec(memory_space=pltpu.SMEM)
    vmem = pl.BlockSpec(memory_space=pltpu.VMEM)
    return pl.pallas_call(
        attend_kernel,
        out_shape=(jax.ShapeDtypeStruct((seq, 128), jnp.float32), jax.ShapeDtypeStruct((seq, 128), jnp.bfloat16), jax.ShapeDtypeStruct((2, seq), jnp.float32)),
        in_specs=[smem] * 4 + [vmem] * len(pieces),
        out_specs=(vmem,) * 3,
        scratch_shapes=[pltpu.VMEM((seq, 384), jnp.bfloat16)],
        compiler_params=pltpu.CompilerParams(vmem_limit_bytes=56 * 1024 * 1024),
        cost_estimate=pl.CostEstimate(
            flops=2 * seq * seq * 128, bytes_accessed=seq * 128 * 14, transcendentals=seq * seq
        ),
    )(info, targets, lengths, there, *pieces)


def add_kernel(a_ref, b_ref, out_ref):
    out_ref[...] = a_ref[...] + b_ref[...]


def add(a, b):
    return pl.pallas_call(
        add_kernel,
        out_shape=jax.ShapeDtypeStruct(a.shape, a.dtype),
        compiler_params=pltpu.CompilerParams(vmem_limit_bytes=1024 * 1024),
        cost_estimate=pl.CostEstimate(flops=a.size, bytes_accessed=a.size * 12, transcendentals=0),
    )(a, b)


def gate_kernel(info, att_ref, u_ref, *refs):
    stats, outs = refs[:4], refs[4:]
    rows = outs[0].shape[0]
    step = 256
    for k, out in enumerate(outs):
        block = lax.rem(info[0] + k, len(outs))

        @pl.loop(0, rows // step)
        def _(i):
            at = pl.ds(pl.multiple_of(block * rows + i * step, step), step)
            sums = stats[0][:, at]
            for other in stats[1:]:
                sums = sums + other[:, at]
            mean = sums[0:1] / D
            square = sums[1:2] / D
            scale = lax.rsqrt(square - mean * mean + eps_norm)
            mean = jnp.broadcast_to(mean, (128, step)).T
            scale = jnp.broadcast_to(scale, (128, step)).T
            gated = ((att_ref[at, :] - mean) * scale) * u_ref[at, :].astype(jnp.float32)
            out[pl.ds(pl.multiple_of(i * step, step), step), :] = gated.astype(jnp.bfloat16)


def gate(info, att, u, stats, count):
    rows = att.shape[0] // count
    vmem = pl.BlockSpec(memory_space=pltpu.VMEM)
    out = jax.ShapeDtypeStruct((rows, 128), jnp.bfloat16)
    return pl.pallas_call(
        gate_kernel,
        out_shape=(out,) * count,
        in_specs=[pl.BlockSpec(memory_space=pltpu.SMEM)] + [vmem] * (2 + len(stats)),
        out_specs=(vmem,) * count,
        compiler_params=pltpu.CompilerParams(vmem_limit_bytes=14 * 1024 * 1024),
        cost_estimate=pl.CostEstimate(flops=att.size * 8, bytes_accessed=att.size * 8, transcendentals=0),
    )(info, att, u, *stats)


def outgoing_kernel(info, targets, events_ref, after_ref, out_ref):
    count = out_ref.shape[0]
    blocks = events_ref.shape[0] // RB
    base = info[0] * blocks

    @pl.loop(0, blocks, unroll=4)
    def _(b):
        t = targets[base + b]
        frm = pl.ds(pl.multiple_of(b * RB, RB), RB)
        to = pl.ds(pl.multiple_of(lax.rem(t, blocks // count) * RB, RB), RB)
        out_ref[pl.ds(t // blocks, 1), to, :] = events_ref[frm, :][None]


def outgoing(info, targets, events, after, count):
    smem = pl.BlockSpec(memory_space=pltpu.SMEM)
    vmem = pl.BlockSpec(memory_space=pltpu.VMEM)
    return pl.pallas_call(
        outgoing_kernel,
        out_shape=jax.ShapeDtypeStruct((count, events.shape[0] // count, events.shape[1]), events.dtype),
        in_specs=[smem, smem, vmem, pl.BlockSpec(memory_space=pl.ANY)],
        out_specs=vmem,
        compiler_params=pltpu.CompilerParams(vmem_limit_bytes=8 * 1024 * 1024),
        cost_estimate=pl.CostEstimate(flops=0, bytes_accessed=events.size * 4, transcendentals=0),
    )(info, targets, events, after)


def finish_kernel(info, quarter, w_ref, *refs):
    residual, pieces, (out_ref, acc_ref) = refs[0], refs[1:-2], refs[-2:]
    count, part = residual.shape[0], residual.shape[1]
    step = acc_ref.shape[0] // 2
    for i in range(2):
        at = pl.ds(i * step, step)
        acc = None
        for n in range(0, len(pieces), 2):
            two = (n, n + 1)
            left = jnp.concatenate([pieces[m][at, :] for m in two], axis=1)
            right = jnp.concatenate(
                [w_ref[pl.ds(pl.multiple_of(info[m] * 128, 128), 128), :] for m in two], axis=0
            )
            term = jnp.dot(left, right, preferred_element_type=jnp.float32)
            acc = term if acc is None else acc + term
        acc_ref[at, :] = acc

    for i in range(count):
        at = pl.ds(pl.multiple_of(quarter[i] * part, part), part)
        out_ref[at, :] = (acc_ref[at, :] + residual[i].astype(jnp.float32)).astype(out_ref.dtype)


def finish(info, quarter, residual, w_out, pieces):
    smem = pl.BlockSpec(memory_space=pltpu.SMEM)
    vmem = pl.BlockSpec(memory_space=pltpu.VMEM)
    shape = (residual.shape[0] * residual.shape[1], residual.shape[2])
    return pl.pallas_call(
        finish_kernel,
        out_shape=jax.ShapeDtypeStruct(shape, jnp.bfloat16),
        in_specs=[smem] * 2 + [vmem] * (2 + len(pieces)),
        out_specs=vmem,
        scratch_shapes=[pltpu.VMEM(shape, jnp.float32)],
        compiler_params=pltpu.CompilerParams(vmem_limit_bytes=14 * 1024 * 1024),
        cost_estimate=pl.CostEstimate(
            flops=2 * shape[0] * shape[1] * D, bytes_accessed=8 * 1024 * 1024, transcendentals=0
        ),
    )(info, quarter, w_out, residual, *pieces)


def team_body(events, w_proj, w_out, block_target, user_lengths):
    half, zlo = lax.axis_index("half"), lax.axis_index("zlo")
    head, core = lax.axis_index("head"), lax.axis_index("core")
    z = half * 2 + zlo
    foreign = core ^ half
    outer = 1 - (zlo ^ half)
    rows = events.shape[0]
    blocks = rows // RB
    targets_here = block_target
    other_ints = move(jnp.concatenate([block_target, user_lengths]), other_core)
    w_mine = lax.dynamic_slice_in_dim(w_proj, zlo * 256, 256, axis=2)

    parts = 2
    span = rows // parts
    partner = move(events, to_partner)
    x_own = move(events, across(lambda half, zlo, head, core: core == half))
    remote = []
    for i in range(parts):
        chunk = events[i * span : (i + 1) * span]
        if remote:
            chunk, _ = lax.optimization_barrier((chunk, remote[-1]))
        remote.append(move(chunk, to_other_team))
    send = outgoing(jnp.stack([z]), targets_here, events, events, 4)
    partner, send = lax.optimization_barrier((partner, send))
    x_partner = move(partner, across(lambda half, zlo, head, core: core != half))
    relayed = [move(r, inner_to_outer) for r in remote]

    def ints(*values):
        return jnp.stack([jnp.asarray(v, jnp.int32) for v in values])

    mine1, sib1 = project(
        ints(foreign, head, 1 - head, core), user_lengths, [events, x_own, partner, x_partner], w_mine, []
    )
    x_inner = [move(r, across(lambda half, zlo, head, core: (zlo ^ half) == 1)) for r in remote]
    x_outer = [move(r, across(lambda half, zlo, head, core: (zlo ^ half) == 0)) for r in relayed]
    mine, got = [mine1], [move(sib1, other_core)]
    residual = lax.all_to_all(send, ("half", "zlo"), split_axis=0, concat_axis=0, tiled=True)
    for i in range(parts):
        m, s = project(
            ints(outer, head, 1 - head, core),
            user_lengths,
            [remote[i], x_inner[i], relayed[i], x_outer[i]],
            w_mine,
            [send] if i == 0 else [],
        )
        mine.append(m)
        got.append(move(s, other_core))

    near = jnp.where(half == 0, 2, 1)
    far = jnp.where(half == 0, 3, 0)
    mine_second = jnp.where(foreign == 0, near, far)
    other_second = jnp.where(foreign == 0, far, near)
    part_blocks = span // RB
    starts = [jnp.where(foreign == 0, z, z ^ 1) * blocks]
    starts += [mine_second * blocks + i * part_blocks for i in range(parts)]
    starts += [jnp.where(foreign == 0, z ^ 1, z) * blocks]
    starts += [other_second * blocks + i * part_blocks for i in range(parts)]
    att, u, stat = attend(ints(*starts, foreign), block_target, user_lengths, other_ints, mine + got)

    by_shard = targets_here.reshape(4, blocks)
    quarter = jnp.max(
        jnp.where(by_shard // blocks == z, by_shard % blocks // (blocks // 4), 0), axis=1
    )

    stat = add(stat, move(stat, other_core))
    stats = [stat]
    for dz, dx in ((0, 1), (1, 0), (1, 1)):
        stats.append(
            move(stat, lambda half, zlo, head, core, dz=dz, dx=dx: (half, zlo ^ dz, head ^ dx, core))
        )
    me = zlo * 2 + core
    gated = gate(ints(me), att, u, stats, 4)

    def to_block(k):
        def rule(half, zlo, head, core):
            j = (zlo * 2 + core + k) % 4
            return (j // 2, j % 2, head, half)

        return rule

    pieces, feats = [], []
    for k in range(4):
        piece = move(gated[k], to_block(k))
        source = lax.rem(z - k + 4, 4)
        pieces += [piece, move(piece, across(lambda *p: True))]
        feats += [head * 4 + source, (1 - head) * 4 + source]
    return finish(ints(*feats), quarter, residual, w_out, pieces)


def solution(mesh):
    sizes = dict(mesh.shape)
    if sizes["seq"] == 4 and sizes["head"] == 2 and sizes["dp"] % 2 == 0:
        rows = P(("y", "core", "half", "zlo"), "head")
        part = P(("y", "core"))
        return jax.shard_map(
            team_body,
            mesh=team_plan(mesh),
            in_specs=(rows, P(None, None, "head"), P(None, "head"), part, part),
            out_specs=rows,
            check_vma=False,
        )
    placed = (P(("dp", "seq"), "head"), P(None, None, "head"), P(None, "head"), P("dp"), P("dp"))
    return jax.shard_map(
        body, mesh=mesh, in_specs=placed, out_specs=P(("dp", "seq"), "head"), check_vma=False
    )
```

```python
import functools

import jax
import jax.numpy as jnp
from jax import lax
from jax.experimental import pallas as pl
from jax.experimental.pallas import tpu as pltpu
from jax.sharding import PartitionSpec as P

D = 1024
DH = 64
RB = 16


eps_norm = 1e-05


def from_behind(block, axis, distance):
    devices = range(lax.axis_size(axis))
    route = [((i - distance) % len(devices), i) for i in devices]
    return lax.ppermute(block, axis, route)


def user_index(positions, user_ends):
    return jnp.sum((positions[:, None] >= user_ends[None, :]).astype(jnp.int32), axis=1)


def body(events, w_proj, w_out, block_target, user_lengths):
    rows_here = events.shape[0]
    col_width = events.shape[1]
    seq_count = lax.axis_size("seq")
    seq_index = lax.axis_index("seq")
    block_count = rows_here // RB
    per_owner = block_count // seq_count

    def window_position(shard, local):
        return shard * rows_here + local

    owners = block_target // block_count
    slots = block_target % block_count
    my_owners = lax.dynamic_slice_in_dim(owners, seq_index * block_count, block_count)
    send_order = jnp.argsort(my_owners, stable=True)
    outgoing = events.reshape(block_count, RB, col_width)[send_order]
    outgoing = outgoing.reshape(seq_count, per_owner, RB, col_width)
    incoming = lax.all_to_all(outgoing, "seq", split_axis=0, concat_axis=0, tiled=True)
    arrived = jnp.argsort(jnp.where(owners == seq_index, 0, 1), stable=True)[:block_count]
    slot_ids = slots[arrived]
    placed = incoming.reshape(block_count, RB, col_width)[jnp.argsort(slot_ids)]
    ordered = placed.reshape(rows_here, col_width)
    widened = ordered.astype(jnp.float32)
    row_sum, row_squares = lax.psum(
        (jnp.sum(widened, axis=1), jnp.sum(widened * widened, axis=1)), "head"
    )
    mean_value = row_sum / D
    square_mean = row_squares / D
    normed = (
        (widened - mean_value[:, None])
        * lax.rsqrt(square_mean - mean_value * mean_value + eps_norm)[:, None]
    ).astype(jnp.bfloat16)
    weight_rows = w_proj
    projected = jnp.einsum(
        "ln,jnc->jlc",
        lax.all_gather(normed, "head", axis=1, tiled=True),
        weight_rows,
        preferred_element_type=jnp.float32,
    )
    activated = jax.nn.silu(projected).astype(jnp.bfloat16)
    gate_rows = activated[0]
    value_rows = activated[1]
    query_rows = activated[2]
    key_rows = activated[3]
    user_ends = jnp.cumsum(user_lengths)
    head_count = col_width // DH
    query_heads = query_rows.reshape(rows_here, head_count, DH)
    local_rows = jnp.arange(rows_here, dtype=jnp.int32)
    query_pos = window_position(seq_index, local_rows)
    query_users = user_index(query_pos, user_ends)
    zero_sum = jnp.zeros((rows_here, col_width), jnp.float32)

    def key_term(key_piece, value_piece, key_pos):
        row_count = key_piece.shape[0]
        key_heads = key_piece.reshape(row_count, head_count, DH)
        value_heads = value_piece.reshape(row_count, head_count, DH)
        key_users = user_index(key_pos, user_ends)
        allowed = (key_pos[None, :] <= query_pos[:, None]) & (
            key_users[None, :] == query_users[:, None]
        )
        scores = jnp.einsum(
            "lhd,nhd->hln", query_heads, key_heads, preferred_element_type=jnp.float32
        )
        weights = jnp.where(allowed[None], jax.nn.silu(scores), 0.0).astype(jnp.bfloat16)
        summed = jnp.einsum(
            "hln,nhd->lhd", weights, value_heads, preferred_element_type=jnp.float32
        )
        return summed.reshape(rows_here, col_width)

    def guarded_term(key_piece, value_piece, key_pos):
        return key_term(key_piece, value_piece, key_pos)

    def sweep_piece(running, key_piece, value_piece, key_pos):
        row_count = key_piece.shape[0]
        block_rows = min(row_count, 1024)
        rounds = row_count // block_rows

        def visit_block(partial_sum, inputs):
            key_block, value_block, block_pos = inputs
            return (partial_sum + guarded_term(key_block, value_block, block_pos), None)

        key_stack = key_piece.reshape(rounds, block_rows, col_width)
        value_stack = value_piece.reshape(rounds, block_rows, col_width)
        pos_stack = key_pos.reshape(rounds, block_rows)
        running, _ = lax.scan(visit_block, running, (key_stack, value_stack, pos_stack))
        return running

    stacked = jnp.stack([key_rows, value_rows])
    own_block = sweep_piece(zero_sum, key_rows, value_rows, query_pos)

    def relay_step(offset, loop_state):
        running, carried = loop_state
        carried = from_behind(carried, "seq", 1)
        source_shard = (seq_index - offset + seq_count) % seq_count
        running = sweep_piece(
            running, carried[0], carried[1], window_position(source_shard, local_rows)
        )
        return (running, carried)

    attended, _ = lax.fori_loop(1, seq_count, relay_step, (own_block, stacked))
    att_sum, att_squares = lax.psum(
        (jnp.sum(attended, axis=1), jnp.sum(attended * attended, axis=1)), "head"
    )
    att_mean = att_sum / D
    att_square_mean = att_squares / D
    scaled = (attended - att_mean[:, None]) * lax.rsqrt(
        att_square_mean - att_mean * att_mean + eps_norm
    )[:, None]
    gated_rows = (scaled * gate_rows.astype(jnp.float32)).astype(jnp.bfloat16)
    weight_rows = w_out
    projected_out = jnp.dot(
        lax.all_gather(gated_rows, "head", axis=1, tiled=True),
        weight_rows,
        preferred_element_type=jnp.float32,
    )
    finished = (widened + projected_out).astype(jnp.bfloat16)
    return finished


def team_plan(mesh):
    return jax.sharding.Mesh(
        mesh.devices.reshape(2, 2, 2, mesh.devices.shape[2] // 2, 2),
        ("half", "zlo", "head", "y", "core"),
    )


ROUTE = ("half", "zlo", "head", "core")


def route(rule):
    pairs = []
    for half in range(2):
        for zlo in range(2):
            for head in range(2):
                for core in range(2):
                    to = rule(half, zlo, head, core)
                    if to is not None:
                        pairs.append(
                            (
                                ((half * 2 + zlo) * 2 + head) * 2 + core,
                                ((to[0] * 2 + to[1]) * 2 + to[2]) * 2 + to[3],
                            )
                        )
    return pairs


def move(value, rule):
    return lax.ppermute(value, ROUTE, route(rule))


def to_partner(half, zlo, head, core):
    if core == half:
        return (half, 1 - zlo, head, 1 - half)
    return None


def to_other_team(half, zlo, head, core):
    if core == half:
        return None
    other = 1 - half
    inner = (zlo ^ half) == 1
    return (other, 1 - other, head, other if inner else 1 - other)


def inner_to_outer(half, zlo, head, core):
    if (zlo ^ half) == 1:
        return (half, 1 - zlo, head, core)
    return None


def across(select):
    def rule(half, zlo, head, core):
        if select(half, zlo, head, core):
            return (half, zlo, 1 - head, core)
        return None

    return rule


def other_core(half, zlo, head, core):
    return (half, zlo, head, 1 - core)


def project_kernel(waited, info, lengths, *refs):
    pairs = refs[: -6 - waited]
    w_ref, mine_ref, sib_ref, own_v, other_v, sems = refs[-6:]
    pairs = [(pairs[i], pairs[i + 1]) for i in range(0, len(pairs), 2)]
    rows, width = own_v.shape
    step = rows // 2

    def copies(pair, i):
        at = pl.ds(i * step, step)
        return (
            pltpu.make_async_copy(pair[0].at[at, :], own_v.at[at, :], sems.at[2 * i]),
            pltpu.make_async_copy(pair[1].at[at, :], other_v.at[at, :], sems.at[2 * i + 1]),
        )

    for n, pair in enumerate(pairs):

        @pl.when(info[0] == n)
        def _():
            for i in range(2):
                for copy in copies(pair, i):
                    copy.start()

    own_rows = pl.multiple_of(info[1] * width, width)
    other_rows = pl.multiple_of(info[2] * width, width)
    low_core = info[3] == 0
    for i in range(2):
        for copy in copies(pairs[0], i):
            copy.wait()
        at = pl.ds(i * step, step)
        a = own_v[at, :].astype(jnp.float32)
        b = other_v[at, :].astype(jnp.float32)
        mean = (jnp.sum(a, axis=1, keepdims=True) + jnp.sum(b, axis=1, keepdims=True)) / (2 * width)
        square = (
            jnp.sum(a * a, axis=1, keepdims=True) + jnp.sum(b * b, axis=1, keepdims=True)
        ) / (2 * width)
        scale = lax.rsqrt(square - mean * mean + eps_norm)
        a = ((a - mean) * scale).astype(jnp.bfloat16)
        b = ((b - mean) * scale).astype(jnp.bfloat16)
        for j in range(4):
            z = jnp.dot(
                a, w_ref[j, pl.ds(own_rows, width), :], preferred_element_type=jnp.float32
            ) + jnp.dot(
                b, w_ref[j, pl.ds(other_rows, width), :], preferred_element_type=jnp.float32
            )
            t = 0.5 * z
            act = (t + t * jnp.tanh(t)).astype(jnp.bfloat16)
            if j == 2:
                act = act * 0.5
            low, high = act[:, :128], act[:, 128:]
            cols = pl.ds(j * 128, 128)
            mine_ref[at, cols] = jnp.where(low_core, low, high)
            sib_ref[at, cols] = jnp.where(low_core, high, low)


def project(info, lengths, pairs, w, after):
    rows, width = pairs[0].shape
    anywhere = pl.BlockSpec(memory_space=pl.ANY)
    vmem = pl.BlockSpec(memory_space=pltpu.VMEM)
    out = jax.ShapeDtypeStruct((rows, 512), jnp.bfloat16)
    return pl.pallas_call(
        functools.partial(project_kernel, len(after)),
        out_shape=(out, out),
        in_specs=[pl.BlockSpec(memory_space=pltpu.SMEM)] * 2 + [anywhere] * (len(pairs) + len(after)) + [vmem],
        out_specs=(vmem, vmem),
        scratch_shapes=[
            pltpu.VMEM((rows, width), jnp.bfloat16),
            pltpu.VMEM((rows, width), jnp.bfloat16),
            pltpu.SemaphoreType.DMA((4,)),
        ],
        compiler_params=pltpu.CompilerParams(vmem_limit_bytes=16 * 1024 * 1024),
        cost_estimate=pl.CostEstimate(
            flops=2 * rows * D * 1024, bytes_accessed=rows * D * 4 + w.size * 2, transcendentals=rows * 1024
        ),
    )(info, lengths, *pairs, *after, w)


TQ = 1536
TK = 1536
SUB = 256
DSUB = 256


def attend_kernel(info, here_targets, here_lengths, there, *refs):
    pieces, (att_ref, u_ref, stat_ref, held) = refs[:-4], refs[-4:]
    own = info[len(pieces)] == 0
    blocks = here_targets.shape[0]
    seq = att_ref.shape[0]
    low = lax.broadcasted_iota(jnp.int32, (512, 128), 1) < DH
    zero = jnp.zeros((512, 128), jnp.bfloat16)
    for n, piece in enumerate(pieces):
        base = info[n]

        @pl.loop(0, piece.shape[0] // RB, unroll=8)
        def _(b):
            frm = pl.ds(pl.multiple_of(b * RB, RB), RB)
            to = pl.ds(
                pl.multiple_of(jnp.where(own, here_targets[base + b], there[base + b]) * RB, RB), RB
            )
            u_ref[to, :] = piece[frm, 0:128]
            held[to, :] = piece[frm, 128:512]

    ends = []
    total = jnp.int32(0)
    for i in range(here_lengths.shape[0]):
        total = total + jnp.where(own, here_lengths[i], there[blocks + i])
        ends.append(total)
    def start_of(p):
        best = p * 0
        for e in ends:
            best = jnp.where(p >= e, e, best)
        return best
    def term(q0, rows, k0_at, keys, first, causal):
        at = pl.ds(pl.multiple_of(q0, 256), rows)
        q = held[at, 128:256]
        total = None
        sub = min(keys, 512)
        for s in range(keys // sub):
            ks = pl.ds(pl.multiple_of(k0_at + s * sub, sub), sub)
            if first is not None:
                kp = k0_at + s * sub + lax.broadcasted_iota(jnp.int32, (1, sub), 1)
                ok = kp >= first
                if causal:
                    ok = ok & (kp <= q0 + lax.broadcasted_iota(jnp.int32, (rows, 1), 0))
            v, k = held[ks, 0:128], held[ks, 256:384]
            for upper in (False, True):
                kk, vv = (jnp.where(low[:sub], zero[:sub], m) if upper else jnp.where(low[:sub], m, zero[:sub]) for m in (k, v))
                t = lax.dot_general(q, kk, (((1,), (1,)), ((), ())), preferred_element_type=jnp.float32)
                w = t + t * jnp.tanh(t)
                if first is not None:
                    w = jnp.where(ok, w, 0.0)
                d = jnp.dot(w.astype(jnp.bfloat16), vv, preferred_element_type=jnp.float32)
                total = d if total is None else total + d
        att_ref[at, :] += total
    @pl.loop(0, seq // TQ)
    def _(qi):
        q0 = qi * TQ
        at = pl.ds(pl.multiple_of(q0, TQ), TQ)
        att_ref[at, :] = jnp.zeros((TQ, 128), jnp.float32)
        first = start_of(q0 + lax.broadcasted_iota(jnp.int32, (TQ, 1), 0))
        diag = q0 // TK
        lo = start_of(q0) // TK
        mid = jnp.minimum((start_of(q0 + TQ - 1) + TK - 1) // TK, diag)
        mid = jnp.maximum(mid, lo)
        @pl.loop(lo, mid)
        def _(j):
            term(q0, TQ, j * TK, TK, first, False)
        @pl.loop(mid, diag)
        def _(j):
            term(q0, TQ, j * TK, TK, None, False)
        for s in range(TQ // DSUB):
            term(q0 + s * DSUB, TQ - s * DSUB, q0 + s * DSUB, DSUB, first[s * DSUB :], True)
        for s in range(TQ // 256):
            part = pl.ds(pl.multiple_of(q0 + s * 256, 256), 256)
            flip = att_ref[part, :].T
            stat_ref[0:1, part] = jnp.sum(flip, axis=0, keepdims=True)
            stat_ref[1:2, part] = jnp.sum(flip * flip, axis=0, keepdims=True)
def attend(info, targets, lengths, there, pieces):
    seq = sum(p.shape[0] for p in pieces)
    smem = pl.BlockSpec(memory_space=pltpu.SMEM)
    vmem = pl.BlockSpec(memory_space=pltpu.VMEM)
    return pl.pallas_call(
        attend_kernel,
        out_shape=(jax.ShapeDtypeStruct((seq, 128), jnp.float32), jax.ShapeDtypeStruct((seq, 128), jnp.bfloat16), jax.ShapeDtypeStruct((2, seq), jnp.float32)),
        in_specs=[smem] * 4 + [vmem] * len(pieces),
        out_specs=(vmem,) * 3,
        scratch_shapes=[pltpu.VMEM((seq, 384), jnp.bfloat16)],
        compiler_params=pltpu.CompilerParams(vmem_limit_bytes=56 * 1024 * 1024),
        cost_estimate=pl.CostEstimate(
            flops=2 * seq * seq * 128, bytes_accessed=seq * 128 * 14, transcendentals=seq * seq
        ),
    )(info, targets, lengths, there, *pieces)


def add_kernel(a_ref, b_ref, out_ref):
    out_ref[...] = a_ref[...] + b_ref[...]


def add(a, b):
    return pl.pallas_call(
        add_kernel,
        out_shape=jax.ShapeDtypeStruct(a.shape, a.dtype),
        compiler_params=pltpu.CompilerParams(vmem_limit_bytes=1024 * 1024),
        cost_estimate=pl.CostEstimate(flops=a.size, bytes_accessed=a.size * 12, transcendentals=0),
    )(a, b)


def gate_kernel(info, att_ref, u_ref, *refs):
    stats, outs = refs[:4], refs[4:]
    rows = outs[0].shape[0]
    step = 256
    for k, out in enumerate(outs):
        block = lax.rem(info[0] + k, len(outs))

        @pl.loop(0, rows // step)
        def _(i):
            at = pl.ds(pl.multiple_of(block * rows + i * step, step), step)
            sums = stats[0][:, at]
            for other in stats[1:]:
                sums = sums + other[:, at]
            mean = sums[0:1] / D
            square = sums[1:2] / D
            scale = lax.rsqrt(square - mean * mean + eps_norm)
            mean = jnp.broadcast_to(mean, (128, step)).T
            scale = jnp.broadcast_to(scale, (128, step)).T
            gated = ((att_ref[at, :] - mean) * scale) * u_ref[at, :].astype(jnp.float32)
            out[pl.ds(pl.multiple_of(i * step, step), step), :] = gated.astype(jnp.bfloat16)


def gate(info, att, u, stats, count):
    rows = att.shape[0] // count
    vmem = pl.BlockSpec(memory_space=pltpu.VMEM)
    out = jax.ShapeDtypeStruct((rows, 128), jnp.bfloat16)
    return pl.pallas_call(
        gate_kernel,
        out_shape=(out,) * count,
        in_specs=[pl.BlockSpec(memory_space=pltpu.SMEM)] + [vmem] * (2 + len(stats)),
        out_specs=(vmem,) * count,
        compiler_params=pltpu.CompilerParams(vmem_limit_bytes=14 * 1024 * 1024),
        cost_estimate=pl.CostEstimate(flops=att.size * 8, bytes_accessed=att.size * 8, transcendentals=0),
    )(info, att, u, *stats)


def outgoing_kernel(info, targets, events_ref, after_ref, out_ref):
    count = out_ref.shape[0]
    blocks = events_ref.shape[0] // RB
    base = info[0] * blocks

    @pl.loop(0, blocks, unroll=4)
    def _(b):
        t = targets[base + b]
        frm = pl.ds(pl.multiple_of(b * RB, RB), RB)
        to = pl.ds(pl.multiple_of(lax.rem(t, blocks // count) * RB, RB), RB)
        out_ref[pl.ds(t // blocks, 1), to, :] = events_ref[frm, :][None]


def outgoing(info, targets, events, after, count):
    smem = pl.BlockSpec(memory_space=pltpu.SMEM)
    vmem = pl.BlockSpec(memory_space=pltpu.VMEM)
    return pl.pallas_call(
        outgoing_kernel,
        out_shape=jax.ShapeDtypeStruct((count, events.shape[0] // count, events.shape[1]), events.dtype),
        in_specs=[smem, smem, vmem, pl.BlockSpec(memory_space=pl.ANY)],
        out_specs=vmem,
        compiler_params=pltpu.CompilerParams(vmem_limit_bytes=8 * 1024 * 1024),
        cost_estimate=pl.CostEstimate(flops=0, bytes_accessed=events.size * 4, transcendentals=0),
    )(info, targets, events, after)


def finish_kernel(info, quarter, w_ref, *refs):
    residual, pieces, (out_ref, acc_ref) = refs[0], refs[1:-2], refs[-2:]
    count, part = residual.shape[0], residual.shape[1]
    step = acc_ref.shape[0] // 2
    for i in range(2):
        at = pl.ds(i * step, step)
        acc = None
        for n in range(0, len(pieces), 2):
            two = (n, n + 1)
            left = jnp.concatenate([pieces[m][at, :] for m in two], axis=1)
            right = jnp.concatenate(
                [w_ref[pl.ds(pl.multiple_of(info[m] * 128, 128), 128), :] for m in two], axis=0
            )
            term = jnp.dot(left, right, preferred_element_type=jnp.float32)
            acc = term if acc is None else acc + term
        acc_ref[at, :] = acc

    for i in range(count):
        at = pl.ds(pl.multiple_of(quarter[i] * part, part), part)
        out_ref[at, :] = (acc_ref[at, :] + residual[i].astype(jnp.float32)).astype(out_ref.dtype)


def finish(info, quarter, residual, w_out, pieces):
    smem = pl.BlockSpec(memory_space=pltpu.SMEM)
    vmem = pl.BlockSpec(memory_space=pltpu.VMEM)
    shape = (residual.shape[0] * residual.shape[1], residual.shape[2])
    return pl.pallas_call(
        finish_kernel,
        out_shape=jax.ShapeDtypeStruct(shape, jnp.bfloat16),
        in_specs=[smem] * 2 + [vmem] * (2 + len(pieces)),
        out_specs=vmem,
        scratch_shapes=[pltpu.VMEM(shape, jnp.float32)],
        compiler_params=pltpu.CompilerParams(vmem_limit_bytes=14 * 1024 * 1024),
        cost_estimate=pl.CostEstimate(
            flops=2 * shape[0] * shape[1] * D, bytes_accessed=8 * 1024 * 1024, transcendentals=0
        ),
    )(info, quarter, w_out, residual, *pieces)


def team_body(events, w_proj, w_out, block_target, user_lengths):
    half, zlo = lax.axis_index("half"), lax.axis_index("zlo")
    head, core = lax.axis_index("head"), lax.axis_index("core")
    z = half * 2 + zlo
    foreign = core ^ half
    outer = 1 - (zlo ^ half)
    rows = events.shape[0]
    blocks = rows // RB
    targets_here = block_target
    other_ints = move(jnp.concatenate([block_target, user_lengths]), other_core)
    w_mine = lax.dynamic_slice_in_dim(w_proj, zlo * 256, 256, axis=2)

    parts = 2
    span = rows // parts
    partner = move(events, to_partner)
    x_own = move(events, across(lambda half, zlo, head, core: core == half))
    remote = []
    for i in range(parts):
        chunk = events[i * span : (i + 1) * span]
        if remote:
            chunk, _ = lax.optimization_barrier((chunk, remote[-1]))
        remote.append(move(chunk, to_other_team))
    send = outgoing(jnp.stack([z]), targets_here, events, events, 4)
    partner, send = lax.optimization_barrier((partner, send))
    x_partner = move(partner, across(lambda half, zlo, head, core: core != half))
    relayed = [move(r, inner_to_outer) for r in remote]

    def ints(*values):
        return jnp.stack([jnp.asarray(v, jnp.int32) for v in values])

    mine1, sib1 = project(
        ints(foreign, head, 1 - head, core), user_lengths, [events, x_own, partner, x_partner], w_mine, []
    )
    x_inner = [move(r, across(lambda half, zlo, head, core: (zlo ^ half) == 1)) for r in remote]
    x_outer = [move(r, across(lambda half, zlo, head, core: (zlo ^ half) == 0)) for r in relayed]
    mine, got = [mine1], [move(sib1, other_core)]
    residual = lax.all_to_all(send, ("half", "zlo"), split_axis=0, concat_axis=0, tiled=True)
    for i in range(parts):
        m, s = project(
            ints(outer, head, 1 - head, core),
            user_lengths,
            [remote[i], x_inner[i], relayed[i], x_outer[i]],
            w_mine,
            [send] if i == 0 else [],
        )
        mine.append(m)
        got.append(move(s, other_core))

    near = jnp.where(half == 0, 2, 1)
    far = jnp.where(half == 0, 3, 0)
    mine_second = jnp.where(foreign == 0, near, far)
    other_second = jnp.where(foreign == 0, far, near)
    part_blocks = span // RB
    starts = [jnp.where(foreign == 0, z, z ^ 1) * blocks]
    starts += [mine_second * blocks + i * part_blocks for i in range(parts)]
    starts += [jnp.where(foreign == 0, z ^ 1, z) * blocks]
    starts += [other_second * blocks + i * part_blocks for i in range(parts)]
    att, u, stat = attend(ints(*starts, foreign), block_target, user_lengths, other_ints, mine + got)

    by_shard = targets_here.reshape(4, blocks)
    quarter = jnp.max(
        jnp.where(by_shard // blocks == z, by_shard % blocks // (blocks // 4), 0), axis=1
    )

    stat = add(stat, move(stat, other_core))
    stats = [stat]
    for dz, dx in ((0, 1), (1, 0), (1, 1)):
        stats.append(
            move(stat, lambda half, zlo, head, core, dz=dz, dx=dx: (half, zlo ^ dz, head ^ dx, core))
        )
    me = zlo * 2 + core
    gated = gate(ints(me), att, u, stats, 4)

    def to_block(k):
        def rule(half, zlo, head, core):
            j = (zlo * 2 + core + k) % 4
            return (j // 2, j % 2, head, half)

        return rule

    pieces, feats = [], []
    for k in range(4):
        piece = move(gated[k], to_block(k))
        source = lax.rem(z - k + 4, 4)
        pieces += [piece, move(piece, across(lambda *p: True))]
        feats += [head * 4 + source, (1 - head) * 4 + source]
    return finish(ints(*feats), quarter, residual, w_out, pieces)


def solution(mesh):
    sizes = dict(mesh.shape)
    if sizes["seq"] == 4 and sizes["head"] == 2 and sizes["dp"] % 2 == 0:
        rows = P(("y", "core", "half", "zlo"), "head")
        part = P(("y", "core"))
        return jax.shard_map(
            team_body,
            mesh=team_plan(mesh),
            in_specs=(rows, P(None, None, "head"), P(None, "head"), part, part),
            out_specs=rows,
            check_vma=False,
        )
    placed = (P(("dp", "seq"), "head"), P(None, None, "head"), P(None, "head"), P("dp"), P("dp"))
    return jax.shard_map(
        body, mesh=mesh, in_specs=placed, out_specs=P(("dp", "seq"), "head"), check_vma=False
    )
```
